512 devices in a mesh: dom: 64 (over z, x), blk: 8 (over y, core).
Axes of the slice: x: 4, y: 4, z: 16, core: 2. Of those that a mesh axis runs over, the one named last changes fastest.
Arguments:
- adjoint_source: float32 [16, 2048, 162], P(None, ('dom', 'blk')), may hold values from -20 to 20
- diag_blocks: float32 [2048, 162, 162], P(('dom', 'blk')), may hold values from -3 to 9
- face_blocks: float32 [2048, 6, 162, 162], P(('dom', 'blk')), may hold values from -0.625 to 0.625
- neighbors: int32 [2048, 6], P(('dom', 'blk')), may hold values from -1 to 2047, as said below
- partner: int32 [2048, 6], P(('dom', 'blk')), may hold values from -1 to 5, as said below
- flags: int32 [2048, 6], P(('dom', 'blk')), may hold values from 0 to 2, as said below
Outputs:
- adjoint: float32 [16, 2048, 162], P(None, ('dom', 'blk'))
- rel_residual: float32 [16], replicated
The draws below stay inside these ranges and needn't reach their ends.
Inputs may be any that keep to these rules, and one draw needn't show every extreme that they name: Elements form a grid of 128 x 16 cells with one layer in the third direction; device number d = index along dom times the blk size plus index along blk holds elements d * 4 to (d + 1) * 4 - 1, a block of 2 x 2 cells in some order. neighbors[e, f] is the element across face f, -1 on a boundary face; the relation is symmetric, and every neighbor lies on the same device or on the next device along dom or along blk, 2 faces of a device meeting each existing next device along dom and 2 each existing next device along blk. partner[e, f] is the face of neighbors[e, f] whose neighbor is e; -1 on a boundary face. `flags`: 0 where the face has a neighbor; on a boundary face of the first or second grid direction 1 for a wall or 2 for the far field; the two faces of the third direction are always 2.
All inputs are finite; a program needn't handle non-finite values.
Results may differ from the reference program's by a relative error of at most 0.00085.
Values sent between devices are 32-bit elements; how exact they have to be, the bound alone decides.
No kernel may reach another device: no remote copies, remote signals or barrier semaphores. Data moves between devices by JAX's collectives and lax.ppermute only.
A program may use at most 64 MiB of HBM per device.

```python
import math
import jax
import jax.numpy as jnp
from jax import lax

B = 162
EX = 2
EY = 2
NRHS = 16
ITERS = 8
SWEEPS = 3
GX = 128
GY = 16
ELEMS = 2048
N_DOM = 64
N_BLK = 8


def mesh_tables(key):
    per_device = EX * EY
    devices = N_DOM * N_BLK
    slot_key = jax.random.fold_in(key, 101)
    face_key = jax.random.fold_in(key, 102)
    kind_key = jax.random.fold_in(key, 103)
    scores = jax.random.randint(slot_key, (devices, per_device), 0, 1 << 20) * per_device + jnp.arange(per_device)[None, :]
    slot_perm = jnp.argsort(scores, axis=1).astype(jnp.int32)
    grid_x = jnp.arange(GX)[:, None]
    grid_y = jnp.arange(GY)[None, :]
    device_of = grid_x // EX * N_BLK + grid_y // EY
    cell_of = grid_x % EX * EY + grid_y % EY
    element_id = (device_of * per_device + slot_perm[device_of, cell_of]).astype(jnp.int32)
    by_element = jnp.argsort(element_id.reshape(-1)).astype(jnp.int32)
    place_x = by_element // GY
    place_y = by_element % GY
    face_scores = jax.random.randint(face_key, (ELEMS, 6), 0, 1 << 20) * 6 + jnp.arange(6)[None, :]
    way_of_face = jnp.argsort(face_scores, axis=1).astype(jnp.int32)
    face_of_way = jnp.argsort(way_of_face, axis=1).astype(jnp.int32)
    step_x = jnp.array([-1, 1, 0, 0, 0, 0], jnp.int32)
    step_y = jnp.array([0, 0, -1, 1, 0, 0], jnp.int32)
    target_x = place_x[:, None] + step_x[way_of_face]
    target_y = place_y[:, None] + step_y[way_of_face]
    planar = way_of_face < 4
    inside = planar & (target_x >= 0) & (target_x < GX) & (target_y >= 0) & (target_y < GY)
    other = element_id[jnp.clip(target_x, 0, GX - 1), jnp.clip(target_y, 0, GY - 1)]
    other = jnp.where(inside, other, 0)
    opposite = jnp.bitwise_xor(way_of_face, 1)
    back_face = jnp.take_along_axis(face_of_way[other], opposite[:, :, None], axis=2)[:, :, 0]
    neighbors = jnp.where(inside, other, -1).astype(jnp.int32)
    partner = jnp.where(inside, back_face, -1).astype(jnp.int32)
    kinds = jax.random.randint(kind_key, (ELEMS, 6), 0, 2)
    flags = jnp.where(inside, 0, jnp.where(planar, 1 + kinds, 2)).astype(jnp.int32)
    return (neighbors, partner, flags)


def draw_neighbors(key, part):
    return mesh_tables(key)[0]


def draw_partner(key, part):
    return mesh_tables(key)[1]


def draw_flags(key, part):
    return mesh_tables(key)[2]


def draw_adjoint_source(key, part):
    key = jax.random.fold_in(key, 7)
    base_key, rough_key = jax.random.split(key)
    position = jnp.arange(ELEMS, dtype=jnp.float32) / max(ELEMS - 1, 1)
    roughness = jax.random.uniform(rough_key, (1, ELEMS, 1), jnp.float32, 0.5, 1.5)
    values = jax.random.normal(base_key, (NRHS, ELEMS, B), jnp.float32)
    rising = 1.0 + 2.0 * position
    return jnp.clip(values * rising[None, :, None] * roughness, -20.0, 20.0)


def draw_diag_blocks(key, part):
    key = jax.random.fold_in(key, 11)
    noise_key, level_key = jax.random.split(key)
    identity = (jnp.arange(B)[:, None] == jnp.arange(B)[None, :]).astype(jnp.float32)
    spread = 0.45 / math.sqrt(B)
    jitter = jnp.clip(jax.random.normal(noise_key, (ELEMS, B, B), jnp.float32), -4.0, 4.0) * spread
    strength = jnp.exp(jax.random.uniform(level_key, (ELEMS, 1, 1), jnp.float32, math.log(3.0), math.log(6.0)))
    return strength * (identity[None, :, :] + jitter)


def level_of(key, dims, cuts, least, high):
    level, own = 1.0, jax.random.fold_in(key, 6)
    for dim, parts in cuts:
        heights = jnp.exp(jax.random.uniform(jax.random.fold_in(own, dim), (parts,), jnp.float32, least / len(cuts), high / len(cuts)))
        level = level * jnp.repeat(heights, dims[dim] // parts).reshape([-1 if axis == dim else 1 for axis in range(len(dims))])
    return level


def gaussian(key, shape, scale, most, shards=(), kind=jnp.bfloat16):
    drawn = jax.random.normal(key, shape, jnp.float32) * scale
    if len(shards) > 0:
        drawn = level_of(key, shape, shards, -0.22, 0.18) * drawn
    return jnp.clip(drawn, min=-most, max=most).astype(kind)


def setup_inputs(seed: int = 0) -> dict:
    splits = jax.random.split(jax.random.key(seed), 7)
    return {
        "adjoint_source": draw_adjoint_source(jax.random.fold_in(splits[6], 71), 0),
        "diag_blocks": draw_diag_blocks(jax.random.fold_in(splits[6], 71), 0),
        "face_blocks": gaussian(splits[2], (ELEMS, 6, B, B), (B // 2) ** -0.5, 0.625, ((0, 512),), jnp.float32),
        "neighbors": draw_neighbors(jax.random.fold_in(splits[6], 71), 0),
        "partner": draw_partner(jax.random.fold_in(splits[6], 71), 0),
        "flags": draw_flags(jax.random.fold_in(splits[6], 71), 0),
    }


HIGH = lax.Precision.HIGHEST

def invert_blocks(center):
    width = center.shape[-1]
    identity = jnp.eye(width, dtype=center.dtype)
    pivots = jnp.diagonal(center, axis1=1, axis2=2)
    estimate = identity[None, :, :] / pivots[:, :, None]
    for sweep_index in range(SWEEPS):
        product = jnp.einsum('eab,ebc->eac', center, estimate, precision=HIGH)
        estimate = 2.0 * estimate - jnp.einsum('eab,ebc->eac', estimate, product, precision=HIGH)
    return estimate

def least_squares(hessen, start_norm):
    count = len(hessen)
    cosines = []
    sines = []
    rotated_rhs = [start_norm] + [jnp.zeros_like(start_norm) for row_index in range(count)]
    upper = []
    for col_index in range(count):
        column = [hessen[col_index][row_index] for row_index in range(col_index + 2)]
        for row_index in range(col_index):
            rotated = cosines[row_index] * column[row_index] + sines[row_index] * column[row_index + 1]
            column[row_index + 1] = -sines[row_index] * column[row_index] + cosines[row_index] * column[row_index + 1]
            column[row_index] = rotated
        radius = jnp.sqrt(column[col_index] * column[col_index] + column[col_index + 1] * column[col_index + 1])
        cosine = column[col_index] / radius
        sine_value = column[col_index + 1] / radius
        column[col_index] = radius
        cosines.append(cosine)
        sines.append(sine_value)
        rotated_rhs[col_index + 1] = -sine_value * rotated_rhs[col_index]
        rotated_rhs[col_index] = cosine * rotated_rhs[col_index]
        upper.append(column[:col_index + 1])
    coeffs = [None] * count
    for row_index in reversed(range(count)):
        total = rotated_rhs[row_index]
        for col_index in range(row_index + 1, count):
            total = total - upper[col_index][row_index] * coeffs[col_index]
        coeffs[row_index] = total / upper[row_index][row_index]
    return (coeffs, jnp.abs(rotated_rhs[count]) / start_norm)

def reference(adjoint_source, diag_blocks, face_blocks, neighbors, partner, flags):
    wall_mask = (flags == 1).astype(jnp.float32)
    center = diag_blocks + jnp.einsum('ef,efab->eab', wall_mask, face_blocks, precision=HIGH)
    inverse = invert_blocks(center)
    inside = neighbors >= 0
    source_elem = jnp.where(inside, neighbors, 0)
    source_face = jnp.where(inside, partner, 0)
    face_weight = inside.astype(jnp.float32)

    def operator(vectors):
        pushed = jnp.einsum('efab,rea->refb', face_blocks, vectors, precision=HIGH)
        pulled = pushed[:, source_elem, source_face, :]
        own_part = jnp.einsum('eab,rea->reb', center, vectors, precision=HIGH)
        return own_part + jnp.einsum('eg,regb->reb', face_weight, pulled, precision=HIGH)

    def precondition(vectors):
        return jnp.einsum('eab,rea->reb', inverse, vectors, precision=HIGH)
    start_norm = jnp.sqrt(lax.optimization_barrier(jnp.sum(adjoint_source * adjoint_source, axis=(1, 2))))
    krylov_basis = [adjoint_source / start_norm[:, None, None]]
    hessen = []
    for iteration in range(ITERS):
        mapped = operator(precondition(krylov_basis[-1]))
        projections = jnp.stack([lax.optimization_barrier(jnp.sum(mapped * member, axis=(1, 2))) for member in krylov_basis])
        for row_index in range(len(krylov_basis)):
            mapped = mapped - projections[row_index][:, None, None] * krylov_basis[row_index]
        new_norm = jnp.sqrt(lax.optimization_barrier(jnp.sum(mapped * mapped, axis=(1, 2))))
        hessen.append(jnp.concatenate([projections, new_norm[None, :]], axis=0))
        krylov_basis.append(mapped / new_norm[:, None, None])
    coeffs, rel_residual = least_squares(hessen, start_norm)
    combined = coeffs[0][:, None, None] * krylov_basis[0]
    for col_index in range(1, ITERS):
        combined = combined + coeffs[col_index][:, None, None] * krylov_basis[col_index]
    return (precondition(combined), rel_residual)
```

```python
import functools

import jax
import jax.numpy as jnp
from jax import lax
from jax.experimental import pallas as pl
from jax.experimental.pallas import tpu as pltpu
from jax.sharding import PartitionSpec as P

EX = 2
EY = 2
ITERS = 8
SWEEPS = 3


HIGH = lax.Precision.HIGHEST


def shifted(value, axis, steps):
    count = lax.axis_size(axis)
    leading, last = (max(0, -steps), min(count, count - steps))
    return lax.ppermute(value, axis, [(source, source + steps) for source in range(leading, last)])


def invert_blocks(center):
    width = center.shape[-1]
    identity = jnp.eye(width, dtype=center.dtype)
    pivots = jnp.diagonal(center, axis1=1, axis2=2)
    estimate = identity[None, :, :] / pivots[:, :, None]
    for sweep_index in range(SWEEPS):
        product = jnp.einsum("eab,ebc->eac", center, estimate, precision=HIGH)
        estimate = 2.0 * estimate - jnp.einsum("eab,ebc->eac", estimate, product, precision=HIGH)
    return estimate


def least_squares(hessen, start_norm):
    count = len(hessen)
    cosines = []
    sines = []
    rotated_rhs = [start_norm] + [jnp.zeros_like(start_norm) for row_index in range(count)]
    upper = []
    for col_index in range(count):
        column = [hessen[col_index][row_index] for row_index in range(col_index + 2)]
        for row_index in range(col_index):
            rotated = (
                cosines[row_index] * column[row_index] + sines[row_index] * column[row_index + 1]
            )
            column[row_index + 1] = (
                -sines[row_index] * column[row_index] + cosines[row_index] * column[row_index + 1]
            )
            column[row_index] = rotated
        radius = jnp.sqrt(
            column[col_index] * column[col_index] + column[col_index + 1] * column[col_index + 1]
        )
        cosine = column[col_index] / radius
        sine_value = column[col_index + 1] / radius
        column[col_index] = radius
        cosines.append(cosine)
        sines.append(sine_value)
        rotated_rhs[col_index + 1] = -sine_value * rotated_rhs[col_index]
        rotated_rhs[col_index] = cosine * rotated_rhs[col_index]
        upper.append(column[: col_index + 1])
    coeffs = [None] * count
    for row_index in reversed(range(count)):
        total = rotated_rhs[row_index]
        for col_index in range(row_index + 1, count):
            total = total - upper[col_index][row_index] * coeffs[col_index]
        coeffs[row_index] = total / upper[row_index][row_index]
    return (coeffs, jnp.abs(rotated_rhs[count]) / start_norm)


def move_vectors_dom(vectors, offset):
    return shifted(vectors, "dom", offset)


def move_vectors_blk(vectors, offset):
    return shifted(vectors, "blk", offset)


def move_facing_dom(blocks, offset):
    return shifted(blocks, "dom", offset)


def move_facing_blk(blocks, offset):
    return shifted(blocks, "blk", offset)


def direct_path(adjoint_source, diag_blocks, face_blocks, neighbors, partner, flags):
    nrhs, elements, width = adjoint_source.shape
    blk_count = lax.axis_size("blk")
    dom_here = lax.axis_index("dom")
    blk_here = lax.axis_index("blk")
    wall_mask = (flags == 1).astype(jnp.float32)
    center = diag_blocks + jnp.einsum("ef,efab->eab", wall_mask, face_blocks, precision=HIGH)
    inverse = invert_blocks(center)
    inside = neighbors >= 0
    source_elem = jnp.where(inside, neighbors, 0)
    source_face = jnp.where(inside, partner, 0)
    owner_dev = source_elem // elements
    owner_dom = owner_dev // blk_count
    owner_blk = owner_dev % blk_count
    direction = jnp.where(
        owner_dom == dom_here - 1,
        1,
        jnp.where(
            owner_dom == dom_here + 1,
            2,
            jnp.where(owner_blk == blk_here - 1, 3, jnp.where(owner_blk == blk_here + 1, 4, 0)),
        ),
    )
    direction = jnp.where(inside, direction, 0).astype(jnp.int32)
    local_slot = source_elem % elements
    flat_direction = direction.reshape(-1)
    flat_inside = inside.reshape(-1)
    flat_local = (local_slot * 6 + source_face).reshape(-1)
    face_keys = (source_elem * 6 + source_face).reshape(-1)
    same_way = (flat_direction[None, :] == flat_direction[:, None]) & flat_inside[None, :]
    placing = jnp.sum(
        (same_way & (face_keys[None, :] < face_keys[:, None])).astype(jnp.int32), axis=1
    )
    offsets = jnp.array(
        [0, 6 * elements, 6 * elements + EY, 6 * elements + 2 * EY, 6 * elements + 2 * EY + EX],
        jnp.int32,
    )
    candidate = jnp.where(flat_direction == 0, flat_local, offsets[flat_direction] + placing)
    slot_range = jnp.arange(elements * 6, dtype=jnp.int32)

    def pick_rows(target, count):
        marked = ((flat_direction == target) & flat_inside).astype(jnp.int32)
        ranking = jnp.cumsum(marked) - marked
        chooser = (ranking[None, :] == jnp.arange(count)[:, None]) & (marked[None, :] > 0)
        return jnp.sum(jnp.where(chooser, slot_range[None, :], 0), axis=1)

    toward_next_dom = pick_rows(2, EY)
    toward_prev_dom = pick_rows(1, EY)
    toward_next_blk = pick_rows(4, EX)
    toward_prev_blk = pick_rows(3, EX)
    flat_blocks = face_blocks.reshape(elements * 6, width, width)
    block_pool = jnp.concatenate(
        [
            flat_blocks,
            move_facing_dom(jnp.take(flat_blocks, toward_next_dom, axis=0), 1),
            move_facing_dom(jnp.take(flat_blocks, toward_prev_dom, axis=0), -1),
            move_facing_blk(jnp.take(flat_blocks, toward_next_blk, axis=0), 1),
            move_facing_blk(jnp.take(flat_blocks, toward_prev_blk, axis=0), -1),
        ],
        axis=0,
    )
    column_blocks = (
        jnp.take(block_pool, candidate, axis=0) * flat_inside.astype(jnp.float32)[:, None, None]
    )
    column_blocks = column_blocks.reshape(elements, 6, width, width)
    vector_index = (direction * elements + local_slot).reshape(-1)

    def precondition(vectors):
        return jnp.einsum("eab,rea->reb", inverse, vectors, precision=HIGH)

    start_norm = jnp.sqrt(
        lax.psum(jnp.sum(adjoint_source * adjoint_source, axis=(1, 2)), ("dom", "blk"))
    )
    krylov_basis = [adjoint_source / start_norm[:, None, None]]
    hessen = []
    for iteration in range(ITERS):
        operator_vectors = precondition(krylov_basis[-1])
        gathered = jnp.concatenate(
            [
                operator_vectors,
                move_vectors_dom(operator_vectors, 1),
                move_vectors_dom(operator_vectors, -1),
                move_vectors_blk(operator_vectors, 1),
                move_vectors_blk(operator_vectors, -1),
            ],
            axis=1,
        )
        nearby = jnp.take(gathered, vector_index, axis=1).reshape(nrhs, elements, 6, width)
        own_part = jnp.einsum("eab,rea->reb", center, operator_vectors, precision=HIGH)
        mapped = own_part + jnp.einsum("egab,rega->reb", column_blocks, nearby, precision=HIGH)
        local_dots = [jnp.sum(mapped * member, axis=(1, 2)) for member in krylov_basis]
        projections = lax.psum(jnp.stack(local_dots), ("dom", "blk"))
        for row_index in range(len(krylov_basis)):
            mapped = mapped - projections[row_index][:, None, None] * krylov_basis[row_index]
        new_norm = jnp.sqrt(lax.psum(jnp.sum(mapped * mapped, axis=(1, 2)), ("dom", "blk")))
        hessen.append(jnp.concatenate([projections, new_norm[None, :]], axis=0))
        krylov_basis.append(mapped / new_norm[:, None, None])
    coeffs, rel_residual = least_squares(hessen, start_norm)
    combined = coeffs[0][:, None, None] * krylov_basis[0]
    for col_index in range(1, ITERS):
        combined = combined + coeffs[col_index][:, None, None] * krylov_basis[col_index]
    return (precondition(combined), rel_residual)


CELLS = EX * EY
F32 = jnp.float32
BF16 = jnp.bfloat16
VMEM_LIMIT = 40 * 1024 * 1024
OUT_CELLS = ((0, 1), (2, 3), (0, 2), (1, 3))
PIVOT_FLOOR = 0.02
RESIDUAL_FLOOR = 0.02


def pair_lane(row, col):
    return row * (row + 1) // 2 + col


def split_halves(value):
    high = value.astype(BF16)
    low = (value - high.astype(F32)).astype(BF16)
    return high, low


def dot32(left, right):
    return jnp.dot(left, right, preferred_element_type=F32)


def dot_full(left, right):
    return jnp.dot(left, right, preferred_element_type=F32, precision=HIGH)


def stack_halves(vector):
    high, low = split_halves(vector)
    return jnp.concatenate([high, low], axis=0), high


def row_times(stacked, high, block_high, block_low):
    rows = high.shape[0]
    both = dot32(stacked, block_high)
    return both[:rows] + both[rows:] + dot32(high, block_low)


def write_sends(halves, out_high_ref, out_low_ref, send_refs):
    for way in range(4):
        for place in range(2):
            stacked, high = halves[OUT_CELLS[way][place]]
            slot = 2 * way + place
            send_refs[way][place] = row_times(
                stacked, high, out_high_ref[slot], out_low_ref[slot]
            )


def setup_kernel(
    nbr_ref, flag_ref, src_ref, diag_ref, face_ref,
    out_high_ref, out_low_ref, loc_high_ref, loc_low_ref, inv_high_ref, inv_low_ref,
    base_ref, send0_ref, send1_ref, send2_ref, send3_ref, slot_ref,
    center_ref, x_ref, y_ref, cell_ref, face_of_ref,
    *, dom_count, blk_count,
):
    width = diag_ref.shape[-1]
    dom_here = lax.axis_index("dom")
    blk_here = lax.axis_index("blk")
    here = dom_here * blk_count + blk_here
    for slot in range(CELLS):
        up_x = jnp.int32(0)
        down_x = jnp.int32(0)
        up_y = jnp.int32(0)
        down_y = jnp.int32(0)
        for face in range(6):
            other = nbr_ref[slot, face]
            gap = jnp.where(other >= 0, other // CELLS - here, 0)
            up_x = jnp.where(gap == blk_count, 1, up_x)
            down_x = jnp.where(gap == -blk_count, 1, down_x)
            up_y = jnp.where(gap == 1, 1, up_y)
            down_y = jnp.where(gap == -1, 1, down_y)
        cell_x = jnp.where(dom_here < dom_count - 1, up_x, 1 - down_x)
        cell_y = jnp.where(blk_here < blk_count - 1, up_y, 1 - down_y)
        cell = 2 * cell_x + cell_y
        cell_ref[slot] = cell
        slot_ref[cell] = slot
    for entry in range(CELLS * 4):
        face_of_ref[entry] = -1
    for slot in range(CELLS):
        cell = cell_ref[slot]
        for face in range(6):
            other = nbr_ref[slot, face]
            inside = other >= 0
            safe = jnp.where(inside, other, 0)
            gap = safe // CELLS - here
            mate = cell_ref[safe % CELLS]
            change = jnp.bitwise_xor(mate, cell)
            way_x = jnp.where(cell >= 2, 0, 1)
            way_y = jnp.where(cell % 2 == 1, 2, 3)
            way_in = jnp.where(change == 2, way_x, way_y)
            way = jnp.where(
                gap == 0, way_in,
                jnp.where(
                    gap == -blk_count, 0,
                    jnp.where(gap == blk_count, 1, jnp.where(gap == -1, 2, 3)),
                ),
            )

            @pl.when(inside)
            def _():
                face_of_ref[cell * 4 + way] = face

    rows = lax.broadcasted_iota(jnp.int32, (width, width), 0)
    cols = lax.broadcasted_iota(jnp.int32, (width, width), 1)
    on_diag = rows == cols
    for cell in range(CELLS):
        slot = slot_ref[cell]
        center = diag_ref[slot]
        for face in range(6):
            wall = jnp.where(flag_ref[slot, face] == 1, 1.0, 0.0).astype(F32)
            center = center + wall * face_ref[slot, face]
        center_ref[cell] = center
        marked = jnp.where(on_diag, center, 0.0)
        inv_row = 1.0 / jnp.sum(marked, axis=0, keepdims=True)
        inv_col = 1.0 / jnp.sum(marked, axis=1, keepdims=True)
        first = jnp.where(on_diag, inv_col, 0.0)
        x_ref[cell] = 2.0 * first - inv_col * (center * inv_row)
    for sweep in range(SWEEPS - 1):
        for cell in range(CELLS):
            y_ref[cell] = dot_full(center_ref[cell], x_ref[cell])
        for cell in range(CELLS):
            x_ref[cell] = 2.0 * x_ref[cell] - dot_full(x_ref[cell], y_ref[cell])
    halves = []
    for cell in range(CELLS):
        base = jnp.zeros(base_ref.shape[1:], F32)
        for slot in range(CELLS):
            base = jnp.where(slot_ref[cell] == slot, src_ref[:, slot, :], base)
        base_ref[cell] = base
        halves.append(stack_halves(base))
        high, low = split_halves(x_ref[cell])
        inv_high_ref[cell] = high
        inv_low_ref[cell] = low
        own = dot_full(x_ref[cell], center_ref[cell]) - jnp.where(on_diag, 1.0, 0.0)
        high, low = split_halves(own)
        loc_high_ref[cell] = high
        loc_low_ref[cell] = low
        slot = slot_ref[cell]
        for way in range(4):
            face = face_of_ref[cell * 4 + way]
            keep = jnp.where(face >= 0, 1.0, 0.0).astype(F32)
            block = face_ref[slot, jnp.maximum(face, 0)] * keep
            f_high, f_low = split_halves(block)
            product = (
                dot32(inv_high_ref[cell], f_high)
                + dot32(inv_low_ref[cell], f_high)
                + dot32(inv_high_ref[cell], f_low)
            )
            high, low = split_halves(product)
            if cell in OUT_CELLS[way]:
                entry = 2 * way + OUT_CELLS[way].index(cell)
                out_high_ref[entry] = high
                out_low_ref[entry] = low
            else:
                entry = (4 if way < 2 else 8) + cell
                loc_high_ref[entry] = high
                loc_low_ref[entry] = low
    write_sends(halves, out_high_ref, out_low_ref, (send0_ref, send1_ref, send2_ref, send3_ref))


def local_kernel(step, base_refs, loc_high_ref, loc_low_ref, gram_in_ref, acc_ref, gram_ref):
    newest = base_refs[step]
    halves = [stack_halves(newest[cell]) for cell in range(CELLS)]
    for cell in range(CELLS):
        total = None
        for source, entry in ((cell, cell), (cell ^ 2, 4 + (cell ^ 2)), (cell ^ 1, 8 + (cell ^ 1))):
            stacked, high = halves[source]
            part = row_times(stacked, high, loc_high_ref[entry], loc_low_ref[entry])
            total = part if total is None else total + part
        acc_ref[cell] = total
    gram_ref[...] = gram_rows(step, base_refs, None if gram_in_ref is None else gram_in_ref[...])


def gram_rows(step, base_refs, gram):
    newest = base_refs[step]
    nrhs = newest.shape[1]
    lanes = lax.broadcasted_iota(jnp.int32, (nrhs, 128), 1)
    if gram is None:
        gram = jnp.zeros((nrhs, 128), F32)
    for col in range(step + 1):
        total = newest[0] * base_refs[col][0]
        for cell in range(1, CELLS):
            total = total + newest[cell] * base_refs[col][cell]
        value = jnp.sum(total, axis=1, keepdims=True)
        gram = jnp.where(lanes == pair_lane(step, col), value, gram)
    return gram


def add_received(acc_ref, recv_refs, base_ref):
    from_dom_prev, from_dom_next, from_blk_prev, from_blk_next = recv_refs
    for cell in range(CELLS):
        dom_part = from_dom_prev[cell % 2] if cell < 2 else from_dom_next[cell % 2]
        blk_part = from_blk_prev[cell // 2] if cell % 2 == 0 else from_blk_next[cell // 2]
        base_ref[cell] = acc_ref[cell] + dom_part + blk_part


def border_kernel(
    acc_ref, recv0_ref, recv1_ref, recv2_ref, recv3_ref, out_high_ref, out_low_ref,
    base_ref, send0_ref, send1_ref, send2_ref, send3_ref,
):
    add_received(acc_ref, (recv0_ref, recv1_ref, recv2_ref, recv3_ref), base_ref)
    halves = [stack_halves(base_ref[cell]) for cell in range(CELLS)]
    write_sends(halves, out_high_ref, out_low_ref, (send0_ref, send1_ref, send2_ref, send3_ref))


def last_kernel(*refs):
    acc_ref, recv0_ref, recv1_ref, recv2_ref, recv3_ref = refs[:5]
    gram_in_ref = refs[5]
    older = refs[6 : 6 + ITERS]
    gram_ref, base_ref = refs[6 + ITERS :]
    add_received(acc_ref, (recv0_ref, recv1_ref, recv2_ref, recv3_ref), base_ref)
    gram_ref[...] = gram_rows(ITERS, list(older) + [base_ref], gram_in_ref[...])


def finish_kernel(*refs):
    gram_ref = refs[0]
    base_refs = refs[1 : 1 + ITERS]
    inv_high_ref, inv_low_ref, slot_ref, adjoint_ref, rel_ref, fine_ref = refs[1 + ITERS :]
    count = ITERS + 1
    gram = gram_ref[...]

    def lane(row, col):
        place = pair_lane(row, col)
        return jnp.broadcast_to(gram[:, place : place + 1], gram.shape)

    diag = [lane(j, j) for j in range(count)]
    scale = [1.0 / jnp.sqrt(value) for value in diag]
    start = jnp.sqrt(diag[0])
    lower = [[None] * count for j in range(count)]
    solved = []
    ratio = [scale[j] * start for j in range(count)]
    smallest = jnp.ones_like(gram)
    inv_pivot = []
    for col in range(count):
        pivot = jnp.ones_like(gram)
        for k in range(col):
            pivot = pivot - lower[col][k] * lower[col][k]
        smallest = jnp.minimum(smallest, pivot)
        inv_root = 1.0 / jnp.sqrt(pivot)
        inv_pivot.append(inv_root)
        for row in range(col + 1, count):
            value = lane(row, col) * scale[row] * scale[col]
            for k in range(col):
                value = value - lower[row][k] * lower[col][k]
            lower[row][col] = value * inv_root
        right = ratio[col] if col % 2 == 0 else -ratio[col]
        for k in range(col):
            right = right - lower[col][k] * solved[k]
        solved.append(right * inv_root)
    squares = solved[0] * solved[0]
    for j in range(1, count):
        squares = squares + solved[j] * solved[j]
    rel = 1.0 / jnp.sqrt(squares)
    back = [None] * count
    for j in reversed(range(count)):
        value = solved[j]
        for k in range(j + 1, count):
            value = value - lower[k][j] * back[k]
        back[j] = value * inv_pivot[j]
    inv_squares = 1.0 / squares
    residual = [ratio[j] * back[j] * inv_squares for j in range(count)]
    coeffs = [None] * ITERS
    coeffs[ITERS - 1] = -residual[ITERS]
    for j in reversed(range(1, ITERS)):
        coeffs[j - 1] = -residual[j] - coeffs[j]
    lanes = lax.broadcasted_iota(jnp.int32, gram.shape, 1)
    good = (smallest > PIVOT_FLOOR) & (rel > RESIDUAL_FLOOR) & (rel < 2.0)
    for j in range(count):
        good = good & (diag[j] > 1e-30) & (diag[j] < 1e36)
    worst = jnp.min(jnp.where(good, 1.0, 0.0))
    fine_ref[0] = jnp.where(worst > 0.5, 1, 0).astype(jnp.int32)
    rel_ref[...] = jnp.transpose(rel)[0:1, :]
    width = base_refs[0].shape[-1]
    wide = [
        jnp.concatenate([value, value], axis=1)[:, :width] for value in coeffs
    ]
    results = []
    for cell in range(CELLS):
        total = wide[0] * base_refs[0][cell]
        for j in range(1, ITERS):
            total = total + wide[j] * base_refs[j][cell]
        stacked, high = stack_halves(total)
        results.append(row_times(stacked, high, inv_high_ref[cell], inv_low_ref[cell]))
    for slot in range(CELLS):
        value = results[0]
        for cell in range(1, CELLS):
            value = jnp.where(slot_ref[cell] == slot, results[cell], value)
        adjoint_ref[:, slot, :] = value


def vmem(count):
    return [pl.BlockSpec(memory_space=pltpu.VMEM)] * count


def smem(count):
    return [pl.BlockSpec(memory_space=pltpu.SMEM)] * count


PARAMS = pltpu.CompilerParams(vmem_limit_bytes=VMEM_LIMIT)


def struct(*shape, kind=F32):
    return jax.ShapeDtypeStruct(shape, kind)


def group_sizes(count):
    return (16, count // 16) if count > 16 and count % 16 == 0 else (count,)


def sum_over(value, axis):
    count = lax.axis_size(axis)
    stride = 1
    for size in group_sizes(count):
        groups = [
            [high * size * stride + k * stride + low for k in range(size)]
            for high in range(count // (size * stride))
            for low in range(stride)
        ]
        copies = jnp.broadcast_to(value[None], (size,) + value.shape)
        parts = lax.all_to_all(
            copies, axis, 0, 0, axis_index_groups=None if size == count else groups
        )
        value = jnp.sum(parts, axis=0)
        stride *= size
    return value


def exchange(sends):
    to_dom_prev, to_dom_next, to_blk_prev, to_blk_next = sends
    return (
        shifted(to_dom_next, "dom", 1),
        shifted(to_dom_prev, "dom", -1),
        shifted(to_blk_next, "blk", 1),
        shifted(to_blk_prev, "blk", -1),
    )


def shards(adjoint_source, diag_blocks, face_blocks, neighbors, partner, flags):
    nrhs, elements, width = adjoint_source.shape
    block = (width, width)
    field = struct(CELLS, nrhs, width)
    edge = struct(2, nrhs, width)
    cost = lambda flops, data: pl.CostEstimate(
        flops=flops, bytes_accessed=data, transcendentals=0
    )
    products = 2 * nrhs * width * width * 3
    setup = pl.pallas_call(
        functools.partial(
            setup_kernel, dom_count=lax.axis_size("dom"), blk_count=lax.axis_size("blk")
        ),
        out_shape=(
            struct(8, *block, kind=BF16), struct(8, *block, kind=BF16),
            struct(12, *block, kind=BF16), struct(12, *block, kind=BF16),
            struct(CELLS, *block, kind=BF16), struct(CELLS, *block, kind=BF16),
            field, edge, edge, edge, edge, struct(CELLS, kind=jnp.int32),
        ),
        in_specs=smem(2) + vmem(3),
        out_specs=tuple(vmem(11) + smem(1)),
        scratch_shapes=[
            pltpu.VMEM((CELLS,) + block, F32),
            pltpu.VMEM((CELLS,) + block, F32),
            pltpu.VMEM((CELLS,) + block, F32),
            pltpu.SMEM((CELLS,), jnp.int32),
            pltpu.SMEM((CELLS * 4,), jnp.int32),
        ],
        compiler_params=PARAMS,
        name="setup_blocks",
    )
    outs = setup(neighbors, flags, adjoint_source, diag_blocks, face_blocks)
    out_high, out_low, loc_high, loc_low, inv_high, inv_low = outs[:6]
    bases = [outs[6]]
    sends = outs[7:11]
    slots = outs[11]
    gram = None
    for step in range(ITERS):
        received = exchange(sends)

        def local_body(*refs, step=step):
            has_gram = step > 0
            base_refs = refs[: step + 1]
            loc_refs = refs[step + 1 : step + 3]
            gram_in = refs[step + 3] if has_gram else None
            local_kernel(step, base_refs, *loc_refs, gram_in, *refs[-2:])

        given = bases + [loc_high, loc_low] + ([gram] if step > 0 else [])
        acc, gram = pl.pallas_call(
            local_body,
            out_shape=(field, struct(nrhs, 128)),
            in_specs=vmem(len(given)),
            out_specs=tuple(vmem(2)),
            compiler_params=PARAMS,
            cost_estimate=cost(12 * products, 3000000),
            name=f"local_part_{step}",
        )(*given)
        if step < ITERS - 1:
            outs = pl.pallas_call(
                border_kernel,
                out_shape=(field, edge, edge, edge, edge),
                in_specs=vmem(7),
                out_specs=tuple(vmem(5)),
                compiler_params=PARAMS,
                cost_estimate=cost(8 * products, 2000000),
                name=f"border_part_{step}",
            )(acc, *received, out_high, out_low)
            bases.append(outs[0])
            sends = outs[1:]
        else:
            given = [acc, *received, gram] + bases
            gram, _ = pl.pallas_call(
                last_kernel,
                out_shape=(struct(nrhs, 128), field),
                in_specs=vmem(len(given)),
                out_specs=tuple(vmem(2)),
                compiler_params=PARAMS,
                name="last_part",
            )(*given)
    gram = sum_over(gram, "blk")
    gram = sum_over(gram, "dom")
    given = [gram] + bases + [inv_high, inv_low, slots]
    adjoint, rel, fine = pl.pallas_call(
        finish_kernel,
        out_shape=(
            struct(nrhs, elements, width), struct(1, nrhs), struct(1, kind=jnp.int32)
        ),
        in_specs=vmem(len(given) - 1) + smem(1),
        out_specs=tuple(vmem(2) + smem(1)),
        compiler_params=PARAMS,
        name="finish_part",
    )(*given)
    return lax.cond(
        fine[0] == 1,
        lambda given: (adjoint, rel.reshape(nrhs)),
        lambda given: direct_path(*given),
        (adjoint_source, diag_blocks, face_blocks, neighbors, partner, flags),
    )


def solution(mesh):
    in_specs = (
        P(None, ("dom", "blk"), None),
        P(("dom", "blk"), None, None),
        P(("dom", "blk"), None, None, None),
        P(("dom", "blk"), None),
        P(("dom", "blk"), None),
        P(("dom", "blk"), None),
    )
    out_specs = (P(None, ("dom", "blk"), None), P())
    return jax.shard_map(shards, mesh=mesh, in_specs=in_specs, out_specs=out_specs, check_vma=False)
```

```python
import functools

import jax
import jax.numpy as jnp
from jax import lax
from jax.experimental import pallas as pl
from jax.experimental.pallas import tpu as pltpu
from jax.sharding import PartitionSpec as P

EX = 2
EY = 2
ITERS = 8
SWEEPS = 3


HIGH = lax.Precision.HIGHEST


def shifted(value, axis, steps):
    count = lax.axis_size(axis)
    leading, last = (max(0, -steps), min(count, count - steps))
    return lax.ppermute(value, axis, [(source, source + steps) for source in range(leading, last)])


def invert_blocks(center):
    width = center.shape[-1]
    identity = jnp.eye(width, dtype=center.dtype)
    pivots = jnp.diagonal(center, axis1=1, axis2=2)
    estimate = identity[None, :, :] / pivots[:, :, None]
    for sweep_index in range(SWEEPS):
        product = jnp.einsum("eab,ebc->eac", center, estimate, precision=HIGH)
        estimate = 2.0 * estimate - jnp.einsum("eab,ebc->eac", estimate, product, precision=HIGH)
    return estimate


def least_squares(hessen, start_norm):
    count = len(hessen)
    cosines = []
    sines = []
    rotated_rhs = [start_norm] + [jnp.zeros_like(start_norm) for row_index in range(count)]
    upper = []
    for col_index in range(count):
        column = [hessen[col_index][row_index] for row_index in range(col_index + 2)]
        for row_index in range(col_index):
            rotated = (
                cosines[row_index] * column[row_index] + sines[row_index] * column[row_index + 1]
            )
            column[row_index + 1] = (
                -sines[row_index] * column[row_index] + cosines[row_index] * column[row_index + 1]
            )
            column[row_index] = rotated
        radius = jnp.sqrt(
            column[col_index] * column[col_index] + column[col_index + 1] * column[col_index + 1]
        )
        cosine = column[col_index] / radius
        sine_value = column[col_index + 1] / radius
        column[col_index] = radius
        cosines.append(cosine)
        sines.append(sine_value)
        rotated_rhs[col_index + 1] = -sine_value * rotated_rhs[col_index]
        rotated_rhs[col_index] = cosine * rotated_rhs[col_index]
        upper.append(column[: col_index + 1])
    coeffs = [None] * count
    for row_index in reversed(range(count)):
        total = rotated_rhs[row_index]
        for col_index in range(row_index + 1, count):
            total = total - upper[col_index][row_index] * coeffs[col_index]
        coeffs[row_index] = total / upper[row_index][row_index]
    return (coeffs, jnp.abs(rotated_rhs[count]) / start_norm)


def move_vectors_dom(vectors, offset):
    return shifted(vectors, "dom", offset)


def move_vectors_blk(vectors, offset):
    return shifted(vectors, "blk", offset)


def move_facing_dom(blocks, offset):
    return shifted(blocks, "dom", offset)


def move_facing_blk(blocks, offset):
    return shifted(blocks, "blk", offset)


def direct_path(adjoint_source, diag_blocks, face_blocks, neighbors, partner, flags):
    nrhs, elements, width = adjoint_source.shape
    blk_count = lax.axis_size("blk")
    dom_here = lax.axis_index("dom")
    blk_here = lax.axis_index("blk")
    wall_mask = (flags == 1).astype(jnp.float32)
    center = diag_blocks + jnp.einsum("ef,efab->eab", wall_mask, face_blocks, precision=HIGH)
    inverse = invert_blocks(center)
    inside = neighbors >= 0
    source_elem = jnp.where(inside, neighbors, 0)
    source_face = jnp.where(inside, partner, 0)
    owner_dev = source_elem // elements
    owner_dom = owner_dev // blk_count
    owner_blk = owner_dev % blk_count
    direction = jnp.where(
        owner_dom == dom_here - 1,
        1,
        jnp.where(
            owner_dom == dom_here + 1,
            2,
            jnp.where(owner_blk == blk_here - 1, 3, jnp.where(owner_blk == blk_here + 1, 4, 0)),
        ),
    )
    direction = jnp.where(inside, direction, 0).astype(jnp.int32)
    local_slot = source_elem % elements
    flat_direction = direction.reshape(-1)
    flat_inside = inside.reshape(-1)
    flat_local = (local_slot * 6 + source_face).reshape(-1)
    face_keys = (source_elem * 6 + source_face).reshape(-1)
    same_way = (flat_direction[None, :] == flat_direction[:, None]) & flat_inside[None, :]
    placing = jnp.sum(
        (same_way & (face_keys[None, :] < face_keys[:, None])).astype(jnp.int32), axis=1
    )
    offsets = jnp.array(
        [0, 6 * elements, 6 * elements + EY, 6 * elements + 2 * EY, 6 * elements + 2 * EY + EX],
        jnp.int32,
    )
    candidate = jnp.where(flat_direction == 0, flat_local, offsets[flat_direction] + placing)
    slot_range = jnp.arange(elements * 6, dtype=jnp.int32)

    def pick_rows(target, count):
        marked = ((flat_direction == target) & flat_inside).astype(jnp.int32)
        ranking = jnp.cumsum(marked) - marked
        chooser = (ranking[None, :] == jnp.arange(count)[:, None]) & (marked[None, :] > 0)
        return jnp.sum(jnp.where(chooser, slot_range[None, :], 0), axis=1)

    toward_next_dom = pick_rows(2, EY)
    toward_prev_dom = pick_rows(1, EY)
    toward_next_blk = pick_rows(4, EX)
    toward_prev_blk = pick_rows(3, EX)
    flat_blocks = face_blocks.reshape(elements * 6, width, width)
    block_pool = jnp.concatenate(
        [
            flat_blocks,
            move_facing_dom(jnp.take(flat_blocks, toward_next_dom, axis=0), 1),
            move_facing_dom(jnp.take(flat_blocks, toward_prev_dom, axis=0), -1),
            move_facing_blk(jnp.take(flat_blocks, toward_next_blk, axis=0), 1),
            move_facing_blk(jnp.take(flat_blocks, toward_prev_blk, axis=0), -1),
        ],
        axis=0,
    )
    column_blocks = (
        jnp.take(block_pool, candidate, axis=0) * flat_inside.astype(jnp.float32)[:, None, None]
    )
    column_blocks = column_blocks.reshape(elements, 6, width, width)
    vector_index = (direction * elements + local_slot).reshape(-1)

    def precondition(vectors):
        return jnp.einsum("eab,rea->reb", inverse, vectors, precision=HIGH)

    start_norm = jnp.sqrt(
        lax.psum(jnp.sum(adjoint_source * adjoint_source, axis=(1, 2)), ("dom", "blk"))
    )
    krylov_basis = [adjoint_source / start_norm[:, None, None]]
    hessen = []
    for iteration in range(ITERS):
        operator_vectors = precondition(krylov_basis[-1])
        gathered = jnp.concatenate(
            [
                operator_vectors,
                move_vectors_dom(operator_vectors, 1),
                move_vectors_dom(operator_vectors, -1),
                move_vectors_blk(operator_vectors, 1),
                move_vectors_blk(operator_vectors, -1),
            ],
            axis=1,
        )
        nearby = jnp.take(gathered, vector_index, axis=1).reshape(nrhs, elements, 6, width)
        own_part = jnp.einsum("eab,rea->reb", center, operator_vectors, precision=HIGH)
        mapped = own_part + jnp.einsum("egab,rega->reb", column_blocks, nearby, precision=HIGH)
        local_dots = [jnp.sum(mapped * member, axis=(1, 2)) for member in krylov_basis]
        projections = lax.psum(jnp.stack(local_dots), ("dom", "blk"))
        for row_index in range(len(krylov_basis)):
            mapped = mapped - projections[row_index][:, None, None] * krylov_basis[row_index]
        new_norm = jnp.sqrt(lax.psum(jnp.sum(mapped * mapped, axis=(1, 2)), ("dom", "blk")))
        hessen.append(jnp.concatenate([projections, new_norm[None, :]], axis=0))
        krylov_basis.append(mapped / new_norm[:, None, None])
    coeffs, rel_residual = least_squares(hessen, start_norm)
    combined = coeffs[0][:, None, None] * krylov_basis[0]
    for col_index in range(1, ITERS):
        combined = combined + coeffs[col_index][:, None, None] * krylov_basis[col_index]
    return (precondition(combined), rel_residual)


CELLS = EX * EY
F32 = jnp.float32
BF16 = jnp.bfloat16
VMEM_LIMIT = 40 * 1024 * 1024
OUT_CELLS = ((0, 1), (2, 3), (0, 2), (1, 3))
PIVOT_FLOOR = 0.02
RESIDUAL_FLOOR = 0.02


def pair_lane(row, col):
    return row * (row + 1) // 2 + col


def split_halves(value):
    high = value.astype(BF16)
    low = (value - high.astype(F32)).astype(BF16)
    return high, low


def dot32(left, right):
    return jnp.dot(left, right, preferred_element_type=F32)


def dot_full(left, right):
    return jnp.dot(left, right, preferred_element_type=F32, precision=HIGH)


def stack_halves(vector):
    high, low = split_halves(vector)
    return jnp.concatenate([high, low], axis=0), high


def row_times(stacked, high, block_high, block_low):
    rows = high.shape[0]
    both = dot32(stacked, block_high)
    return both[:rows] + both[rows:] + dot32(high, block_low)


def write_sends(halves, out_high_ref, out_low_ref, send_refs):
    for way in range(4):
        for place in range(2):
            stacked, high = halves[OUT_CELLS[way][place]]
            slot = 2 * way + place
            send_refs[way][place] = row_times(
                stacked, high, out_high_ref[slot], out_low_ref[slot]
            )


def setup_kernel(
    nbr_ref, flag_ref, src_ref, diag_ref, face_ref,
    out_high_ref, out_low_ref, loc_high_ref, loc_low_ref, inv_high_ref, inv_low_ref,
    base_ref, send0_ref, send1_ref, send2_ref, send3_ref, slot_ref,
    center_ref, x_ref, y_ref, cell_ref, face_of_ref,
    *, dom_count, blk_count,
):
    width = diag_ref.shape[-1]
    dom_here = lax.axis_index("dom")
    blk_here = lax.axis_index("blk")
    here = dom_here * blk_count + blk_here
    for slot in range(CELLS):
        up_x = jnp.int32(0)
        down_x = jnp.int32(0)
        up_y = jnp.int32(0)
        down_y = jnp.int32(0)
        for face in range(6):
            other = nbr_ref[slot, face]
            gap = jnp.where(other >= 0, other // CELLS - here, 0)
            up_x = jnp.where(gap == blk_count, 1, up_x)
            down_x = jnp.where(gap == -blk_count, 1, down_x)
            up_y = jnp.where(gap == 1, 1, up_y)
            down_y = jnp.where(gap == -1, 1, down_y)
        cell_x = jnp.where(dom_here < dom_count - 1, up_x, 1 - down_x)
        cell_y = jnp.where(blk_here < blk_count - 1, up_y, 1 - down_y)
        cell = 2 * cell_x + cell_y
        cell_ref[slot] = cell
        slot_ref[cell] = slot
    for entry in range(CELLS * 4):
        face_of_ref[entry] = -1
    for slot in range(CELLS):
        cell = cell_ref[slot]
        for face in range(6):
            other = nbr_ref[slot, face]
            inside = other >= 0
            safe = jnp.where(inside, other, 0)
            gap = safe // CELLS - here
            mate = cell_ref[safe % CELLS]
            change = jnp.bitwise_xor(mate, cell)
            way_x = jnp.where(cell >= 2, 0, 1)
            way_y = jnp.where(cell % 2 == 1, 2, 3)
            way_in = jnp.where(change == 2, way_x, way_y)
            way = jnp.where(
                gap == 0, way_in,
                jnp.where(
                    gap == -blk_count, 0,
                    jnp.where(gap == blk_count, 1, jnp.where(gap == -1, 2, 3)),
                ),
            )

            @pl.when(inside)
            def _():
                face_of_ref[cell * 4 + way] = face

    rows = lax.broadcasted_iota(jnp.int32, (width, width), 0)
    cols = lax.broadcasted_iota(jnp.int32, (width, width), 1)
    on_diag = rows == cols
    for cell in range(CELLS):
        slot = slot_ref[cell]
        center = diag_ref[slot]
        for face in range(6):
            wall = jnp.where(flag_ref[slot, face] == 1, 1.0, 0.0).astype(F32)
            center = center + wall * face_ref[slot, face]
        center_ref[cell] = center
        marked = jnp.where(on_diag, center, 0.0)
        inv_row = 1.0 / jnp.sum(marked, axis=0, keepdims=True)
        inv_col = 1.0 / jnp.sum(marked, axis=1, keepdims=True)
        first = jnp.where(on_diag, inv_col, 0.0)
        x_ref[cell] = 2.0 * first - inv_col * (center * inv_row)
    for sweep in range(SWEEPS - 1):
        for cell in range(CELLS):
            y_ref[cell] = dot_full(center_ref[cell], x_ref[cell])
        for cell in range(CELLS):
            x_ref[cell] = 2.0 * x_ref[cell] - dot_full(x_ref[cell], y_ref[cell])
    halves = []
    for cell in range(CELLS):
        base = jnp.zeros(base_ref.shape[1:], F32)
        for slot in range(CELLS):
            base = jnp.where(slot_ref[cell] == slot, src_ref[:, slot, :], base)
        base_ref[cell] = base
        halves.append(stack_halves(base))
        high, low = split_halves(x_ref[cell])
        inv_high_ref[cell] = high
        inv_low_ref[cell] = low
        own = dot_full(x_ref[cell], center_ref[cell]) - jnp.where(on_diag, 1.0, 0.0)
        high, low = split_halves(own)
        loc_high_ref[cell] = high
        loc_low_ref[cell] = low
        slot = slot_ref[cell]
        for way in range(4):
            face = face_of_ref[cell * 4 + way]
            keep = jnp.where(face >= 0, 1.0, 0.0).astype(F32)
            block = face_ref[slot, jnp.maximum(face, 0)] * keep
            f_high, f_low = split_halves(block)
            product = (
                dot32(inv_high_ref[cell], f_high)
                + dot32(inv_low_ref[cell], f_high)
                + dot32(inv_high_ref[cell], f_low)
            )
            high, low = split_halves(product)
            if cell in OUT_CELLS[way]:
                entry = 2 * way + OUT_CELLS[way].index(cell)
                out_high_ref[entry] = high
                out_low_ref[entry] = low
            else:
                entry = (4 if way < 2 else 8) + cell
                loc_high_ref[entry] = high
                loc_low_ref[entry] = low
    write_sends(halves, out_high_ref, out_low_ref, (send0_ref, send1_ref, send2_ref, send3_ref))


def local_kernel(step, base_refs, loc_high_ref, loc_low_ref, gram_in_ref, acc_ref, gram_ref):
    newest = base_refs[step]
    halves = [stack_halves(newest[cell]) for cell in range(CELLS)]
    for cell in range(CELLS):
        total = None
        for source, entry in ((cell, cell), (cell ^ 2, 4 + (cell ^ 2)), (cell ^ 1, 8 + (cell ^ 1))):
            stacked, high = halves[source]
            part = row_times(stacked, high, loc_high_ref[entry], loc_low_ref[entry])
            total = part if total is None else total + part
        acc_ref[cell] = total
    gram_ref[...] = gram_rows(step, base_refs, None if gram_in_ref is None else gram_in_ref[...])


def gram_rows(step, base_refs, gram):
    newest = base_refs[step]
    nrhs = newest.shape[1]
    lanes = lax.broadcasted_iota(jnp.int32, (nrhs, 128), 1)
    if gram is None:
        gram = jnp.zeros((nrhs, 128), F32)
    for col in range(step + 1):
        total = newest[0] * base_refs[col][0]
        for cell in range(1, CELLS):
            total = total + newest[cell] * base_refs[col][cell]
        value = jnp.sum(total, axis=1, keepdims=True)
        gram = jnp.where(lanes == pair_lane(step, col), value, gram)
    return gram


def add_received(acc_ref, recv_refs, base_ref):
    from_dom_prev, from_dom_next, from_blk_prev, from_blk_next = recv_refs
    for cell in range(CELLS):
        dom_part = from_dom_prev[cell % 2] if cell < 2 else from_dom_next[cell % 2]
        blk_part = from_blk_prev[cell // 2] if cell % 2 == 0 else from_blk_next[cell // 2]
        base_ref[cell] = acc_ref[cell] + dom_part + blk_part


def border_kernel(
    acc_ref, recv0_ref, recv1_ref, recv2_ref, recv3_ref, out_high_ref, out_low_ref,
    base_ref, send0_ref, send1_ref, send2_ref, send3_ref,
):
    add_received(acc_ref, (recv0_ref, recv1_ref, recv2_ref, recv3_ref), base_ref)
    halves = [stack_halves(base_ref[cell]) for cell in range(CELLS)]
    write_sends(halves, out_high_ref, out_low_ref, (send0_ref, send1_ref, send2_ref, send3_ref))


def last_kernel(*refs):
    acc_ref, recv0_ref, recv1_ref, recv2_ref, recv3_ref = refs[:5]
    gram_in_ref = refs[5]
    older = refs[6 : 6 + ITERS]
    gram_ref, base_ref = refs[6 + ITERS :]
    add_received(acc_ref, (recv0_ref, recv1_ref, recv2_ref, recv3_ref), base_ref)
    gram = gram_rows(ITERS, list(older) + [base_ref], gram_in_ref[...])
    half = gram.shape[0] // 2
    gram_ref[...] = gram[:half] + pltpu.roll(gram[half:], 64, 1)


def finish_kernel(*refs):
    gram_ref = refs[0]
    base_refs = refs[1 : 1 + ITERS]
    inv_high_ref, inv_low_ref, slot_ref, adjoint_ref, rel_ref, fine_ref = refs[1 + ITERS :]
    count = ITERS + 1
    packed = gram_ref[...]
    gram = jnp.concatenate([packed, pltpu.roll(packed, 64, 1)], axis=0)

    def lane(row, col):
        place = pair_lane(row, col)
        return jnp.broadcast_to(gram[:, place : place + 1], gram.shape)

    diag = [lane(j, j) for j in range(count)]
    scale = [1.0 / jnp.sqrt(value) for value in diag]
    start = jnp.sqrt(diag[0])
    lower = [[None] * count for j in range(count)]
    solved = []
    ratio = [scale[j] * start for j in range(count)]
    smallest = jnp.ones_like(gram)
    inv_pivot = []
    for col in range(count):
        pivot = jnp.ones_like(gram)
        for k in range(col):
            pivot = pivot - lower[col][k] * lower[col][k]
        smallest = jnp.minimum(smallest, pivot)
        inv_root = 1.0 / jnp.sqrt(pivot)
        inv_pivot.append(inv_root)
        for row in range(col + 1, count):
            value = lane(row, col) * scale[row] * scale[col]
            for k in range(col):
                value = value - lower[row][k] * lower[col][k]
            lower[row][col] = value * inv_root
        right = ratio[col] if col % 2 == 0 else -ratio[col]
        for k in range(col):
            right = right - lower[col][k] * solved[k]
        solved.append(right * inv_root)
    squares = solved[0] * solved[0]
    for j in range(1, count):
        squares = squares + solved[j] * solved[j]
    rel = 1.0 / jnp.sqrt(squares)
    back = [None] * count
    for j in reversed(range(count)):
        value = solved[j]
        for k in range(j + 1, count):
            value = value - lower[k][j] * back[k]
        back[j] = value * inv_pivot[j]
    inv_squares = 1.0 / squares
    residual = [ratio[j] * back[j] * inv_squares for j in range(count)]
    coeffs = [None] * ITERS
    coeffs[ITERS - 1] = -residual[ITERS]
    for j in reversed(range(1, ITERS)):
        coeffs[j - 1] = -residual[j] - coeffs[j]
    lanes = lax.broadcasted_iota(jnp.int32, gram.shape, 1)
    good = (smallest > PIVOT_FLOOR) & (rel > RESIDUAL_FLOOR) & (rel < 2.0)
    for j in range(count):
        good = good & (diag[j] > 1e-30) & (diag[j] < 1e36)
    worst = jnp.min(jnp.where(good, 1.0, 0.0))
    fine_ref[0] = jnp.where(worst > 0.5, 1, 0).astype(jnp.int32)
    rel_ref[...] = jnp.transpose(rel)[0:1, :]
    width = base_refs[0].shape[-1]
    wide = [
        jnp.concatenate([value, value], axis=1)[:, :width] for value in coeffs
    ]
    results = []
    for cell in range(CELLS):
        total = wide[0] * base_refs[0][cell]
        for j in range(1, ITERS):
            total = total + wide[j] * base_refs[j][cell]
        stacked, high = stack_halves(total)
        results.append(row_times(stacked, high, inv_high_ref[cell], inv_low_ref[cell]))
    for slot in range(CELLS):
        value = results[0]
        for cell in range(1, CELLS):
            value = jnp.where(slot_ref[cell] == slot, results[cell], value)
        adjoint_ref[:, slot, :] = value


def vmem(count):
    return [pl.BlockSpec(memory_space=pltpu.VMEM)] * count


def smem(count):
    return [pl.BlockSpec(memory_space=pltpu.SMEM)] * count


PARAMS = pltpu.CompilerParams(vmem_limit_bytes=VMEM_LIMIT)


def struct(*shape, kind=F32):
    return jax.ShapeDtypeStruct(shape, kind)


def sum_groups(value, axes, groups):
    size = len(groups[0])
    copies = jnp.broadcast_to(value[None], (size,) + value.shape)
    parts = lax.all_to_all(
        copies, axes, 0, 0, axis_index_groups=groups if len(groups) > 1 else None
    )
    return jnp.sum(parts, axis=0)


def sum_devices(value):
    dom_count, blk_count = (lax.axis_size("dom"), lax.axis_size("blk"))
    inner = 4 if dom_count % 4 == 0 else dom_count
    size = inner * blk_count
    near = [
        [first + k for k in range(size)] for first in range(0, dom_count * blk_count, size)
    ]
    value = sum_groups(value, ("dom", "blk"), near)
    if inner < dom_count:
        far = [[first + k for k in range(0, dom_count, inner)] for first in range(inner)]
        value = sum_groups(value, "dom", far)
    return value


def rotated(value, axis, steps):
    count = lax.axis_size(axis)
    return lax.ppermute(
        value, axis, [(source, (source + steps) % count) for source in range(count)]
    )


def exchange(sends):
    to_dom_prev, to_dom_next, to_blk_prev, to_blk_next = sends
    return (
        rotated(to_dom_next, "dom", 1),
        rotated(to_dom_prev, "dom", -1),
        rotated(to_blk_next, "blk", 1),
        rotated(to_blk_prev, "blk", -1),
    )


def shards(adjoint_source, diag_blocks, face_blocks, neighbors, partner, flags):
    nrhs, elements, width = adjoint_source.shape
    block = (width, width)
    field = struct(CELLS, nrhs, width)
    edge = struct(2, nrhs, width)
    cost = lambda flops, data: pl.CostEstimate(
        flops=flops, bytes_accessed=data, transcendentals=0
    )
    products = 2 * nrhs * width * width * 3
    setup = pl.pallas_call(
        functools.partial(
            setup_kernel, dom_count=lax.axis_size("dom"), blk_count=lax.axis_size("blk")
        ),
        out_shape=(
            struct(8, *block, kind=BF16), struct(8, *block, kind=BF16),
            struct(12, *block, kind=BF16), struct(12, *block, kind=BF16),
            struct(CELLS, *block, kind=BF16), struct(CELLS, *block, kind=BF16),
            field, edge, edge, edge, edge, struct(CELLS, kind=jnp.int32),
        ),
        in_specs=smem(2) + vmem(3),
        out_specs=tuple(vmem(11) + smem(1)),
        scratch_shapes=[
            pltpu.VMEM((CELLS,) + block, F32),
            pltpu.VMEM((CELLS,) + block, F32),
            pltpu.VMEM((CELLS,) + block, F32),
            pltpu.SMEM((CELLS,), jnp.int32),
            pltpu.SMEM((CELLS * 4,), jnp.int32),
        ],
        compiler_params=PARAMS,
        name="setup_blocks",
    )
    outs = setup(neighbors, flags, adjoint_source, diag_blocks, face_blocks)
    out_high, out_low, loc_high, loc_low, inv_high, inv_low = outs[:6]
    bases = [outs[6]]
    sends = outs[7:11]
    slots = outs[11]
    gram = None
    for step in range(ITERS):
        received = exchange(sends)

        def local_body(*refs, step=step):
            has_gram = step > 0
            base_refs = refs[: step + 1]
            loc_refs = refs[step + 1 : step + 3]
            gram_in = refs[step + 3] if has_gram else None
            local_kernel(step, base_refs, *loc_refs, gram_in, *refs[-2:])

        given = bases + [loc_high, loc_low] + ([gram] if step > 0 else [])
        acc, gram = pl.pallas_call(
            local_body,
            out_shape=(field, struct(nrhs, 128)),
            in_specs=vmem(len(given)),
            out_specs=tuple(vmem(2)),
            compiler_params=PARAMS,
            cost_estimate=cost(12 * products, 3000000),
            name=f"local_part_{step}",
        )(*given)
        if step < ITERS - 1:
            outs = pl.pallas_call(
                border_kernel,
                out_shape=(field, edge, edge, edge, edge),
                in_specs=vmem(7),
                out_specs=tuple(vmem(5)),
                compiler_params=PARAMS,
                cost_estimate=cost(8 * products, 2000000),
                name=f"border_part_{step}",
            )(acc, *received, out_high, out_low)
            bases.append(outs[0])
            sends = outs[1:]
        else:
            given = [acc, *received, gram] + bases
            gram, _ = pl.pallas_call(
                last_kernel,
                out_shape=(struct(nrhs // 2, 128), field),
                in_specs=vmem(len(given)),
                out_specs=tuple(vmem(2)),
                compiler_params=PARAMS,
                name="last_part",
            )(*given)
    gram = sum_devices(gram)
    given = [gram] + bases + [inv_high, inv_low, slots]
    adjoint, rel, fine = pl.pallas_call(
        finish_kernel,
        out_shape=(
            struct(nrhs, elements, width), struct(1, nrhs), struct(1, kind=jnp.int32)
        ),
        in_specs=vmem(len(given) - 1) + smem(1),
        out_specs=tuple(vmem(2) + smem(1)),
        compiler_params=PARAMS,
        name="finish_part",
    )(*given)
    return lax.cond(
        fine[0] == 1,
        lambda given: (adjoint, rel.reshape(nrhs)),
        lambda given: direct_path(*given),
        (adjoint_source, diag_blocks, face_blocks, neighbors, partner, flags),
    )


def solution(mesh):
    in_specs = (
        P(None, ("dom", "blk"), None),
        P(("dom", "blk"), None, None),
        P(("dom", "blk"), None, None, None),
        P(("dom", "blk"), None),
        P(("dom", "blk"), None),
        P(("dom", "blk"), None),
    )
    out_specs = (P(None, ("dom", "blk"), None), P())
    return jax.shard_map(shards, mesh=mesh, in_specs=in_specs, out_specs=out_specs, check_vma=False)
```

```python
import functools

import jax
import jax.numpy as jnp
from jax import lax
from jax.experimental import pallas as pl
from jax.experimental.pallas import tpu as pltpu
from jax.sharding import PartitionSpec as P

EX = 2
EY = 2
ITERS = 8
SWEEPS = 3


HIGH = lax.Precision.HIGHEST


def shifted(value, axis, steps):
    count = lax.axis_size(axis)
    leading, last = (max(0, -steps), min(count, count - steps))
    return lax.ppermute(value, axis, [(source, source + steps) for source in range(leading, last)])


def invert_blocks(center):
    width = center.shape[-1]
    identity = jnp.eye(width, dtype=center.dtype)
    pivots = jnp.diagonal(center, axis1=1, axis2=2)
    estimate = identity[None, :, :] / pivots[:, :, None]
    for sweep_index in range(SWEEPS):
        product = jnp.einsum("eab,ebc->eac", center, estimate, precision=HIGH)
        estimate = 2.0 * estimate - jnp.einsum("eab,ebc->eac", estimate, product, precision=HIGH)
    return estimate


def least_squares(hessen, start_norm):
    count = len(hessen)
    cosines = []
    sines = []
    rotated_rhs = [start_norm] + [jnp.zeros_like(start_norm) for row_index in range(count)]
    upper = []
    for col_index in range(count):
        column = [hessen[col_index][row_index] for row_index in range(col_index + 2)]
        for row_index in range(col_index):
            rotated = (
                cosines[row_index] * column[row_index] + sines[row_index] * column[row_index + 1]
            )
            column[row_index + 1] = (
                -sines[row_index] * column[row_index] + cosines[row_index] * column[row_index + 1]
            )
            column[row_index] = rotated
        radius = jnp.sqrt(
            column[col_index] * column[col_index] + column[col_index + 1] * column[col_index + 1]
        )
        cosine = column[col_index] / radius
        sine_value = column[col_index + 1] / radius
        column[col_index] = radius
        cosines.append(cosine)
        sines.append(sine_value)
        rotated_rhs[col_index + 1] = -sine_value * rotated_rhs[col_index]
        rotated_rhs[col_index] = cosine * rotated_rhs[col_index]
        upper.append(column[: col_index + 1])
    coeffs = [None] * count
    for row_index in reversed(range(count)):
        total = rotated_rhs[row_index]
        for col_index in range(row_index + 1, count):
            total = total - upper[col_index][row_index] * coeffs[col_index]
        coeffs[row_index] = total / upper[row_index][row_index]
    return (coeffs, jnp.abs(rotated_rhs[count]) / start_norm)


def move_vectors_dom(vectors, offset):
    return shifted(vectors, "dom", offset)


def move_vectors_blk(vectors, offset):
    return shifted(vectors, "blk", offset)


def move_facing_dom(blocks, offset):
    return shifted(blocks, "dom", offset)


def move_facing_blk(blocks, offset):
    return shifted(blocks, "blk", offset)


def direct_path(adjoint_source, diag_blocks, face_blocks, neighbors, partner, flags):
    nrhs, elements, width = adjoint_source.shape
    blk_count = lax.axis_size("blk")
    dom_here = lax.axis_index("dom")
    blk_here = lax.axis_index("blk")
    wall_mask = (flags == 1).astype(jnp.float32)
    center = diag_blocks + jnp.einsum("ef,efab->eab", wall_mask, face_blocks, precision=HIGH)
    inverse = invert_blocks(center)
    inside = neighbors >= 0
    source_elem = jnp.where(inside, neighbors, 0)
    source_face = jnp.where(inside, partner, 0)
    owner_dev = source_elem // elements
    owner_dom = owner_dev // blk_count
    owner_blk = owner_dev % blk_count
    direction = jnp.where(
        owner_dom == dom_here - 1,
        1,
        jnp.where(
            owner_dom == dom_here + 1,
            2,
            jnp.where(owner_blk == blk_here - 1, 3, jnp.where(owner_blk == blk_here + 1, 4, 0)),
        ),
    )
    direction = jnp.where(inside, direction, 0).astype(jnp.int32)
    local_slot = source_elem % elements
    flat_direction = direction.reshape(-1)
    flat_inside = inside.reshape(-1)
    flat_local = (local_slot * 6 + source_face).reshape(-1)
    face_keys = (source_elem * 6 + source_face).reshape(-1)
    same_way = (flat_direction[None, :] == flat_direction[:, None]) & flat_inside[None, :]
    placing = jnp.sum(
        (same_way & (face_keys[None, :] < face_keys[:, None])).astype(jnp.int32), axis=1
    )
    offsets = jnp.array(
        [0, 6 * elements, 6 * elements + EY, 6 * elements + 2 * EY, 6 * elements + 2 * EY + EX],
        jnp.int32,
    )
    candidate = jnp.where(flat_direction == 0, flat_local, offsets[flat_direction] + placing)
    slot_range = jnp.arange(elements * 6, dtype=jnp.int32)

    def pick_rows(target, count):
        marked = ((flat_direction == target) & flat_inside).astype(jnp.int32)
        ranking = jnp.cumsum(marked) - marked
        chooser = (ranking[None, :] == jnp.arange(count)[:, None]) & (marked[None, :] > 0)
        return jnp.sum(jnp.where(chooser, slot_range[None, :], 0), axis=1)

    toward_next_dom = pick_rows(2, EY)
    toward_prev_dom = pick_rows(1, EY)
    toward_next_blk = pick_rows(4, EX)
    toward_prev_blk = pick_rows(3, EX)
    flat_blocks = face_blocks.reshape(elements * 6, width, width)
    block_pool = jnp.concatenate(
        [
            flat_blocks,
            move_facing_dom(jnp.take(flat_blocks, toward_next_dom, axis=0), 1),
            move_facing_dom(jnp.take(flat_blocks, toward_prev_dom, axis=0), -1),
            move_facing_blk(jnp.take(flat_blocks, toward_next_blk, axis=0), 1),
            move_facing_blk(jnp.take(flat_blocks, toward_prev_blk, axis=0), -1),
        ],
        axis=0,
    )
    column_blocks = (
        jnp.take(block_pool, candidate, axis=0) * flat_inside.astype(jnp.float32)[:, None, None]
    )
    column_blocks = column_blocks.reshape(elements, 6, width, width)
    vector_index = (direction * elements + local_slot).reshape(-1)

    def precondition(vectors):
        return jnp.einsum("eab,rea->reb", inverse, vectors, precision=HIGH)

    start_norm = jnp.sqrt(
        lax.psum(jnp.sum(adjoint_source * adjoint_source, axis=(1, 2)), ("dom", "blk"))
    )
    krylov_basis = [adjoint_source / start_norm[:, None, None]]
    hessen = []
    for iteration in range(ITERS):
        operator_vectors = precondition(krylov_basis[-1])
        gathered = jnp.concatenate(
            [
                operator_vectors,
                move_vectors_dom(operator_vectors, 1),
                move_vectors_dom(operator_vectors, -1),
                move_vectors_blk(operator_vectors, 1),
                move_vectors_blk(operator_vectors, -1),
            ],
            axis=1,
        )
        nearby = jnp.take(gathered, vector_index, axis=1).reshape(nrhs, elements, 6, width)
        own_part = jnp.einsum("eab,rea->reb", center, operator_vectors, precision=HIGH)
        mapped = own_part + jnp.einsum("egab,rega->reb", column_blocks, nearby, precision=HIGH)
        local_dots = [jnp.sum(mapped * member, axis=(1, 2)) for member in krylov_basis]
        projections = lax.psum(jnp.stack(local_dots), ("dom", "blk"))
        for row_index in range(len(krylov_basis)):
            mapped = mapped - projections[row_index][:, None, None] * krylov_basis[row_index]
        new_norm = jnp.sqrt(lax.psum(jnp.sum(mapped * mapped, axis=(1, 2)), ("dom", "blk")))
        hessen.append(jnp.concatenate([projections, new_norm[None, :]], axis=0))
        krylov_basis.append(mapped / new_norm[:, None, None])
    coeffs, rel_residual = least_squares(hessen, start_norm)
    combined = coeffs[0][:, None, None] * krylov_basis[0]
    for col_index in range(1, ITERS):
        combined = combined + coeffs[col_index][:, None, None] * krylov_basis[col_index]
    return (precondition(combined), rel_residual)


CELLS = EX * EY
F32 = jnp.float32
BF16 = jnp.bfloat16
VMEM_LIMIT = 40 * 1024 * 1024
OUT_CELLS = ((0, 1), (2, 3), (0, 2), (1, 3))
PIVOT_FLOOR = 0.02
RESIDUAL_FLOOR = 0.02


def pair_lane(row, col):
    return row * (row + 1) // 2 + col


def split_halves(value):
    high = value.astype(BF16)
    low = (value - high.astype(F32)).astype(BF16)
    return high, low


def dot32(left, right):
    return jnp.dot(left, right, preferred_element_type=F32)


def dot_full(left, right):
    return jnp.dot(left, right, preferred_element_type=F32, precision=HIGH)


def stack_halves(vector):
    high, low = split_halves(vector)
    return jnp.concatenate([high, low], axis=0), high


def row_times(stacked, high, block_high, block_low):
    rows = high.shape[0]
    both = dot32(stacked, block_high)
    return both[:rows] + both[rows:] + dot32(high, block_low)


FROM_X = CELLS
FROM_Y = 2 * CELLS
OUTWARD = 3 * CELLS
BLOCKS = OUTWARD + 8
RING_TARGETS = (0, 1, 2, 3, 0, 2, 1, 3)


def local_products(halves, high_ref, low_ref):
    results = []
    for cell in range(CELLS):
        total = None
        for source, entry in (
            (cell, cell), (cell ^ 2, FROM_X + (cell ^ 2)), (cell ^ 1, FROM_Y + (cell ^ 1))
        ):
            part = row_times(*halves[source], high_ref[entry], low_ref[entry])
            total = part if total is None else total + part
        results.append(total)
    return results


def outward_products(halves, high_ref, low_ref):
    results = []
    for way in range(4):
        for place in range(2):
            entry = OUTWARD + 2 * way + place
            results.append(
                row_times(*halves[OUT_CELLS[way][place]], high_ref[entry], low_ref[entry])
            )
    return results


def padded(width):
    return (width + 7) // 8 * 8


def put_rows(ref, first, values):
    rows = values[0].shape[0]
    for place, value in enumerate(values):
        ref[first + rows * place : first + rows * (place + 1), :] = value


def get_rows(ref, first, rows, place):
    return ref[first + rows * place : first + rows * (place + 1), :]


def send_along_blk(local, outward, prev_ref, next_ref, first):
    for ref, way, cells in ((prev_ref, 2, (0, 2)), (next_ref, 3, (1, 3))):
        put_rows(
            ref, first,
            [
                outward[2 * way], outward[2 * way + 1], local[cells[0]], local[cells[1]],
                outward[cells[0] % 2], outward[2 + cells[0] % 2],
            ],
        )


def setup_kernel(
    nbr_ref, flag_ref, src_ref, diag_ref, face_ref,
    high_ref, low_ref, inv_high_ref, inv_low_ref, base_ref, local_ref, outward_ref,
    blk_prev_ref, blk_next_ref, dom_prev_ref, dom_next_ref, slot_ref,
    center_ref, x_ref, y_ref, product_ref, cell_ref, face_of_ref,
    *, dom_count, blk_count,
):
    width = diag_ref.shape[0]
    dom_here = lax.axis_index("dom")
    blk_here = lax.axis_index("blk")
    here = dom_here * blk_count + blk_here
    for slot in range(CELLS):
        up_x = jnp.int32(0)
        down_x = jnp.int32(0)
        up_y = jnp.int32(0)
        down_y = jnp.int32(0)
        for face in range(6):
            other = nbr_ref[slot, face]
            gap = jnp.where(other >= 0, other // CELLS - here, 0)
            up_x = jnp.where(gap == blk_count, 1, up_x)
            down_x = jnp.where(gap == -blk_count, 1, down_x)
            up_y = jnp.where(gap == 1, 1, up_y)
            down_y = jnp.where(gap == -1, 1, down_y)
        cell_x = jnp.where(dom_here < dom_count - 1, up_x, 1 - down_x)
        cell_y = jnp.where(blk_here < blk_count - 1, up_y, 1 - down_y)
        cell = 2 * cell_x + cell_y
        cell_ref[slot] = cell
        slot_ref[cell] = slot
    for entry in range(CELLS * 4):
        face_of_ref[entry] = -1
    for slot in range(CELLS):
        cell = cell_ref[slot]
        for face in range(6):
            other = nbr_ref[slot, face]
            inside = other >= 0
            safe = jnp.where(inside, other, 0)
            gap = safe // CELLS - here
            mate = cell_ref[safe % CELLS]
            change = jnp.bitwise_xor(mate, cell)
            way_x = jnp.where(cell >= 2, 0, 1)
            way_y = jnp.where(cell % 2 == 1, 2, 3)
            way_in = jnp.where(change == 2, way_x, way_y)
            way = jnp.where(
                gap == 0, way_in,
                jnp.where(
                    gap == -blk_count, 0,
                    jnp.where(gap == blk_count, 1, jnp.where(gap == -1, 2, 3)),
                ),
            )

            @pl.when(inside)
            def _():
                face_of_ref[slot * 4 + way] = face

    rows = lax.broadcasted_iota(jnp.int32, (width, width), 0)
    cols = lax.broadcasted_iota(jnp.int32, (width, width), 1)
    on_diag = rows == cols
    for slot in range(CELLS):
        base_ref[cell_ref[slot]] = src_ref[:, slot, :]
        center = diag_ref[:, slot, :]
        for face in range(6):
            wall = jnp.where(flag_ref[slot, face] == 1, 1.0, 0.0).astype(F32)
            center = center + wall * face_ref[face, :, slot, :]
        center_ref[slot] = center
        marked = jnp.where(on_diag, center, 0.0)
        inv_row = 1.0 / jnp.sum(marked, axis=0, keepdims=True)
        inv_col = 1.0 / jnp.sum(marked, axis=1, keepdims=True)
        first = jnp.where(on_diag, inv_col, 0.0)
        x_ref[slot] = 2.0 * first - inv_col * (center * inv_row)
    for sweep in range(SWEEPS - 1):
        for slot in range(CELLS):
            y_ref[slot] = dot_full(center_ref[slot], x_ref[slot])
        for slot in range(CELLS):
            x_ref[slot] = 2.0 * x_ref[slot] - dot_full(x_ref[slot], y_ref[slot])
    for slot in range(CELLS):
        cell = cell_ref[slot]
        x_high, x_low = split_halves(x_ref[slot])
        inv_high_ref[cell] = x_high
        inv_low_ref[cell] = x_low
        own = dot_full(x_ref[slot], center_ref[slot]) - jnp.where(on_diag, 1.0, 0.0)
        high_ref[cell], low_ref[cell] = split_halves(own)
        for way in range(4):
            face = face_of_ref[slot * 4 + way]
            keep = jnp.where(face >= 0, 1.0, 0.0).astype(F32)
            block = face_ref[jnp.maximum(face, 0), :, slot, :] * keep
            f_high, f_low = split_halves(block)
            product = dot32(x_high, f_high) + dot32(x_low, f_high) + dot32(x_high, f_low)
            if way < 2:
                leaves = cell // 2 == way
                inner = FROM_X + cell
                place = cell % 2
            else:
                leaves = cell % 2 == way - 2
                inner = FROM_Y + cell
                place = cell // 2
            entry = jnp.where(leaves, OUTWARD + 2 * way + place, inner)
            high_ref[entry], low_ref[entry] = split_halves(product)
            product_ref[entry] = product
    tall = padded(width)
    for way, ref in enumerate((dom_prev_ref, dom_next_ref, blk_prev_ref, blk_next_ref)):
        for place in range(2):
            ref[tall * place : tall * place + width, :] = product_ref[OUTWARD + 2 * way + place]
    halves = [stack_halves(base_ref[cell]) for cell in range(CELLS)]
    local = local_products(halves, high_ref, low_ref)
    outward = outward_products(halves, high_ref, low_ref)
    for cell in range(CELLS):
        local_ref[cell] = local[cell]
    for entry in range(8):
        outward_ref[entry] = outward[entry]
    send_along_blk(local, outward, blk_prev_ref, blk_next_ref, 2 * tall)


def middle_kernel(first_pair, *refs):
    local_ref, outward_ref, from_prev_ref, from_next_ref = refs[:4]
    sum_ref, dom_prev_ref, dom_next_ref = refs[-3:]
    rows = local_ref.shape[1]
    first = 0
    if first_pair:
        blocks_prev_ref, blocks_next_ref = refs[4:6]
        first = blocks_prev_ref.shape[0]
        dom_prev_ref[:first, :] = blocks_prev_ref[...]
        dom_next_ref[:first, :] = blocks_next_ref[...]
    sums = []
    for cell in range(CELLS):
        given = from_prev_ref if cell % 2 == 0 else from_next_ref
        sums.append(local_ref[cell] + get_rows(given, first, rows, cell // 2))
        sum_ref[cell] = sums[cell]
    for ref, way in ((dom_prev_ref, 0), (dom_next_ref, 1)):
        put_rows(
            ref, first,
            [
                outward_ref[2 * way], outward_ref[2 * way + 1],
                sums[2 * way], sums[2 * way + 1],
                get_rows(from_prev_ref, first, rows, 4 + way),
                get_rows(from_next_ref, first, rows, 4 + way),
            ],
        )


def pair_kernel(first_pair, last_pair, older_count, *refs):
    sum_ref, outward_ref, blk_prev_ref, blk_next_ref, dom_prev_ref, dom_next_ref = refs[:6]
    high_ref, low_ref = refs[6:8]
    refs = refs[8:]
    rows = sum_ref.shape[1]
    width = sum_ref.shape[2]
    first = 0
    if first_pair:
        tall = padded(width)
        first = 2 * tall
    else:
        in_high_ref, in_low_ref = refs[:2]
        refs = refs[2:]
    older = refs[:older_count]
    refs = refs[older_count:]
    if last_pair:
        gram_in_ref, gram_ref, odd_ref, even_ref = refs
    else:
        odd_ref, even_ref, local_out_ref, outward_out_ref, prev_ref, next_ref = refs[:6]
    if first_pair:
        in_high_ref, in_low_ref = refs[6:]
        for way, ref in enumerate((dom_prev_ref, dom_next_ref, blk_prev_ref, blk_next_ref)):
            for place in range(2):
                high, low = split_halves(ref[tall * place : tall * place + width, :])
                in_high_ref[2 * way + place] = high
                in_low_ref[2 * way + place] = low

    def got(ref, place):
        return get_rows(ref, first, rows, place)

    odd = [
        sum_ref[cell] + got(dom_prev_ref if cell < 2 else dom_next_ref, cell % 2)
        for cell in range(CELLS)
    ]
    ring = []
    for way, ref in enumerate((dom_prev_ref, dom_next_ref)):
        for place in range(2):
            ring.append(got(ref, 2 + place) + outward_ref[2 * way + place])
    for way, ref in enumerate((blk_prev_ref, blk_next_ref)):
        for place, corner_ref in enumerate((dom_prev_ref, dom_next_ref)):
            ring.append(
                got(ref, 2 + place) + outward_ref[4 + 2 * way + place] + got(corner_ref, 4 + way)
            )
    for cell in range(CELLS):
        odd_ref[cell] = odd[cell]
    even = local_products([stack_halves(value) for value in odd], high_ref, low_ref)
    for place, value in enumerate(ring):
        cell = RING_TARGETS[place]
        even[cell] = even[cell] + row_times(
            *stack_halves(value), in_high_ref[place], in_low_ref[place]
        )
    for cell in range(CELLS):
        even_ref[cell] = even[cell]
    if last_pair:
        bases = list(older) + [odd_ref, even_ref]
        gram = gram_rows(ITERS - 1, bases, gram_in_ref[...])
        gram = gram_rows(ITERS, bases, gram)
        half = gram.shape[0] // 2
        gram_ref[...] = gram[:half] + pltpu.roll(gram[half:], 64, 1)
    else:
        halves = [stack_halves(value) for value in even]
        local = local_products(halves, high_ref, low_ref)
        outward = outward_products(halves, high_ref, low_ref)
        for cell in range(CELLS):
            local_out_ref[cell] = local[cell]
        for entry in range(8):
            outward_out_ref[entry] = outward[entry]
        send_along_blk(local, outward, prev_ref, next_ref, 0)


def gram_kernel(newest, *refs):
    base_refs = refs[: newest + 1]
    gram = None
    if newest > 0:
        gram = gram_rows(newest - 1, base_refs, refs[newest + 1][...])
    refs[-1][...] = gram_rows(newest, base_refs, gram)


def gram_rows(step, base_refs, gram):
    newest = base_refs[step]
    nrhs = newest.shape[1]
    lanes = lax.broadcasted_iota(jnp.int32, (nrhs, 128), 1)
    if gram is None:
        gram = jnp.zeros((nrhs, 128), F32)
    for col in range(step + 1):
        total = newest[0] * base_refs[col][0]
        for cell in range(1, CELLS):
            total = total + newest[cell] * base_refs[col][cell]
        value = jnp.sum(total, axis=1, keepdims=True)
        gram = jnp.where(lanes == pair_lane(step, col), value, gram)
    return gram


def finish_kernel(*refs):
    gram_ref = refs[0]
    base_refs = refs[1 : 1 + ITERS]
    inv_high_ref, inv_low_ref, slot_ref, adjoint_ref, rel_ref, fine_ref = refs[1 + ITERS :]
    count = ITERS + 1
    packed = gram_ref[...]
    gram = jnp.concatenate([packed, pltpu.roll(packed, 64, 1)], axis=0)

    def lane(row, col):
        place = pair_lane(row, col)
        return jnp.broadcast_to(gram[:, place : place + 1], gram.shape)

    diag = [lane(j, j) for j in range(count)]
    scale = [1.0 / jnp.sqrt(value) for value in diag]
    start = jnp.sqrt(diag[0])
    lower = [[None] * count for j in range(count)]
    solved = []
    ratio = [scale[j] * start for j in range(count)]
    smallest = jnp.ones_like(gram)
    inv_pivot = []
    for col in range(count):
        pivot = jnp.ones_like(gram)
        for k in range(col):
            pivot = pivot - lower[col][k] * lower[col][k]
        smallest = jnp.minimum(smallest, pivot)
        inv_root = 1.0 / jnp.sqrt(pivot)
        inv_pivot.append(inv_root)
        for row in range(col + 1, count):
            value = lane(row, col) * scale[row] * scale[col]
            for k in range(col):
                value = value - lower[row][k] * lower[col][k]
            lower[row][col] = value * inv_root
        right = ratio[col] if col % 2 == 0 else -ratio[col]
        for k in range(col):
            right = right - lower[col][k] * solved[k]
        solved.append(right * inv_root)
    squares = solved[0] * solved[0]
    for j in range(1, count):
        squares = squares + solved[j] * solved[j]
    rel = 1.0 / jnp.sqrt(squares)
    back = [None] * count
    for j in reversed(range(count)):
        value = solved[j]
        for k in range(j + 1, count):
            value = value - lower[k][j] * back[k]
        back[j] = value * inv_pivot[j]
    inv_squares = 1.0 / squares
    residual = [ratio[j] * back[j] * inv_squares for j in range(count)]
    coeffs = [None] * ITERS
    coeffs[ITERS - 1] = -residual[ITERS]
    for j in reversed(range(1, ITERS)):
        coeffs[j - 1] = -residual[j] - coeffs[j]
    lanes = lax.broadcasted_iota(jnp.int32, gram.shape, 1)
    good = (smallest > PIVOT_FLOOR) & (rel > RESIDUAL_FLOOR) & (rel < 2.0)
    for j in range(count):
        good = good & (diag[j] > 1e-30) & (diag[j] < 1e36)
    worst = jnp.min(jnp.where(good, 1.0, 0.0))
    fine_ref[0] = jnp.where(worst > 0.5, 1, 0).astype(jnp.int32)
    rel_ref[...] = jnp.transpose(rel)[0:1, :]
    width = base_refs[0].shape[-1]
    wide = [
        jnp.concatenate([value, value], axis=1)[:, :width] for value in coeffs
    ]
    results = []
    for cell in range(CELLS):
        total = wide[0] * base_refs[0][cell]
        for j in range(1, ITERS):
            total = total + wide[j] * base_refs[j][cell]
        stacked, high = stack_halves(total)
        results.append(row_times(stacked, high, inv_high_ref[cell], inv_low_ref[cell]))
    for slot in range(CELLS):
        value = results[0]
        for cell in range(1, CELLS):
            value = jnp.where(slot_ref[cell] == slot, results[cell], value)
        adjoint_ref[:, slot, :] = value


def vmem(count):
    return [pl.BlockSpec(memory_space=pltpu.VMEM)] * count


def smem(count):
    return [pl.BlockSpec(memory_space=pltpu.SMEM)] * count


PARAMS = pltpu.CompilerParams(vmem_limit_bytes=VMEM_LIMIT)


def struct(*shape, kind=F32):
    return jax.ShapeDtypeStruct(shape, kind)


def sum_groups(value, axes, groups):
    size = len(groups[0])
    copies = jnp.broadcast_to(value[None], (size,) + value.shape)
    parts = lax.all_to_all(
        copies, axes, 0, 0, axis_index_groups=groups if len(groups) > 1 else None
    )
    return jnp.sum(parts, axis=0)


def sum_devices(value):
    dom_count, blk_count = (lax.axis_size("dom"), lax.axis_size("blk"))
    inner = 4 if dom_count % 4 == 0 else dom_count
    size = inner * blk_count
    near = [
        [first + k for k in range(size)] for first in range(0, dom_count * blk_count, size)
    ]
    value = sum_groups(value, ("dom", "blk"), near)
    if inner < dom_count:
        far = [[first + k for k in range(0, dom_count, inner)] for first in range(inner)]
        value = sum_groups(value, "dom", far)
    return value


def rotated(value, axis, steps):
    count = lax.axis_size(axis)
    return lax.ppermute(
        value, axis, [(source, (source + steps) % count) for source in range(count)]
    )


def both_ways(to_prev, to_next, axis):
    return rotated(to_next, axis, 1), rotated(to_prev, axis, -1)


def shards(adjoint_source, diag_blocks, face_blocks, neighbors, partner, flags):
    nrhs, elements, width = adjoint_source.shape
    block = (width, width)
    tall = padded(width)
    field = struct(CELLS, nrhs, width)
    ring = struct(8, nrhs, width)
    edge = struct(6 * nrhs, width)
    edge_blocks = struct(2 * tall + 6 * nrhs, width)
    cost = lambda flops, data: pl.CostEstimate(
        flops=flops, bytes_accessed=data, transcendentals=0
    )
    products = 2 * nrhs * width * width * 3
    outs = pl.pallas_call(
        functools.partial(
            setup_kernel, dom_count=lax.axis_size("dom"), blk_count=lax.axis_size("blk")
        ),
        out_shape=(
            struct(BLOCKS, *block, kind=BF16), struct(BLOCKS, *block, kind=BF16),
            struct(CELLS, *block, kind=BF16), struct(CELLS, *block, kind=BF16),
            field, field, ring, edge_blocks, edge_blocks,
            struct(2 * tall, width), struct(2 * tall, width),
            struct(CELLS, kind=jnp.int32),
        ),
        in_specs=smem(2) + vmem(3),
        out_specs=tuple(vmem(11) + smem(1)),
        scratch_shapes=[
            pltpu.VMEM((CELLS,) + block, F32),
            pltpu.VMEM((CELLS,) + block, F32),
            pltpu.VMEM((CELLS,) + block, F32),
            pltpu.VMEM((BLOCKS,) + block, F32),
            pltpu.SMEM((CELLS,), jnp.int32),
            pltpu.SMEM((CELLS * 4,), jnp.int32),
        ],
        compiler_params=PARAMS,
        name="setup_blocks",
    )(
        neighbors, flags, adjoint_source,
        jnp.transpose(diag_blocks, (1, 0, 2)), jnp.transpose(face_blocks, (1, 2, 0, 3)),
    )
    high, low, inv_high, inv_low, base, local, outward = outs[:7]
    blk_sends = outs[7:9]
    dom_blocks = outs[9:11]
    slots = outs[11]
    bases = [base]
    gram = None
    inward = ()
    for pair in range(ITERS // 2):
        first_pair = pair == 0
        last_pair = pair == ITERS // 2 - 1
        from_blk = both_ways(*blk_sends, "blk")
        given = [local, outward, *from_blk] + (list(dom_blocks) if first_pair else [])
        kind = edge_blocks if first_pair else edge
        sums, *dom_sends = pl.pallas_call(
            functools.partial(middle_kernel, first_pair),
            out_shape=(field, kind, kind),
            in_specs=vmem(len(given)),
            out_specs=tuple(vmem(3)),
            compiler_params=PARAMS,
            name=f"middle_part_{pair}",
        )(*given)
        from_dom = both_ways(*dom_sends, "dom")
        newest = len(bases) - 1
        given = bases + ([gram] if newest > 0 else [])
        gram = pl.pallas_call(
            functools.partial(gram_kernel, newest),
            out_shape=struct(nrhs, 128),
            in_specs=vmem(len(given)),
            out_specs=vmem(1)[0],
            compiler_params=PARAMS,
            cost_estimate=cost(100000 * (newest + 1), 2000000),
            name=f"gram_part_{pair}",
        )(*given)
        older = bases if last_pair else []
        given = [sums, outward, *from_blk, *from_dom, high, low, *inward, *older]
        if last_pair:
            given.append(gram)
            shapes = (struct(nrhs // 2, 128), field, field)
        else:
            shapes = (field, field, field, ring, edge, edge)
        if first_pair:
            shapes += (struct(8, *block, kind=BF16), struct(8, *block, kind=BF16))
        outs = pl.pallas_call(
            functools.partial(pair_kernel, first_pair, last_pair, len(older)),
            out_shape=shapes,
            in_specs=vmem(len(given)),
            out_specs=tuple(vmem(len(shapes))),
            compiler_params=PARAMS,
            cost_estimate=cost(40 * products, 6000000),
            name=f"pair_part_{pair}",
        )(*given)
        if last_pair:
            gram = outs[0]
            bases.append(outs[1])
        else:
            bases += outs[:2]
            local, outward = outs[2:4]
            blk_sends = outs[4:6]
        if first_pair:
            inward = outs[6:]
    gram = sum_devices(gram)
    given = [gram] + bases + [inv_high, inv_low, slots]
    adjoint, rel, fine = pl.pallas_call(
        finish_kernel,
        out_shape=(
            struct(nrhs, elements, width), struct(1, nrhs), struct(1, kind=jnp.int32)
        ),
        in_specs=vmem(len(given) - 1) + smem(1),
        out_specs=tuple(vmem(2) + smem(1)),
        compiler_params=PARAMS,
        name="finish_part",
    )(*given)
    return lax.cond(
        fine[0] == 1,
        lambda given: (adjoint, rel.reshape(nrhs)),
        lambda given: direct_path(*given),
        (adjoint_source, diag_blocks, face_blocks, neighbors, partner, flags),
    )


def solution(mesh):
    in_specs = (
        P(None, ("dom", "blk"), None),
        P(("dom", "blk"), None, None),
        P(("dom", "blk"), None, None, None),
        P(("dom", "blk"), None),
        P(("dom", "blk"), None),
        P(("dom", "blk"), None),
    )
    out_specs = (P(None, ("dom", "blk"), None), P())
    return jax.shard_map(shards, mesh=mesh, in_specs=in_specs, out_specs=out_specs, check_vma=False)
```

```python
import functools

import jax
import jax.numpy as jnp
from jax import lax
from jax.experimental import pallas as pl
from jax.experimental.pallas import tpu as pltpu
from jax.sharding import PartitionSpec as P

EX = 2
EY = 2
ITERS = 8
SWEEPS = 3


HIGH = lax.Precision.HIGHEST


def shifted(value, axis, steps):
    count = lax.axis_size(axis)
    leading, last = (max(0, -steps), min(count, count - steps))
    return lax.ppermute(value, axis, [(source, source + steps) for source in range(leading, last)])


def invert_blocks(center):
    width = center.shape[-1]
    identity = jnp.eye(width, dtype=center.dtype)
    pivots = jnp.diagonal(center, axis1=1, axis2=2)
    estimate = identity[None, :, :] / pivots[:, :, None]
    for sweep_index in range(SWEEPS):
        product = jnp.einsum("eab,ebc->eac", center, estimate, precision=HIGH)
        estimate = 2.0 * estimate - jnp.einsum("eab,ebc->eac", estimate, product, precision=HIGH)
    return estimate


def least_squares(hessen, start_norm):
    count = len(hessen)
    cosines = []
    sines = []
    rotated_rhs = [start_norm] + [jnp.zeros_like(start_norm) for row_index in range(count)]
    upper = []
    for col_index in range(count):
        column = [hessen[col_index][row_index] for row_index in range(col_index + 2)]
        for row_index in range(col_index):
            rotated = (
                cosines[row_index] * column[row_index] + sines[row_index] * column[row_index + 1]
            )
            column[row_index + 1] = (
                -sines[row_index] * column[row_index] + cosines[row_index] * column[row_index + 1]
            )
            column[row_index] = rotated
        radius = jnp.sqrt(
            column[col_index] * column[col_index] + column[col_index + 1] * column[col_index + 1]
        )
        cosine = column[col_index] / radius
        sine_value = column[col_index + 1] / radius
        column[col_index] = radius
        cosines.append(cosine)
        sines.append(sine_value)
        rotated_rhs[col_index + 1] = -sine_value * rotated_rhs[col_index]
        rotated_rhs[col_index] = cosine * rotated_rhs[col_index]
        upper.append(column[: col_index + 1])
    coeffs = [None] * count
    for row_index in reversed(range(count)):
        total = rotated_rhs[row_index]
        for col_index in range(row_index + 1, count):
            total = total - upper[col_index][row_index] * coeffs[col_index]
        coeffs[row_index] = total / upper[row_index][row_index]
    return (coeffs, jnp.abs(rotated_rhs[count]) / start_norm)


def move_vectors_dom(vectors, offset):
    return shifted(vectors, "dom", offset)


def move_vectors_blk(vectors, offset):
    return shifted(vectors, "blk", offset)


def move_facing_dom(blocks, offset):
    return shifted(blocks, "dom", offset)


def move_facing_blk(blocks, offset):
    return shifted(blocks, "blk", offset)


def direct_path(adjoint_source, diag_blocks, face_blocks, neighbors, partner, flags):
    nrhs, elements, width = adjoint_source.shape
    blk_count = lax.axis_size("blk")
    dom_here = lax.axis_index("dom")
    blk_here = lax.axis_index("blk")
    wall_mask = (flags == 1).astype(jnp.float32)
    center = diag_blocks + jnp.einsum("ef,efab->eab", wall_mask, face_blocks, precision=HIGH)
    inverse = invert_blocks(center)
    inside = neighbors >= 0
    source_elem = jnp.where(inside, neighbors, 0)
    source_face = jnp.where(inside, partner, 0)
    owner_dev = source_elem // elements
    owner_dom = owner_dev // blk_count
    owner_blk = owner_dev % blk_count
    direction = jnp.where(
        owner_dom == dom_here - 1,
        1,
        jnp.where(
            owner_dom == dom_here + 1,
            2,
            jnp.where(owner_blk == blk_here - 1, 3, jnp.where(owner_blk == blk_here + 1, 4, 0)),
        ),
    )
    direction = jnp.where(inside, direction, 0).astype(jnp.int32)
    local_slot = source_elem % elements
    flat_direction = direction.reshape(-1)
    flat_inside = inside.reshape(-1)
    flat_local = (local_slot * 6 + source_face).reshape(-1)
    face_keys = (source_elem * 6 + source_face).reshape(-1)
    same_way = (flat_direction[None, :] == flat_direction[:, None]) & flat_inside[None, :]
    placing = jnp.sum(
        (same_way & (face_keys[None, :] < face_keys[:, None])).astype(jnp.int32), axis=1
    )
    offsets = jnp.array(
        [0, 6 * elements, 6 * elements + EY, 6 * elements + 2 * EY, 6 * elements + 2 * EY + EX],
        jnp.int32,
    )
    candidate = jnp.where(flat_direction == 0, flat_local, offsets[flat_direction] + placing)
    slot_range = jnp.arange(elements * 6, dtype=jnp.int32)

    def pick_rows(target, count):
        marked = ((flat_direction == target) & flat_inside).astype(jnp.int32)
        ranking = jnp.cumsum(marked) - marked
        chooser = (ranking[None, :] == jnp.arange(count)[:, None]) & (marked[None, :] > 0)
        return jnp.sum(jnp.where(chooser, slot_range[None, :], 0), axis=1)

    toward_next_dom = pick_rows(2, EY)
    toward_prev_dom = pick_rows(1, EY)
    toward_next_blk = pick_rows(4, EX)
    toward_prev_blk = pick_rows(3, EX)
    flat_blocks = face_blocks.reshape(elements * 6, width, width)
    block_pool = jnp.concatenate(
        [
            flat_blocks,
            move_facing_dom(jnp.take(flat_blocks, toward_next_dom, axis=0), 1),
            move_facing_dom(jnp.take(flat_blocks, toward_prev_dom, axis=0), -1),
            move_facing_blk(jnp.take(flat_blocks, toward_next_blk, axis=0), 1),
            move_facing_blk(jnp.take(flat_blocks, toward_prev_blk, axis=0), -1),
        ],
        axis=0,
    )
    column_blocks = (
        jnp.take(block_pool, candidate, axis=0) * flat_inside.astype(jnp.float32)[:, None, None]
    )
    column_blocks = column_blocks.reshape(elements, 6, width, width)
    vector_index = (direction * elements + local_slot).reshape(-1)

    def precondition(vectors):
        return jnp.einsum("eab,rea->reb", inverse, vectors, precision=HIGH)

    start_norm = jnp.sqrt(
        lax.psum(jnp.sum(adjoint_source * adjoint_source, axis=(1, 2)), ("dom", "blk"))
    )
    krylov_basis = [adjoint_source / start_norm[:, None, None]]
    hessen = []
    for iteration in range(ITERS):
        operator_vectors = precondition(krylov_basis[-1])
        gathered = jnp.concatenate(
            [
                operator_vectors,
                move_vectors_dom(operator_vectors, 1),
                move_vectors_dom(operator_vectors, -1),
                move_vectors_blk(operator_vectors, 1),
                move_vectors_blk(operator_vectors, -1),
            ],
            axis=1,
        )
        nearby = jnp.take(gathered, vector_index, axis=1).reshape(nrhs, elements, 6, width)
        own_part = jnp.einsum("eab,rea->reb", center, operator_vectors, precision=HIGH)
        mapped = own_part + jnp.einsum("egab,rega->reb", column_blocks, nearby, precision=HIGH)
        local_dots = [jnp.sum(mapped * member, axis=(1, 2)) for member in krylov_basis]
        projections = lax.psum(jnp.stack(local_dots), ("dom", "blk"))
        for row_index in range(len(krylov_basis)):
            mapped = mapped - projections[row_index][:, None, None] * krylov_basis[row_index]
        new_norm = jnp.sqrt(lax.psum(jnp.sum(mapped * mapped, axis=(1, 2)), ("dom", "blk")))
        hessen.append(jnp.concatenate([projections, new_norm[None, :]], axis=0))
        krylov_basis.append(mapped / new_norm[:, None, None])
    coeffs, rel_residual = least_squares(hessen, start_norm)
    combined = coeffs[0][:, None, None] * krylov_basis[0]
    for col_index in range(1, ITERS):
        combined = combined + coeffs[col_index][:, None, None] * krylov_basis[col_index]
    return (precondition(combined), rel_residual)


CELLS = EX * EY
F32 = jnp.float32
BF16 = jnp.bfloat16
VMEM_LIMIT = 40 * 1024 * 1024
OUT_CELLS = ((0, 1), (2, 3), (0, 2), (1, 3))
PIVOT_FLOOR = 0.02
RESIDUAL_FLOOR = 0.02


def pair_lane(row, col):
    return row * (row + 1) // 2 + col


def split_halves(value):
    high = value.astype(BF16)
    low = (value - high.astype(F32)).astype(BF16)
    return high, low


def dot32(left, right):
    return jnp.dot(left, right, preferred_element_type=F32)


def dot_full(left, right):
    return jnp.dot(left, right, preferred_element_type=F32, precision=HIGH)


def stack_halves(vector):
    high, low = split_halves(vector)
    return jnp.concatenate([high, low], axis=0), high


def row_times(stacked, high, block_high, block_low):
    rows = high.shape[0]
    both = dot32(stacked, block_high)
    return both[:rows] + both[rows:] + dot32(high, block_low)


FROM_X = CELLS
FROM_Y = 2 * CELLS
OUTWARD = 3 * CELLS
BLOCKS = OUTWARD + 8
RING_TARGETS = (0, 1, 2, 3, 0, 2, 1, 3)


def local_products(halves, high_ref, low_ref):
    results = []
    for cell in range(CELLS):
        total = None
        for source, entry in (
            (cell, cell), (cell ^ 2, FROM_X + (cell ^ 2)), (cell ^ 1, FROM_Y + (cell ^ 1))
        ):
            part = row_times(*halves[source], high_ref[entry], low_ref[entry])
            total = part if total is None else total + part
        results.append(total)
    return results


def outward_products(halves, high_ref, low_ref):
    results = []
    for way in range(4):
        for place in range(2):
            entry = OUTWARD + 2 * way + place
            results.append(
                row_times(*halves[OUT_CELLS[way][place]], high_ref[entry], low_ref[entry])
            )
    return results


def padded(width):
    return (width + 7) // 8 * 8


def tails_of(values):
    rows, width = values[0].shape
    tail = width - 128
    total = None
    for place, value in enumerate(values):
        tile = jnp.concatenate([value[:, 128:], jnp.zeros((rows, 128 - tail), F32)], axis=1)
        tile = tile if place == 0 else pltpu.roll(tile, tail * place, 1)
        total = tile if total is None else total + tile
    return total


def tail_at(tile, tail, place):
    turned = tile if place == 0 else pltpu.roll(tile, 128 - tail * place, 1)
    return turned[:, :tail]


def put_rows(ref, first, values):
    rows = values[0].shape[0]
    for place, value in enumerate(values):
        ref[first + rows * place : first + rows * (place + 1), :] = value[:, :128]
    for part in range(2):
        start = first + rows * (6 + part)
        ref[start : start + rows, :] = tails_of(values[3 * part : 3 * part + 3])


def get_rows(ref, first, rows, tail, place):
    main = ref[first + rows * place : first + rows * (place + 1), :]
    start = first + rows * (6 + place // 3)
    return jnp.concatenate([main, tail_at(ref[start : start + rows, :], tail, place % 3)], axis=1)


def send_along_blk(local, outward, prev_ref, next_ref, first):
    for ref, way, cells in ((prev_ref, 2, (0, 2)), (next_ref, 3, (1, 3))):
        put_rows(
            ref, first,
            [
                outward[2 * way], outward[2 * way + 1], local[cells[0]], local[cells[1]],
                outward[cells[0] % 2], outward[2 + cells[0] % 2],
            ],
        )


def setup_kernel(
    nbr_ref, flag_ref, src_ref, diag_hbm_ref, face_hbm_ref,
    high_ref, low_ref, inv_high_ref, inv_low_ref, base_ref, local_ref, outward_ref,
    blk_prev_ref, blk_next_ref, dom_prev_ref, dom_next_ref, slot_ref,
    center_ref, x_ref, y_ref, product_ref, face_ref, cell_ref, face_of_ref, diag_sem, face_sem,
    *, dom_count, blk_count,
):
    width = diag_hbm_ref.shape[0]
    diag_copies = [
        pltpu.make_async_copy(
            diag_hbm_ref.at[:, slot, :], center_ref.at[slot], diag_sem.at[slot]
        )
        for slot in range(CELLS)
    ]
    face_copies = [
        [
            pltpu.make_async_copy(
                face_hbm_ref.at[face, :, slot, :], face_ref.at[slot, face], face_sem.at[slot, face]
            )
            for face in range(6)
        ]
        for slot in range(CELLS)
    ]
    for slot in range(CELLS):
        diag_copies[slot].start()
    for slot in range(CELLS):
        for face in range(6):
            pl.when(flag_ref[slot, face] == 1)(face_copies[slot][face].start)
    for slot in range(CELLS):
        for face in range(6):
            pl.when(nbr_ref[slot, face] >= 0)(face_copies[slot][face].start)
    dom_here = lax.axis_index("dom")
    blk_here = lax.axis_index("blk")
    here = dom_here * blk_count + blk_here
    for slot in range(CELLS):
        up_x = jnp.int32(0)
        down_x = jnp.int32(0)
        up_y = jnp.int32(0)
        down_y = jnp.int32(0)
        for face in range(6):
            other = nbr_ref[slot, face]
            gap = jnp.where(other >= 0, other // CELLS - here, 0)
            up_x = jnp.where(gap == blk_count, 1, up_x)
            down_x = jnp.where(gap == -blk_count, 1, down_x)
            up_y = jnp.where(gap == 1, 1, up_y)
            down_y = jnp.where(gap == -1, 1, down_y)
        cell_x = jnp.where(dom_here < dom_count - 1, up_x, 1 - down_x)
        cell_y = jnp.where(blk_here < blk_count - 1, up_y, 1 - down_y)
        cell = 2 * cell_x + cell_y
        cell_ref[slot] = cell
        slot_ref[cell] = slot
    for entry in range(CELLS * 4):
        face_of_ref[entry] = -1
    for slot in range(CELLS):
        cell = cell_ref[slot]
        for face in range(6):
            other = nbr_ref[slot, face]
            inside = other >= 0
            safe = jnp.where(inside, other, 0)
            gap = safe // CELLS - here
            mate = cell_ref[safe % CELLS]
            change = jnp.bitwise_xor(mate, cell)
            way_x = jnp.where(cell >= 2, 0, 1)
            way_y = jnp.where(cell % 2 == 1, 2, 3)
            way_in = jnp.where(change == 2, way_x, way_y)
            way = jnp.where(
                gap == 0, way_in,
                jnp.where(
                    gap == -blk_count, 0,
                    jnp.where(gap == blk_count, 1, jnp.where(gap == -1, 2, 3)),
                ),
            )

            @pl.when(inside)
            def _():
                face_of_ref[slot * 4 + way] = face

    rows = lax.broadcasted_iota(jnp.int32, (width, width), 0)
    cols = lax.broadcasted_iota(jnp.int32, (width, width), 1)
    on_diag = rows == cols
    for slot in range(CELLS):
        base_ref[cell_ref[slot]] = src_ref[:, slot, :]
        diag_copies[slot].wait()
    for slot in range(CELLS):
        for face in range(6):

            @pl.when(flag_ref[slot, face] == 1)
            def _():
                face_copies[slot][face].wait()
                center_ref[slot] = center_ref[slot] + face_ref[slot, face]

    for slot in range(CELLS):
        center = center_ref[slot]
        marked = jnp.where(on_diag, center, 0.0)
        inv_row = 1.0 / jnp.sum(marked, axis=0, keepdims=True)
        inv_col = 1.0 / jnp.sum(marked, axis=1, keepdims=True)
        first = jnp.where(on_diag, inv_col, 0.0)
        x_ref[slot] = 2.0 * first - inv_col * (center * inv_row)
    for sweep in range(SWEEPS - 1):
        for slot in range(CELLS):
            y_ref[slot] = dot_full(center_ref[slot], x_ref[slot])
        for slot in range(CELLS):
            x_ref[slot] = 2.0 * x_ref[slot] - dot_full(x_ref[slot], y_ref[slot])
    for slot in range(CELLS):
        for face in range(6):
            pl.when(nbr_ref[slot, face] >= 0)(face_copies[slot][face].wait)
    for slot in range(CELLS):
        cell = cell_ref[slot]
        x_high, x_low = split_halves(x_ref[slot])
        inv_high_ref[cell] = x_high
        inv_low_ref[cell] = x_low
        own = dot_full(x_ref[slot], center_ref[slot]) - jnp.where(on_diag, 1.0, 0.0)
        high_ref[cell], low_ref[cell] = split_halves(own)
        for way in range(4):
            face = face_of_ref[slot * 4 + way]
            block = jnp.where(face >= 0, face_ref[slot, jnp.maximum(face, 0)], 0.0)
            f_high, f_low = split_halves(block)
            product = dot32(x_high, f_high) + dot32(x_low, f_high) + dot32(x_high, f_low)
            if way < 2:
                leaves = cell // 2 == way
                inner = FROM_X + cell
                place = cell % 2
            else:
                leaves = cell % 2 == way - 2
                inner = FROM_Y + cell
                place = cell // 2
            entry = jnp.where(leaves, OUTWARD + 2 * way + place, inner)
            high_ref[entry], low_ref[entry] = split_halves(product)
            product_ref[entry] = product
    tall = padded(width)
    for way, ref in enumerate((dom_prev_ref, dom_next_ref, blk_prev_ref, blk_next_ref)):
        pair = [product_ref[OUTWARD + 2 * way + place] for place in range(2)]
        for place in range(2):
            ref[tall * place : tall * place + width, :] = pair[place][:, :128]
        ref[2 * tall : 2 * tall + width, :] = tails_of(pair)
    halves = [stack_halves(base_ref[cell]) for cell in range(CELLS)]
    local = local_products(halves, high_ref, low_ref)
    outward = outward_products(halves, high_ref, low_ref)
    for cell in range(CELLS):
        local_ref[cell] = local[cell]
    for entry in range(8):
        outward_ref[entry] = outward[entry]
    send_along_blk(local, outward, blk_prev_ref, blk_next_ref, 3 * tall)


def middle_kernel(first_pair, *refs):
    local_ref, outward_ref, from_prev_ref, from_next_ref = refs[:4]
    sum_ref, dom_prev_ref, dom_next_ref = refs[-3:]
    rows = local_ref.shape[1]
    tail = local_ref.shape[2] - 128
    first = 0
    if first_pair:
        blocks_prev_ref, blocks_next_ref = refs[4:6]
        first = blocks_prev_ref.shape[0]
        dom_prev_ref[:first, :] = blocks_prev_ref[...]
        dom_next_ref[:first, :] = blocks_next_ref[...]
    sums = []
    for cell in range(CELLS):
        given = from_prev_ref if cell % 2 == 0 else from_next_ref
        sums.append(local_ref[cell] + get_rows(given, first, rows, tail, cell // 2))
        sum_ref[cell] = sums[cell]
    for ref, way in ((dom_prev_ref, 0), (dom_next_ref, 1)):
        put_rows(
            ref, first,
            [
                outward_ref[2 * way], outward_ref[2 * way + 1],
                sums[2 * way], sums[2 * way + 1],
                get_rows(from_prev_ref, first, rows, tail, 4 + way),
                get_rows(from_next_ref, first, rows, tail, 4 + way),
            ],
        )


def pair_kernel(first_pair, last_pair, older_count, *refs):
    sum_ref, outward_ref, blk_prev_ref, blk_next_ref, dom_prev_ref, dom_next_ref = refs[:6]
    high_ref, low_ref = refs[6:8]
    refs = refs[8:]
    rows = sum_ref.shape[1]
    width = sum_ref.shape[2]
    first = 0
    if first_pair:
        tall = padded(width)
        first = 3 * tall
    else:
        in_high_ref, in_low_ref = refs[:2]
        refs = refs[2:]
    older = refs[:older_count]
    refs = refs[older_count:]
    if last_pair:
        gram_in_ref, gram_ref, odd_ref, even_ref = refs
    else:
        odd_ref, even_ref, local_out_ref, outward_out_ref, prev_ref, next_ref = refs[:6]
    if first_pair:
        in_high_ref, in_low_ref = refs[6:]
        for way, ref in enumerate((dom_prev_ref, dom_next_ref, blk_prev_ref, blk_next_ref)):
            for place in range(2):
                main = ref[tall * place : tall * place + width, :]
                tail = tail_at(ref[2 * tall : 2 * tall + width, :], width - 128, place)
                high, low = split_halves(jnp.concatenate([main, tail], axis=1))
                in_high_ref[2 * way + place] = high
                in_low_ref[2 * way + place] = low

    def got(ref, place):
        return get_rows(ref, first, rows, width - 128, place)

    odd = [
        sum_ref[cell] + got(dom_prev_ref if cell < 2 else dom_next_ref, cell % 2)
        for cell in range(CELLS)
    ]
    ring = []
    for way, ref in enumerate((dom_prev_ref, dom_next_ref)):
        for place in range(2):
            ring.append(got(ref, 2 + place) + outward_ref[2 * way + place])
    for way, ref in enumerate((blk_prev_ref, blk_next_ref)):
        for place, corner_ref in enumerate((dom_prev_ref, dom_next_ref)):
            ring.append(
                got(ref, 2 + place) + outward_ref[4 + 2 * way + place] + got(corner_ref, 4 + way)
            )
    for cell in range(CELLS):
        odd_ref[cell] = odd[cell]
    even = local_products([stack_halves(value) for value in odd], high_ref, low_ref)
    for place, value in enumerate(ring):
        cell = RING_TARGETS[place]
        even[cell] = even[cell] + row_times(
            *stack_halves(value), in_high_ref[place], in_low_ref[place]
        )
    for cell in range(CELLS):
        even_ref[cell] = even[cell]
    if last_pair:
        bases = list(older) + [odd_ref, even_ref]
        gram = gram_rows(ITERS - 1, bases, gram_in_ref[...])
        gram = gram_rows(ITERS, bases, gram)
        half = gram.shape[0] // 2
        gram = gram[:half] + pltpu.roll(gram[half:], 64, 1)
        for place in range(gram_ref.shape[0]):
            gram_ref[place] = gram
    else:
        halves = [stack_halves(value) for value in even]
        local = local_products(halves, high_ref, low_ref)
        outward = outward_products(halves, high_ref, low_ref)
        for cell in range(CELLS):
            local_out_ref[cell] = local[cell]
        for entry in range(8):
            outward_out_ref[entry] = outward[entry]
        send_along_blk(local, outward, prev_ref, next_ref, 0)


def gram_kernel(newest, *refs):
    base_refs = refs[: newest + 1]
    gram = None
    if newest > 0:
        gram = gram_rows(newest - 1, base_refs, refs[newest + 1][...])
    refs[-1][...] = gram_rows(newest, base_refs, gram)


def gram_rows(step, base_refs, gram):
    newest = base_refs[step]
    nrhs = newest.shape[1]
    lanes = lax.broadcasted_iota(jnp.int32, (nrhs, 128), 1)
    if gram is None:
        gram = jnp.zeros((nrhs, 128), F32)
    for col in range(step + 1):
        total = newest[0] * base_refs[col][0]
        for cell in range(1, CELLS):
            total = total + newest[cell] * base_refs[col][cell]
        value = jnp.sum(total, axis=1, keepdims=True)
        gram = jnp.where(lanes == pair_lane(step, col), value, gram)
    return gram


def finish_kernel(*refs):
    gram_ref = refs[0]
    base_refs = refs[1 : 1 + ITERS]
    inv_high_ref, inv_low_ref, slot_ref, adjoint_ref, rel_ref, fine_ref = refs[1 + ITERS :]
    count = ITERS + 1
    packed = sum_parts(gram_ref)
    gram = jnp.concatenate([packed, pltpu.roll(packed, 64, 1)], axis=0)

    def lane(row, col):
        place = pair_lane(row, col)
        return jnp.broadcast_to(gram[:, place : place + 1], gram.shape)

    diag = [lane(j, j) for j in range(count)]
    scale = [1.0 / jnp.sqrt(value) for value in diag]
    start = jnp.sqrt(diag[0])
    lower = [[None] * count for j in range(count)]
    solved = []
    ratio = [scale[j] * start for j in range(count)]
    smallest = jnp.ones_like(gram)
    inv_pivot = []
    for col in range(count):
        pivot = jnp.ones_like(gram)
        for k in range(col):
            pivot = pivot - lower[col][k] * lower[col][k]
        smallest = jnp.minimum(smallest, pivot)
        inv_root = 1.0 / jnp.sqrt(pivot)
        inv_pivot.append(inv_root)
        for row in range(col + 1, count):
            value = lane(row, col) * scale[row] * scale[col]
            for k in range(col):
                value = value - lower[row][k] * lower[col][k]
            lower[row][col] = value * inv_root
        right = ratio[col] if col % 2 == 0 else -ratio[col]
        for k in range(col):
            right = right - lower[col][k] * solved[k]
        solved.append(right * inv_root)
    squares = solved[0] * solved[0]
    for j in range(1, count):
        squares = squares + solved[j] * solved[j]
    rel = 1.0 / jnp.sqrt(squares)
    back = [None] * count
    for j in reversed(range(count)):
        value = solved[j]
        for k in range(j + 1, count):
            value = value - lower[k][j] * back[k]
        back[j] = value * inv_pivot[j]
    inv_squares = 1.0 / squares
    residual = [ratio[j] * back[j] * inv_squares for j in range(count)]
    coeffs = [None] * ITERS
    coeffs[ITERS - 1] = -residual[ITERS]
    for j in reversed(range(1, ITERS)):
        coeffs[j - 1] = -residual[j] - coeffs[j]
    lanes = lax.broadcasted_iota(jnp.int32, gram.shape, 1)
    good = (smallest > PIVOT_FLOOR) & (rel > RESIDUAL_FLOOR) & (rel < 2.0)
    for j in range(count):
        good = good & (diag[j] > 1e-30) & (diag[j] < 1e36)
    worst = jnp.min(jnp.where(good, 1.0, 0.0))
    fine_ref[0] = jnp.where(worst > 0.5, 1, 0).astype(jnp.int32)
    rel_ref[...] = jnp.transpose(rel)[0:1, :]
    width = base_refs[0].shape[-1]
    wide = [
        jnp.concatenate([value, value], axis=1)[:, :width] for value in coeffs
    ]
    results = []
    for cell in range(CELLS):
        total = wide[0] * base_refs[0][cell]
        for j in range(1, ITERS):
            total = total + wide[j] * base_refs[j][cell]
        stacked, high = stack_halves(total)
        results.append(row_times(stacked, high, inv_high_ref[cell], inv_low_ref[cell]))
    for slot in range(CELLS):
        value = results[0]
        for cell in range(1, CELLS):
            value = jnp.where(slot_ref[cell] == slot, results[cell], value)
        adjoint_ref[:, slot, :] = value


def vmem(count):
    return [pl.BlockSpec(memory_space=pltpu.VMEM)] * count


def smem(count):
    return [pl.BlockSpec(memory_space=pltpu.SMEM)] * count


PARAMS = pltpu.CompilerParams(vmem_limit_bytes=VMEM_LIMIT)


def struct(*shape, kind=F32):
    return jax.ShapeDtypeStruct(shape, kind)


def spread_kernel(parts_ref, copies_ref):
    total = sum_parts(parts_ref)
    for place in range(copies_ref.shape[0]):
        copies_ref[place] = total


def sum_parts(parts_ref):
    total = parts_ref[0]
    for place in range(1, parts_ref.shape[0]):
        total = total + parts_ref[place]
    return total


def near_size():
    dom_count = lax.axis_size("dom")
    return 4 if dom_count % 4 == 0 else dom_count


def sum_devices(copies):
    dom_count, blk_count = (lax.axis_size("dom"), lax.axis_size("blk"))
    inner = near_size()
    size = inner * blk_count
    near = [
        [first + k for k in range(size)] for first in range(0, dom_count * blk_count, size)
    ]
    far = [[first + k for k in range(0, dom_count, inner)] for first in range(inner)]
    parts = lax.all_to_all(copies, ("dom", "blk"), 0, 0, axis_index_groups=near)
    copies = pl.pallas_call(
        spread_kernel,
        out_shape=struct(dom_count // inner, *copies.shape[1:]),
        in_specs=vmem(1),
        out_specs=vmem(1)[0],
        compiler_params=PARAMS,
        name="sum_near",
    )(parts)
    return lax.all_to_all(copies, "dom", 0, 0, axis_index_groups=far)


def rotated(value, axis, steps):
    count = lax.axis_size(axis)
    return lax.ppermute(
        value, axis, [(source, (source + steps) % count) for source in range(count)]
    )


def both_ways(to_prev, to_next, axis):
    return rotated(to_next, axis, 1), rotated(to_prev, axis, -1)


def shards(adjoint_source, diag_blocks, face_blocks, neighbors, partner, flags):
    nrhs, elements, width = adjoint_source.shape
    block = (width, width)
    tall = padded(width)
    field = struct(CELLS, nrhs, width)
    ring = struct(8, nrhs, width)
    edge = struct(8 * nrhs, 128)
    edge_blocks = struct(3 * tall + 8 * nrhs, 128)
    cost = lambda flops, data: pl.CostEstimate(
        flops=flops, bytes_accessed=data, transcendentals=0
    )
    products = 2 * nrhs * width * width * 3
    outs = pl.pallas_call(
        functools.partial(
            setup_kernel, dom_count=lax.axis_size("dom"), blk_count=lax.axis_size("blk")
        ),
        out_shape=(
            struct(BLOCKS, *block, kind=BF16), struct(BLOCKS, *block, kind=BF16),
            struct(CELLS, *block, kind=BF16), struct(CELLS, *block, kind=BF16),
            field, field, ring, edge_blocks, edge_blocks,
            struct(3 * tall, 128), struct(3 * tall, 128),
            struct(CELLS, kind=jnp.int32),
        ),
        in_specs=smem(2) + vmem(1) + [pl.BlockSpec(memory_space=pl.ANY)] * 2,
        out_specs=tuple(vmem(11) + smem(1)),
        scratch_shapes=[
            pltpu.VMEM((CELLS,) + block, F32),
            pltpu.VMEM((CELLS,) + block, F32),
            pltpu.VMEM((CELLS,) + block, F32),
            pltpu.VMEM((BLOCKS,) + block, F32),
            pltpu.VMEM((CELLS, 6) + block, F32),
            pltpu.SMEM((CELLS,), jnp.int32),
            pltpu.SMEM((CELLS * 4,), jnp.int32),
            pltpu.SemaphoreType.DMA((CELLS,)),
            pltpu.SemaphoreType.DMA((CELLS, 6)),
        ],
        compiler_params=PARAMS,
        name="setup_blocks",
    )(
        neighbors, flags, adjoint_source,
        jnp.transpose(diag_blocks, (1, 0, 2)), jnp.transpose(face_blocks, (1, 2, 0, 3)),
    )
    high, low, inv_high, inv_low, base, local, outward = outs[:7]
    blk_sends = outs[7:9]
    dom_blocks = outs[9:11]
    slots = outs[11]
    bases = [base]
    gram = None
    inward = ()
    for pair in range(ITERS // 2):
        first_pair = pair == 0
        last_pair = pair == ITERS // 2 - 1
        from_blk = both_ways(*blk_sends, "blk")
        given = [local, outward, *from_blk] + (list(dom_blocks) if first_pair else [])
        kind = edge_blocks if first_pair else edge
        sums, *dom_sends = pl.pallas_call(
            functools.partial(middle_kernel, first_pair),
            out_shape=(field, kind, kind),
            in_specs=vmem(len(given)),
            out_specs=tuple(vmem(3)),
            compiler_params=PARAMS,
            name=f"middle_part_{pair}",
        )(*given)
        from_dom = both_ways(*dom_sends, "dom")
        newest = len(bases) - 1
        given = bases + ([gram] if newest > 0 else [])
        gram = pl.pallas_call(
            functools.partial(gram_kernel, newest),
            out_shape=struct(nrhs, 128),
            in_specs=vmem(len(given)),
            out_specs=vmem(1)[0],
            compiler_params=PARAMS,
            cost_estimate=cost(100000 * (newest + 1), 2000000),
            name=f"gram_part_{pair}",
        )(*given)
        older = bases if last_pair else []
        given = [sums, outward, *from_blk, *from_dom, high, low, *inward, *older]
        if last_pair:
            given.append(gram)
            shapes = (struct(near_size() * lax.axis_size("blk"), nrhs // 2, 128), field, field)
        else:
            shapes = (field, field, field, ring, edge, edge)
        if first_pair:
            shapes += (struct(8, *block, kind=BF16), struct(8, *block, kind=BF16))
        outs = pl.pallas_call(
            functools.partial(pair_kernel, first_pair, last_pair, len(older)),
            out_shape=shapes,
            in_specs=vmem(len(given)),
            out_specs=tuple(vmem(len(shapes))),
            compiler_params=PARAMS,
            cost_estimate=cost(40 * products, 6000000),
            name=f"pair_part_{pair}",
        )(*given)
        if last_pair:
            gram = outs[0]
            bases.append(outs[1])
        else:
            bases += outs[:2]
            local, outward = outs[2:4]
            blk_sends = outs[4:6]
        if first_pair:
            inward = outs[6:]
    gram = sum_devices(gram)
    given = [gram] + bases + [inv_high, inv_low, slots]
    adjoint, rel, fine = pl.pallas_call(
        finish_kernel,
        out_shape=(
            struct(nrhs, elements, width), struct(1, nrhs), struct(1, kind=jnp.int32)
        ),
        in_specs=vmem(len(given) - 1) + smem(1),
        out_specs=tuple(vmem(2) + smem(1)),
        compiler_params=PARAMS,
        name="finish_part",
    )(*given)
    return lax.cond(
        fine[0] == 1,
        lambda given: (adjoint, rel.reshape(nrhs)),
        lambda given: direct_path(*given),
        (adjoint_source, diag_blocks, face_blocks, neighbors, partner, flags),
    )


def solution(mesh):
    in_specs = (
        P(None, ("dom", "blk"), None),
        P(("dom", "blk"), None, None),
        P(("dom", "blk"), None, None, None),
        P(("dom", "blk"), None),
        P(("dom", "blk"), None),
        P(("dom", "blk"), None),
    )
    out_specs = (P(None, ("dom", "blk"), None), P())
    return jax.shard_map(shards, mesh=mesh, in_specs=in_specs, out_specs=out_specs, check_vma=False)
```

```python
import functools

import jax
import jax.numpy as jnp
from jax import lax
from jax.experimental import pallas as pl
from jax.experimental.pallas import tpu as pltpu
from jax.sharding import PartitionSpec as P

EX = 2
EY = 2
ITERS = 8
SWEEPS = 3


HIGH = lax.Precision.HIGHEST


def shifted(value, axis, steps):
    count = lax.axis_size(axis)
    leading, last = (max(0, -steps), min(count, count - steps))
    return lax.ppermute(value, axis, [(source, source + steps) for source in range(leading, last)])


def invert_blocks(center):
    width = center.shape[-1]
    identity = jnp.eye(width, dtype=center.dtype)
    pivots = jnp.diagonal(center, axis1=1, axis2=2)
    estimate = identity[None, :, :] / pivots[:, :, None]
    for sweep_index in range(SWEEPS):
        product = jnp.einsum("eab,ebc->eac", center, estimate, precision=HIGH)
        estimate = 2.0 * estimate - jnp.einsum("eab,ebc->eac", estimate, product, precision=HIGH)
    return estimate


def least_squares(hessen, start_norm):
    count = len(hessen)
    cosines = []
    sines = []
    rotated_rhs = [start_norm] + [jnp.zeros_like(start_norm) for row_index in range(count)]
    upper = []
    for col_index in range(count):
        column = [hessen[col_index][row_index] for row_index in range(col_index + 2)]
        for row_index in range(col_index):
            rotated = (
                cosines[row_index] * column[row_index] + sines[row_index] * column[row_index + 1]
            )
            column[row_index + 1] = (
                -sines[row_index] * column[row_index] + cosines[row_index] * column[row_index + 1]
            )
            column[row_index] = rotated
        radius = jnp.sqrt(
            column[col_index] * column[col_index] + column[col_index + 1] * column[col_index + 1]
        )
        cosine = column[col_index] / radius
        sine_value = column[col_index + 1] / radius
        column[col_index] = radius
        cosines.append(cosine)
        sines.append(sine_value)
        rotated_rhs[col_index + 1] = -sine_value * rotated_rhs[col_index]
        rotated_rhs[col_index] = cosine * rotated_rhs[col_index]
        upper.append(column[: col_index + 1])
    coeffs = [None] * count
    for row_index in reversed(range(count)):
        total = rotated_rhs[row_index]
        for col_index in range(row_index + 1, count):
            total = total - upper[col_index][row_index] * coeffs[col_index]
        coeffs[row_index] = total / upper[row_index][row_index]
    return (coeffs, jnp.abs(rotated_rhs[count]) / start_norm)


def move_vectors_dom(vectors, offset):
    return shifted(vectors, "dom", offset)


def move_vectors_blk(vectors, offset):
    return shifted(vectors, "blk", offset)


def move_facing_dom(blocks, offset):
    return shifted(blocks, "dom", offset)


def move_facing_blk(blocks, offset):
    return shifted(blocks, "blk", offset)


def direct_path(adjoint_source, diag_blocks, face_blocks, neighbors, partner, flags):
    nrhs, elements, width = adjoint_source.shape
    blk_count = lax.axis_size("blk")
    dom_here = lax.axis_index("dom")
    blk_here = lax.axis_index("blk")
    wall_mask = (flags == 1).astype(jnp.float32)
    center = diag_blocks + jnp.einsum("ef,efab->eab", wall_mask, face_blocks, precision=HIGH)
    inverse = invert_blocks(center)
    inside = neighbors >= 0
    source_elem = jnp.where(inside, neighbors, 0)
    source_face = jnp.where(inside, partner, 0)
    owner_dev = source_elem // elements
    owner_dom = owner_dev // blk_count
    owner_blk = owner_dev % blk_count
    direction = jnp.where(
        owner_dom == dom_here - 1,
        1,
        jnp.where(
            owner_dom == dom_here + 1,
            2,
            jnp.where(owner_blk == blk_here - 1, 3, jnp.where(owner_blk == blk_here + 1, 4, 0)),
        ),
    )
    direction = jnp.where(inside, direction, 0).astype(jnp.int32)
    local_slot = source_elem % elements
    flat_direction = direction.reshape(-1)
    flat_inside = inside.reshape(-1)
    flat_local = (local_slot * 6 + source_face).reshape(-1)
    face_keys = (source_elem * 6 + source_face).reshape(-1)
    same_way = (flat_direction[None, :] == flat_direction[:, None]) & flat_inside[None, :]
    placing = jnp.sum(
        (same_way & (face_keys[None, :] < face_keys[:, None])).astype(jnp.int32), axis=1
    )
    offsets = jnp.array(
        [0, 6 * elements, 6 * elements + EY, 6 * elements + 2 * EY, 6 * elements + 2 * EY + EX],
        jnp.int32,
    )
    candidate = jnp.where(flat_direction == 0, flat_local, offsets[flat_direction] + placing)
    slot_range = jnp.arange(elements * 6, dtype=jnp.int32)

    def pick_rows(target, count):
        marked = ((flat_direction == target) & flat_inside).astype(jnp.int32)
        ranking = jnp.cumsum(marked) - marked
        chooser = (ranking[None, :] == jnp.arange(count)[:, None]) & (marked[None, :] > 0)
        return jnp.sum(jnp.where(chooser, slot_range[None, :], 0), axis=1)

    toward_next_dom = pick_rows(2, EY)
    toward_prev_dom = pick_rows(1, EY)
    toward_next_blk = pick_rows(4, EX)
    toward_prev_blk = pick_rows(3, EX)
    flat_blocks = face_blocks.reshape(elements * 6, width, width)
    block_pool = jnp.concatenate(
        [
            flat_blocks,
            move_facing_dom(jnp.take(flat_blocks, toward_next_dom, axis=0), 1),
            move_facing_dom(jnp.take(flat_blocks, toward_prev_dom, axis=0), -1),
            move_facing_blk(jnp.take(flat_blocks, toward_next_blk, axis=0), 1),
            move_facing_blk(jnp.take(flat_blocks, toward_prev_blk, axis=0), -1),
        ],
        axis=0,
    )
    column_blocks = (
        jnp.take(block_pool, candidate, axis=0) * flat_inside.astype(jnp.float32)[:, None, None]
    )
    column_blocks = column_blocks.reshape(elements, 6, width, width)
    vector_index = (direction * elements + local_slot).reshape(-1)

    def precondition(vectors):
        return jnp.einsum("eab,rea->reb", inverse, vectors, precision=HIGH)

    start_norm = jnp.sqrt(
        lax.psum(jnp.sum(adjoint_source * adjoint_source, axis=(1, 2)), ("dom", "blk"))
    )
    krylov_basis = [adjoint_source / start_norm[:, None, None]]
    hessen = []
    for iteration in range(ITERS):
        operator_vectors = precondition(krylov_basis[-1])
        gathered = jnp.concatenate(
            [
                operator_vectors,
                move_vectors_dom(operator_vectors, 1),
                move_vectors_dom(operator_vectors, -1),
                move_vectors_blk(operator_vectors, 1),
                move_vectors_blk(operator_vectors, -1),
            ],
            axis=1,
        )
        nearby = jnp.take(gathered, vector_index, axis=1).reshape(nrhs, elements, 6, width)
        own_part = jnp.einsum("eab,rea->reb", center, operator_vectors, precision=HIGH)
        mapped = own_part + jnp.einsum("egab,rega->reb", column_blocks, nearby, precision=HIGH)
        local_dots = [jnp.sum(mapped * member, axis=(1, 2)) for member in krylov_basis]
        projections = lax.psum(jnp.stack(local_dots), ("dom", "blk"))
        for row_index in range(len(krylov_basis)):
            mapped = mapped - projections[row_index][:, None, None] * krylov_basis[row_index]
        new_norm = jnp.sqrt(lax.psum(jnp.sum(mapped * mapped, axis=(1, 2)), ("dom", "blk")))
        hessen.append(jnp.concatenate([projections, new_norm[None, :]], axis=0))
        krylov_basis.append(mapped / new_norm[:, None, None])
    coeffs, rel_residual = least_squares(hessen, start_norm)
    combined = coeffs[0][:, None, None] * krylov_basis[0]
    for col_index in range(1, ITERS):
        combined = combined + coeffs[col_index][:, None, None] * krylov_basis[col_index]
    return (precondition(combined), rel_residual)


CELLS = EX * EY
F32 = jnp.float32
BF16 = jnp.bfloat16
VMEM_LIMIT = 40 * 1024 * 1024
OUT_CELLS = ((0, 1), (2, 3), (0, 2), (1, 3))
PIVOT_FLOOR = 0.02
RESIDUAL_FLOOR = 0.02


def pair_lane(row, col):
    return row * (row + 1) // 2 + col


def split_halves(value):
    high = value.astype(BF16)
    low = (value - high.astype(F32)).astype(BF16)
    return high, low


def dot32(left, right):
    return jnp.dot(left, right, preferred_element_type=F32)


def dot_full(left, right):
    return jnp.dot(left, right, preferred_element_type=F32, precision=HIGH)


def stack_halves(vector):
    high, low = split_halves(vector)
    return jnp.concatenate([high, low], axis=0), high


def row_times(stacked, high, block_high, block_low):
    rows = high.shape[0]
    both = dot32(stacked, block_high)
    return both[:rows] + both[rows:] + dot32(high, block_low)


FROM_X = CELLS
FROM_Y = 2 * CELLS
OUTWARD = 3 * CELLS
BLOCKS = OUTWARD + 8
RING_TARGETS = (0, 1, 2, 3, 0, 2, 1, 3)


def local_products(halves, high_ref, low_ref):
    results = []
    for cell in range(CELLS):
        total = None
        for source, entry in (
            (cell, cell), (cell ^ 2, FROM_X + (cell ^ 2)), (cell ^ 1, FROM_Y + (cell ^ 1))
        ):
            part = row_times(*halves[source], high_ref[entry], low_ref[entry])
            total = part if total is None else total + part
        results.append(total)
    return results


def outward_products(halves, high_ref, low_ref):
    results = []
    for way in range(4):
        for place in range(2):
            entry = OUTWARD + 2 * way + place
            results.append(
                row_times(*halves[OUT_CELLS[way][place]], high_ref[entry], low_ref[entry])
            )
    return results


def padded(width):
    return (width + 7) // 8 * 8


def tails_of(values):
    rows, width = values[0].shape
    tail = width - 128
    total = None
    for place, value in enumerate(values):
        tile = jnp.concatenate([value[:, 128:], jnp.zeros((rows, 128 - tail), F32)], axis=1)
        tile = tile if place == 0 else pltpu.roll(tile, tail * place, 1)
        total = tile if total is None else total + tile
    return total


def tail_at(tile, tail, place):
    turned = tile if place == 0 else pltpu.roll(tile, 128 - tail * place, 1)
    return turned[:, :tail]


def put_rows(ref, first, values):
    rows = values[0].shape[0]
    for place, value in enumerate(values):
        ref[first + rows * place : first + rows * (place + 1), :] = value[:, :128]
    for part in range(0, len(values), 3):
        start = first + rows * (len(values) + part // 3)
        ref[start : start + rows, :] = tails_of(values[part : part + 3])


def get_rows(ref, first, rows, tail, count, place):
    main = ref[first + rows * place : first + rows * (place + 1), :]
    start = first + rows * (count + place // 3)
    return jnp.concatenate([main, tail_at(ref[start : start + rows, :], tail, place % 3)], axis=1)


def send_along_blk(local, outward, prev_ref, next_ref, first):
    for ref, way, cells in ((prev_ref, 2, (0, 2)), (next_ref, 3, (1, 3))):
        put_rows(
            ref, first,
            [
                outward[2 * way], outward[2 * way + 1], local[cells[0]], local[cells[1]],
                outward[2 + cells[0] % 2],
            ],
        )


def send_to_dom_prev(local, outward, prev_ref, first):
    put_rows(
        prev_ref, first,
        [outward[0], outward[1], local[0], local[1], outward[4], outward[6]],
    )


def setup_kernel(
    nbr_ref, flag_ref, src_ref, diag_hbm_ref, face_hbm_ref,
    high_ref, low_ref, inv_high_ref, inv_low_ref, base_ref, local_ref, outward_ref,
    blk_prev_ref, blk_next_ref, dom_prev_ref, dom_next_ref, slot_ref,
    center_ref, x_ref, y_ref, product_ref, face_ref, cell_ref, face_of_ref, diag_sem, face_sem,
    *, dom_count, blk_count,
):
    width = diag_hbm_ref.shape[0]
    diag_copies = [
        pltpu.make_async_copy(
            diag_hbm_ref.at[:, slot, :], center_ref.at[slot], diag_sem.at[slot]
        )
        for slot in range(CELLS)
    ]
    face_copies = [
        [
            pltpu.make_async_copy(
                face_hbm_ref.at[face, :, slot, :], face_ref.at[slot, face], face_sem.at[slot, face]
            )
            for face in range(6)
        ]
        for slot in range(CELLS)
    ]
    for slot in range(CELLS):
        diag_copies[slot].start()
    for slot in range(CELLS):
        for face in range(6):
            pl.when(flag_ref[slot, face] == 1)(face_copies[slot][face].start)
    for slot in range(CELLS):
        for face in range(6):
            pl.when(nbr_ref[slot, face] >= 0)(face_copies[slot][face].start)
    dom_here = lax.axis_index("dom")
    blk_here = lax.axis_index("blk")
    here = dom_here * blk_count + blk_here
    for slot in range(CELLS):
        up_x = jnp.int32(0)
        down_x = jnp.int32(0)
        up_y = jnp.int32(0)
        down_y = jnp.int32(0)
        for face in range(6):
            other = nbr_ref[slot, face]
            gap = jnp.where(other >= 0, other // CELLS - here, 0)
            up_x = jnp.where(gap == blk_count, 1, up_x)
            down_x = jnp.where(gap == -blk_count, 1, down_x)
            up_y = jnp.where(gap == 1, 1, up_y)
            down_y = jnp.where(gap == -1, 1, down_y)
        cell_x = jnp.where(dom_here < dom_count - 1, up_x, 1 - down_x)
        cell_y = jnp.where(blk_here < blk_count - 1, up_y, 1 - down_y)
        cell = 2 * cell_x + cell_y
        cell_ref[slot] = cell
        slot_ref[cell] = slot
    for entry in range(CELLS * 4):
        face_of_ref[entry] = -1
    for slot in range(CELLS):
        cell = cell_ref[slot]
        for face in range(6):
            other = nbr_ref[slot, face]
            inside = other >= 0
            safe = jnp.where(inside, other, 0)
            gap = safe // CELLS - here
            mate = cell_ref[safe % CELLS]
            change = jnp.bitwise_xor(mate, cell)
            way_x = jnp.where(cell >= 2, 0, 1)
            way_y = jnp.where(cell % 2 == 1, 2, 3)
            way_in = jnp.where(change == 2, way_x, way_y)
            way = jnp.where(
                gap == 0, way_in,
                jnp.where(
                    gap == -blk_count, 0,
                    jnp.where(gap == blk_count, 1, jnp.where(gap == -1, 2, 3)),
                ),
            )

            @pl.when(inside)
            def _():
                face_of_ref[slot * 4 + way] = face

    rows = lax.broadcasted_iota(jnp.int32, (width, width), 0)
    cols = lax.broadcasted_iota(jnp.int32, (width, width), 1)
    on_diag = rows == cols
    for slot in range(CELLS):
        base_ref[cell_ref[slot]] = src_ref[:, slot, :]
        diag_copies[slot].wait()
    for slot in range(CELLS):
        for face in range(6):

            @pl.when(flag_ref[slot, face] == 1)
            def _():
                face_copies[slot][face].wait()
                center_ref[slot] = center_ref[slot] + face_ref[slot, face]

    for slot in range(CELLS):
        center = center_ref[slot]
        marked = jnp.where(on_diag, center, 0.0)
        inv_row = 1.0 / jnp.sum(marked, axis=0, keepdims=True)
        inv_col = 1.0 / jnp.sum(marked, axis=1, keepdims=True)
        first = jnp.where(on_diag, inv_col, 0.0)
        x_ref[slot] = 2.0 * first - inv_col * (center * inv_row)
    for sweep in range(SWEEPS - 1):
        for slot in range(CELLS):
            y_ref[slot] = dot_full(center_ref[slot], x_ref[slot])
        for slot in range(CELLS):
            x_ref[slot] = 2.0 * x_ref[slot] - dot_full(x_ref[slot], y_ref[slot])
    for slot in range(CELLS):
        for face in range(6):
            pl.when(nbr_ref[slot, face] >= 0)(face_copies[slot][face].wait)
    for slot in range(CELLS):
        cell = cell_ref[slot]
        x_high, x_low = split_halves(x_ref[slot])
        inv_high_ref[cell] = x_high
        inv_low_ref[cell] = x_low
        own = dot_full(x_ref[slot], center_ref[slot]) - jnp.where(on_diag, 1.0, 0.0)
        high_ref[cell], low_ref[cell] = split_halves(own)
        for way in range(4):
            face = face_of_ref[slot * 4 + way]
            block = jnp.where(face >= 0, face_ref[slot, jnp.maximum(face, 0)], 0.0)
            f_high, f_low = split_halves(block)
            product = dot32(x_high, f_high) + dot32(x_low, f_high) + dot32(x_high, f_low)
            if way < 2:
                leaves = cell // 2 == way
                inner = FROM_X + cell
                place = cell % 2
            else:
                leaves = cell % 2 == way - 2
                inner = FROM_Y + cell
                place = cell // 2
            entry = jnp.where(leaves, OUTWARD + 2 * way + place, inner)
            high_ref[entry], low_ref[entry] = split_halves(product)
            product_ref[entry] = product
    tall = padded(width)
    for way, ref in enumerate((dom_prev_ref, dom_next_ref, blk_prev_ref, blk_next_ref)):
        pair = [product_ref[OUTWARD + 2 * way + place] for place in range(2)]
        for place in range(2):
            ref[tall * place : tall * place + width, :] = pair[place][:, :128]
        ref[2 * tall : 2 * tall + width, :] = tails_of(pair)
    halves = [stack_halves(base_ref[cell]) for cell in range(CELLS)]
    local = local_products(halves, high_ref, low_ref)
    outward = outward_products(halves, high_ref, low_ref)
    for cell in range(CELLS):
        local_ref[cell] = local[cell]
    for entry in range(8):
        outward_ref[entry] = outward[entry]
    send_along_blk(local, outward, blk_prev_ref, blk_next_ref, 3 * tall)
    send_to_dom_prev(local, outward, dom_prev_ref, 3 * tall)


FROM_BLK = 5
FROM_DOM = 6
RELAYED = 2


def middle_kernel(first, local_ref, outward_ref, prev_ref, next_ref, sum_ref, dom_next_ref):
    rows = local_ref.shape[1]
    tail = local_ref.shape[2] - 128

    def got(ref, place):
        return get_rows(ref, first, rows, tail, FROM_BLK, place)

    sums = []
    for cell in range(CELLS):
        given = prev_ref if cell % 2 == 0 else next_ref
        sums.append(local_ref[cell] + got(given, cell // 2))
        sum_ref[cell] = sums[cell]
    put_rows(
        dom_next_ref, 0,
        [outward_ref[2], outward_ref[3], sums[2], sums[3], got(prev_ref, 4), got(next_ref, 4)],
    )


def relay_kernel(first, tail, sum_ref, dom_ref, prev_ref, next_ref):
    rows = sum_ref.shape[1]

    def got(place):
        return get_rows(dom_ref, first, rows, tail, FROM_DOM, place)

    put_rows(prev_ref, 0, [got(4), got(0)])
    put_rows(next_ref, 0, [got(5), got(1)])


def pair_kernel(first_pair, last_pair, older_count, *refs):
    sum_ref, outward_ref, blk_prev_ref, blk_next_ref, dom_prev_ref, dom_next_ref = refs[:6]
    turn_prev_ref, turn_next_ref, high_ref, low_ref = refs[6:10]
    refs = refs[10:]
    rows = sum_ref.shape[1]
    width = sum_ref.shape[2]
    first = 0
    if first_pair:
        tall = padded(width)
        first = 3 * tall
        dom_blocks_ref = refs[0]
        refs = refs[1:]
    else:
        in_high_ref, in_low_ref = refs[:2]
        refs = refs[2:]
    older = refs[:older_count]
    refs = refs[older_count:]
    if last_pair:
        gram_in_ref, gram_ref, odd_ref, even_ref = refs
    else:
        odd_ref, even_ref, local_out_ref, outward_out_ref, prev_ref, next_ref, dom_out_ref = refs[:7]
    if first_pair:
        in_high_ref, in_low_ref = refs[7:]
        for way, ref in enumerate((dom_blocks_ref, dom_next_ref, blk_prev_ref, blk_next_ref)):
            for place in range(2):
                main = ref[tall * place : tall * place + width, :]
                tail = tail_at(ref[2 * tall : 2 * tall + width, :], width - 128, place)
                high, low = split_halves(jnp.concatenate([main, tail], axis=1))
                in_high_ref[2 * way + place] = high
                in_low_ref[2 * way + place] = low

    tail = width - 128

    def from_blk(ref, place):
        return get_rows(ref, first, rows, tail, FROM_BLK, place)

    def from_dom_prev(place):
        return get_rows(dom_prev_ref, 0, rows, tail, FROM_DOM, place)

    def from_dom_next(place):
        return get_rows(dom_next_ref, first, rows, tail, FROM_DOM, place)

    def turned(ref, place):
        return get_rows(ref, 0, rows, tail, RELAYED, place)

    odd = [
        sum_ref[cell] + (from_dom_prev if cell < 2 else from_dom_next)(cell % 2)
        for cell in range(CELLS)
    ]
    ring = [
        from_dom_prev(2) + outward_ref[0],
        from_dom_prev(3) + outward_ref[1],
        from_dom_next(2) + outward_ref[2] + turned(turn_prev_ref, 0),
        from_dom_next(3) + outward_ref[3] + turned(turn_next_ref, 0),
        from_blk(blk_prev_ref, 2) + outward_ref[4] + from_dom_prev(4),
        from_blk(blk_prev_ref, 3) + outward_ref[5] + turned(turn_prev_ref, 1),
        from_blk(blk_next_ref, 2) + outward_ref[6] + from_dom_prev(5),
        from_blk(blk_next_ref, 3) + outward_ref[7] + turned(turn_next_ref, 1),
    ]
    for cell in range(CELLS):
        odd_ref[cell] = odd[cell]
    even = local_products([stack_halves(value) for value in odd], high_ref, low_ref)
    for place, value in enumerate(ring):
        cell = RING_TARGETS[place]
        even[cell] = even[cell] + row_times(
            *stack_halves(value), in_high_ref[place], in_low_ref[place]
        )
    for cell in range(CELLS):
        even_ref[cell] = even[cell]
    if last_pair:
        bases = list(older) + [odd_ref, even_ref]
        gram = gram_rows(ITERS - 1, bases, gram_in_ref[...])
        gram = gram_rows(ITERS, bases, gram)
        half = gram.shape[0] // 2
        gram = gram[:half] + pltpu.roll(gram[half:], 64, 1)
        for place in range(gram_ref.shape[0]):
            gram_ref[place] = gram
    else:
        halves = [stack_halves(value) for value in even]
        local = local_products(halves, high_ref, low_ref)
        outward = outward_products(halves, high_ref, low_ref)
        for cell in range(CELLS):
            local_out_ref[cell] = local[cell]
        for entry in range(8):
            outward_out_ref[entry] = outward[entry]
        send_along_blk(local, outward, prev_ref, next_ref, 0)
        send_to_dom_prev(local, outward, dom_out_ref, 0)


def gram_kernel(newest, *refs):
    base_refs = refs[: newest + 1]
    gram = None
    if newest > 0:
        gram = gram_rows(newest - 1, base_refs, refs[newest + 1][...])
    refs[-1][...] = gram_rows(newest, base_refs, gram)


def gram_rows(step, base_refs, gram):
    newest = base_refs[step]
    nrhs = newest.shape[1]
    lanes = lax.broadcasted_iota(jnp.int32, (nrhs, 128), 1)
    if gram is None:
        gram = jnp.zeros((nrhs, 128), F32)
    for col in range(step + 1):
        total = newest[0] * base_refs[col][0]
        for cell in range(1, CELLS):
            total = total + newest[cell] * base_refs[col][cell]
        value = jnp.sum(total, axis=1, keepdims=True)
        gram = jnp.where(lanes == pair_lane(step, col), value, gram)
    return gram


def finish_kernel(*refs):
    gram_ref = refs[0]
    base_refs = refs[1 : 1 + ITERS]
    inv_high_ref, inv_low_ref, slot_ref, adjoint_ref, rel_ref, fine_ref = refs[1 + ITERS :]
    count = ITERS + 1
    packed = sum_parts(gram_ref)
    gram = jnp.concatenate([packed, pltpu.roll(packed, 64, 1)], axis=0)

    def lane(row, col):
        place = pair_lane(row, col)
        return jnp.broadcast_to(gram[:, place : place + 1], gram.shape)

    diag = [lane(j, j) for j in range(count)]
    scale = [1.0 / jnp.sqrt(value) for value in diag]
    start = jnp.sqrt(diag[0])
    lower = [[None] * count for j in range(count)]
    solved = []
    ratio = [scale[j] * start for j in range(count)]
    smallest = jnp.ones_like(gram)
    inv_pivot = []
    for col in range(count):
        pivot = jnp.ones_like(gram)
        for k in range(col):
            pivot = pivot - lower[col][k] * lower[col][k]
        smallest = jnp.minimum(smallest, pivot)
        inv_root = 1.0 / jnp.sqrt(pivot)
        inv_pivot.append(inv_root)
        for row in range(col + 1, count):
            value = lane(row, col) * scale[row] * scale[col]
            for k in range(col):
                value = value - lower[row][k] * lower[col][k]
            lower[row][col] = value * inv_root
        right = ratio[col] if col % 2 == 0 else -ratio[col]
        for k in range(col):
            right = right - lower[col][k] * solved[k]
        solved.append(right * inv_root)
    squares = solved[0] * solved[0]
    for j in range(1, count):
        squares = squares + solved[j] * solved[j]
    rel = 1.0 / jnp.sqrt(squares)
    back = [None] * count
    for j in reversed(range(count)):
        value = solved[j]
        for k in range(j + 1, count):
            value = value - lower[k][j] * back[k]
        back[j] = value * inv_pivot[j]
    inv_squares = 1.0 / squares
    residual = [ratio[j] * back[j] * inv_squares for j in range(count)]
    coeffs = [None] * ITERS
    coeffs[ITERS - 1] = -residual[ITERS]
    for j in reversed(range(1, ITERS)):
        coeffs[j - 1] = -residual[j] - coeffs[j]
    lanes = lax.broadcasted_iota(jnp.int32, gram.shape, 1)
    good = (smallest > PIVOT_FLOOR) & (rel > RESIDUAL_FLOOR) & (rel < 2.0)
    for j in range(count):
        good = good & (diag[j] > 1e-30) & (diag[j] < 1e36)
    worst = jnp.min(jnp.where(good, 1.0, 0.0))
    fine_ref[0] = jnp.where(worst > 0.5, 1, 0).astype(jnp.int32)
    rel_ref[...] = jnp.transpose(rel)[0:1, :]
    width = base_refs[0].shape[-1]
    wide = [
        jnp.concatenate([value, value], axis=1)[:, :width] for value in coeffs
    ]
    results = []
    for cell in range(CELLS):
        total = wide[0] * base_refs[0][cell]
        for j in range(1, ITERS):
            total = total + wide[j] * base_refs[j][cell]
        stacked, high = stack_halves(total)
        results.append(row_times(stacked, high, inv_high_ref[cell], inv_low_ref[cell]))
    for slot in range(CELLS):
        value = results[0]
        for cell in range(1, CELLS):
            value = jnp.where(slot_ref[cell] == slot, results[cell], value)
        adjoint_ref[:, slot, :] = value


def vmem(count):
    return [pl.BlockSpec(memory_space=pltpu.VMEM)] * count


def smem(count):
    return [pl.BlockSpec(memory_space=pltpu.SMEM)] * count


PARAMS = pltpu.CompilerParams(vmem_limit_bytes=VMEM_LIMIT)


def struct(*shape, kind=F32):
    return jax.ShapeDtypeStruct(shape, kind)


def spread_kernel(parts_ref, copies_ref):
    total = sum_parts(parts_ref)
    for place in range(copies_ref.shape[0]):
        copies_ref[place] = total


def sum_parts(parts_ref):
    total = parts_ref[0]
    for place in range(1, parts_ref.shape[0]):
        total = total + parts_ref[place]
    return total


def near_size():
    dom_count = lax.axis_size("dom")
    return 4 if dom_count % 4 == 0 else dom_count


def sum_devices(copies):
    dom_count, blk_count = (lax.axis_size("dom"), lax.axis_size("blk"))
    inner = near_size()
    size = inner * blk_count
    near = [
        [first + k for k in range(size)] for first in range(0, dom_count * blk_count, size)
    ]
    far = [[first + k for k in range(0, dom_count, inner)] for first in range(inner)]
    parts = lax.all_to_all(copies, ("dom", "blk"), 0, 0, axis_index_groups=near)
    copies = pl.pallas_call(
        spread_kernel,
        out_shape=struct(dom_count // inner, *copies.shape[1:]),
        in_specs=vmem(1),
        out_specs=vmem(1)[0],
        compiler_params=PARAMS,
        name="sum_near",
    )(parts)
    return lax.all_to_all(copies, "dom", 0, 0, axis_index_groups=far)


def rotated(value, axis, steps):
    count = lax.axis_size(axis)
    return lax.ppermute(
        value, axis, [(source, (source + steps) % count) for source in range(count)]
    )


def both_ways(to_prev, to_next, axis):
    return rotated(to_next, axis, 1), rotated(to_prev, axis, -1)


def shards(adjoint_source, diag_blocks, face_blocks, neighbors, partner, flags):
    nrhs, elements, width = adjoint_source.shape
    block = (width, width)
    tall = padded(width)
    field = struct(CELLS, nrhs, width)
    ring = struct(8, nrhs, width)
    blk_edge = struct(7 * nrhs, 128)
    dom_edge = struct(8 * nrhs, 128)
    turn_edge = struct(3 * nrhs, 128)
    with_blocks = lambda edge: struct(3 * tall + edge.shape[0], 128)
    cost = lambda flops, data: pl.CostEstimate(
        flops=flops, bytes_accessed=data, transcendentals=0
    )
    products = 2 * nrhs * width * width * 3
    outs = pl.pallas_call(
        functools.partial(
            setup_kernel, dom_count=lax.axis_size("dom"), blk_count=lax.axis_size("blk")
        ),
        out_shape=(
            struct(BLOCKS, *block, kind=BF16), struct(BLOCKS, *block, kind=BF16),
            struct(CELLS, *block, kind=BF16), struct(CELLS, *block, kind=BF16),
            field, field, ring, with_blocks(blk_edge), with_blocks(blk_edge),
            with_blocks(dom_edge), struct(3 * tall, 128),
            struct(CELLS, kind=jnp.int32),
        ),
        in_specs=smem(2) + vmem(1) + [pl.BlockSpec(memory_space=pl.ANY)] * 2,
        out_specs=tuple(vmem(11) + smem(1)),
        scratch_shapes=[
            pltpu.VMEM((CELLS,) + block, F32),
            pltpu.VMEM((CELLS,) + block, F32),
            pltpu.VMEM((CELLS,) + block, F32),
            pltpu.VMEM((BLOCKS,) + block, F32),
            pltpu.VMEM((CELLS, 6) + block, F32),
            pltpu.SMEM((CELLS,), jnp.int32),
            pltpu.SMEM((CELLS * 4,), jnp.int32),
            pltpu.SemaphoreType.DMA((CELLS,)),
            pltpu.SemaphoreType.DMA((CELLS, 6)),
        ],
        compiler_params=PARAMS,
        name="setup_blocks",
    )(
        neighbors, flags, adjoint_source,
        jnp.transpose(diag_blocks, (1, 0, 2)), jnp.transpose(face_blocks, (1, 2, 0, 3)),
    )
    high, low, inv_high, inv_low, base, local, outward = outs[:7]
    blk_sends = outs[7:9]
    dom_send, dom_blocks = outs[9:11]
    slots = outs[11]
    bases = [base]
    gram = None
    inward = ()
    for pair in range(ITERS // 2):
        first_pair = pair == 0
        last_pair = pair == ITERS // 2 - 1
        first = 3 * tall if first_pair else 0
        from_blk = both_ways(*blk_sends, "blk")
        from_dom_next = rotated(dom_send, "dom", -1)
        if first_pair:
            inward = (rotated(dom_blocks, "dom", 1),)
        sums, dom_send = pl.pallas_call(
            functools.partial(middle_kernel, first),
            out_shape=(field, dom_edge),
            in_specs=vmem(4),
            out_specs=tuple(vmem(2)),
            compiler_params=PARAMS,
            name=f"middle_part_{pair}",
        )(local, outward, *from_blk)
        from_dom_prev = rotated(dom_send, "dom", 1)
        turns = pl.pallas_call(
            functools.partial(relay_kernel, first, width - 128),
            out_shape=(turn_edge, turn_edge),
            in_specs=vmem(2),
            out_specs=tuple(vmem(2)),
            compiler_params=PARAMS,
            name=f"relay_part_{pair}",
        )(sums, from_dom_next)
        turns = both_ways(*turns, "blk")
        newest = len(bases) - 1
        given = bases + ([gram] if newest > 0 else [])
        gram = pl.pallas_call(
            functools.partial(gram_kernel, newest),
            out_shape=struct(nrhs, 128),
            in_specs=vmem(len(given)),
            out_specs=vmem(1)[0],
            compiler_params=PARAMS,
            cost_estimate=cost(100000 * (newest + 1), 2000000),
            name=f"gram_part_{pair}",
        )(*given)
        older = bases if last_pair else []
        given = [
            sums, outward, *from_blk, from_dom_prev, from_dom_next, *turns, high, low,
            *inward, *older,
        ]
        if last_pair:
            given.append(gram)
            shapes = (struct(near_size() * lax.axis_size("blk"), nrhs // 2, 128), field, field)
        else:
            shapes = (field, field, field, ring, blk_edge, blk_edge, dom_edge)
        if first_pair:
            shapes += (struct(8, *block, kind=BF16), struct(8, *block, kind=BF16))
        outs = pl.pallas_call(
            functools.partial(pair_kernel, first_pair, last_pair, len(older)),
            out_shape=shapes,
            in_specs=vmem(len(given)),
            out_specs=tuple(vmem(len(shapes))),
            compiler_params=PARAMS,
            cost_estimate=cost(40 * products, 6000000),
            name=f"pair_part_{pair}",
        )(*given)
        if last_pair:
            gram = outs[0]
            bases.append(outs[1])
        else:
            bases += outs[:2]
            local, outward = outs[2:4]
            blk_sends = outs[4:6]
            dom_send = outs[6]
        if first_pair:
            inward = outs[7:]
    gram = sum_devices(gram)
    given = [gram] + bases + [inv_high, inv_low, slots]
    adjoint, rel, fine = pl.pallas_call(
        finish_kernel,
        out_shape=(
            struct(nrhs, elements, width), struct(1, nrhs), struct(1, kind=jnp.int32)
        ),
        in_specs=vmem(len(given) - 1) + smem(1),
        out_specs=tuple(vmem(2) + smem(1)),
        compiler_params=PARAMS,
        name="finish_part",
    )(*given)
    return lax.cond(
        fine[0] == 1,
        lambda given: (adjoint, rel.reshape(nrhs)),
        lambda given: direct_path(*given),
        (adjoint_source, diag_blocks, face_blocks, neighbors, partner, flags),
    )


def solution(mesh):
    in_specs = (
        P(None, ("dom", "blk"), None),
        P(("dom", "blk"), None, None),
        P(("dom", "blk"), None, None, None),
        P(("dom", "blk"), None),
        P(("dom", "blk"), None),
        P(("dom", "blk"), None),
    )
    out_specs = (P(None, ("dom", "blk"), None), P())
    return jax.shard_map(shards, mesh=mesh, in_specs=in_specs, out_specs=out_specs, check_vma=False)
```

```python
import functools

import jax
import jax.numpy as jnp
from jax import lax
from jax.experimental import pallas as pl
from jax.experimental.pallas import tpu as pltpu
from jax.sharding import PartitionSpec as P

EX = 2
EY = 2
ITERS = 8
SWEEPS = 3


HIGH = lax.Precision.HIGHEST


def shifted(value, axis, steps):
    count = lax.axis_size(axis)
    leading, last = (max(0, -steps), min(count, count - steps))
    return lax.ppermute(value, axis, [(source, source + steps) for source in range(leading, last)])


def invert_blocks(center):
    width = center.shape[-1]
    identity = jnp.eye(width, dtype=center.dtype)
    pivots = jnp.diagonal(center, axis1=1, axis2=2)
    estimate = identity[None, :, :] / pivots[:, :, None]
    for sweep_index in range(SWEEPS):
        product = jnp.einsum("eab,ebc->eac", center, estimate, precision=HIGH)
        estimate = 2.0 * estimate - jnp.einsum("eab,ebc->eac", estimate, product, precision=HIGH)
    return estimate


def least_squares(hessen, start_norm):
    count = len(hessen)
    cosines = []
    sines = []
    rotated_rhs = [start_norm] + [jnp.zeros_like(start_norm) for row_index in range(count)]
    upper = []
    for col_index in range(count):
        column = [hessen[col_index][row_index] for row_index in range(col_index + 2)]
        for row_index in range(col_index):
            rotated = (
                cosines[row_index] * column[row_index] + sines[row_index] * column[row_index + 1]
            )
            column[row_index + 1] = (
                -sines[row_index] * column[row_index] + cosines[row_index] * column[row_index + 1]
            )
            column[row_index] = rotated
        radius = jnp.sqrt(
            column[col_index] * column[col_index] + column[col_index + 1] * column[col_index + 1]
        )
        cosine = column[col_index] / radius
        sine_value = column[col_index + 1] / radius
        column[col_index] = radius
        cosines.append(cosine)
        sines.append(sine_value)
        rotated_rhs[col_index + 1] = -sine_value * rotated_rhs[col_index]
        rotated_rhs[col_index] = cosine * rotated_rhs[col_index]
        upper.append(column[: col_index + 1])
    coeffs = [None] * count
    for row_index in reversed(range(count)):
        total = rotated_rhs[row_index]
        for col_index in range(row_index + 1, count):
            total = total - upper[col_index][row_index] * coeffs[col_index]
        coeffs[row_index] = total / upper[row_index][row_index]
    return (coeffs, jnp.abs(rotated_rhs[count]) / start_norm)


def move_vectors_dom(vectors, offset):
    return shifted(vectors, "dom", offset)


def move_vectors_blk(vectors, offset):
    return shifted(vectors, "blk", offset)


def move_facing_dom(blocks, offset):
    return shifted(blocks, "dom", offset)


def move_facing_blk(blocks, offset):
    return shifted(blocks, "blk", offset)


def direct_path(adjoint_source, diag_blocks, face_blocks, neighbors, partner, flags):
    nrhs, elements, width = adjoint_source.shape
    blk_count = lax.axis_size("blk")
    dom_here = lax.axis_index("dom")
    blk_here = lax.axis_index("blk")
    wall_mask = (flags == 1).astype(jnp.float32)
    center = diag_blocks + jnp.einsum("ef,efab->eab", wall_mask, face_blocks, precision=HIGH)
    inverse = invert_blocks(center)
    inside = neighbors >= 0
    source_elem = jnp.where(inside, neighbors, 0)
    source_face = jnp.where(inside, partner, 0)
    owner_dev = source_elem // elements
    owner_dom = owner_dev // blk_count
    owner_blk = owner_dev % blk_count
    direction = jnp.where(
        owner_dom == dom_here - 1,
        1,
        jnp.where(
            owner_dom == dom_here + 1,
            2,
            jnp.where(owner_blk == blk_here - 1, 3, jnp.where(owner_blk == blk_here + 1, 4, 0)),
        ),
    )
    direction = jnp.where(inside, direction, 0).astype(jnp.int32)
    local_slot = source_elem % elements
    flat_direction = direction.reshape(-1)
    flat_inside = inside.reshape(-1)
    flat_local = (local_slot * 6 + source_face).reshape(-1)
    face_keys = (source_elem * 6 + source_face).reshape(-1)
    same_way = (flat_direction[None, :] == flat_direction[:, None]) & flat_inside[None, :]
    placing = jnp.sum(
        (same_way & (face_keys[None, :] < face_keys[:, None])).astype(jnp.int32), axis=1
    )
    offsets = jnp.array(
        [0, 6 * elements, 6 * elements + EY, 6 * elements + 2 * EY, 6 * elements + 2 * EY + EX],
        jnp.int32,
    )
    candidate = jnp.where(flat_direction == 0, flat_local, offsets[flat_direction] + placing)
    slot_range = jnp.arange(elements * 6, dtype=jnp.int32)

    def pick_rows(target, count):
        marked = ((flat_direction == target) & flat_inside).astype(jnp.int32)
        ranking = jnp.cumsum(marked) - marked
        chooser = (ranking[None, :] == jnp.arange(count)[:, None]) & (marked[None, :] > 0)
        return jnp.sum(jnp.where(chooser, slot_range[None, :], 0), axis=1)

    toward_next_dom = pick_rows(2, EY)
    toward_prev_dom = pick_rows(1, EY)
    toward_next_blk = pick_rows(4, EX)
    toward_prev_blk = pick_rows(3, EX)
    flat_blocks = face_blocks.reshape(elements * 6, width, width)
    block_pool = jnp.concatenate(
        [
            flat_blocks,
            move_facing_dom(jnp.take(flat_blocks, toward_next_dom, axis=0), 1),
            move_facing_dom(jnp.take(flat_blocks, toward_prev_dom, axis=0), -1),
            move_facing_blk(jnp.take(flat_blocks, toward_next_blk, axis=0), 1),
            move_facing_blk(jnp.take(flat_blocks, toward_prev_blk, axis=0), -1),
        ],
        axis=0,
    )
    column_blocks = (
        jnp.take(block_pool, candidate, axis=0) * flat_inside.astype(jnp.float32)[:, None, None]
    )
    column_blocks = column_blocks.reshape(elements, 6, width, width)
    vector_index = (direction * elements + local_slot).reshape(-1)

    def precondition(vectors):
        return jnp.einsum("eab,rea->reb", inverse, vectors, precision=HIGH)

    start_norm = jnp.sqrt(
        lax.psum(jnp.sum(adjoint_source * adjoint_source, axis=(1, 2)), ("dom", "blk"))
    )
    krylov_basis = [adjoint_source / start_norm[:, None, None]]
    hessen = []
    for iteration in range(ITERS):
        operator_vectors = precondition(krylov_basis[-1])
        gathered = jnp.concatenate(
            [
                operator_vectors,
                move_vectors_dom(operator_vectors, 1),
                move_vectors_dom(operator_vectors, -1),
                move_vectors_blk(operator_vectors, 1),
                move_vectors_blk(operator_vectors, -1),
            ],
            axis=1,
        )
        nearby = jnp.take(gathered, vector_index, axis=1).reshape(nrhs, elements, 6, width)
        own_part = jnp.einsum("eab,rea->reb", center, operator_vectors, precision=HIGH)
        mapped = own_part + jnp.einsum("egab,rega->reb", column_blocks, nearby, precision=HIGH)
        local_dots = [jnp.sum(mapped * member, axis=(1, 2)) for member in krylov_basis]
        projections = lax.psum(jnp.stack(local_dots), ("dom", "blk"))
        for row_index in range(len(krylov_basis)):
            mapped = mapped - projections[row_index][:, None, None] * krylov_basis[row_index]
        new_norm = jnp.sqrt(lax.psum(jnp.sum(mapped * mapped, axis=(1, 2)), ("dom", "blk")))
        hessen.append(jnp.concatenate([projections, new_norm[None, :]], axis=0))
        krylov_basis.append(mapped / new_norm[:, None, None])
    coeffs, rel_residual = least_squares(hessen, start_norm)
    combined = coeffs[0][:, None, None] * krylov_basis[0]
    for col_index in range(1, ITERS):
        combined = combined + coeffs[col_index][:, None, None] * krylov_basis[col_index]
    return (precondition(combined), rel_residual)


CELLS = EX * EY
F32 = jnp.float32
BF16 = jnp.bfloat16
VMEM_LIMIT = 40 * 1024 * 1024
OUT_CELLS = ((0, 1), (2, 3), (0, 2), (1, 3))
PIVOT_FLOOR = 0.02
RESIDUAL_FLOOR = 0.02


def pair_lane(row, col):
    return row * (row + 1) // 2 + col


def split_halves(value):
    high = value.astype(BF16)
    low = (value - high.astype(F32)).astype(BF16)
    return high, low


def dot32(left, right):
    return jnp.dot(left, right, preferred_element_type=F32)


def dot_full(left, right):
    return jnp.dot(left, right, preferred_element_type=F32, precision=HIGH)


def stack_halves(vector):
    high, low = split_halves(vector)
    return jnp.concatenate([high, low], axis=0), high


def row_times(stacked, high, block_high, block_low):
    rows = high.shape[0]
    both = dot32(stacked, block_high)
    return both[:rows] + both[rows:] + dot32(high, block_low)


FROM_X = CELLS
FROM_Y = 2 * CELLS
OUTWARD = 3 * CELLS
BLOCKS = OUTWARD + 8
RING_TARGETS = (0, 1, 2, 3, 0, 2, 1, 3)


def local_products(halves, high_ref, low_ref):
    results = []
    for cell in range(CELLS):
        total = None
        for source, entry in (
            (cell, cell), (cell ^ 2, FROM_X + (cell ^ 2)), (cell ^ 1, FROM_Y + (cell ^ 1))
        ):
            part = row_times(*halves[source], high_ref[entry], low_ref[entry])
            total = part if total is None else total + part
        results.append(total)
    return results


def outward_products(halves, high_ref, low_ref):
    results = []
    for way in range(4):
        for place in range(2):
            entry = OUTWARD + 2 * way + place
            results.append(
                row_times(*halves[OUT_CELLS[way][place]], high_ref[entry], low_ref[entry])
            )
    return results


def padded(width):
    return (width + 7) // 8 * 8


def tails_of(values):
    rows, width = values[0].shape
    tail = width - 128
    total = None
    for place, value in enumerate(values):
        tile = jnp.concatenate([value[:, 128:], jnp.zeros((rows, 128 - tail), F32)], axis=1)
        tile = tile if place == 0 else pltpu.roll(tile, tail * place, 1)
        total = tile if total is None else total + tile
    return total


def tail_at(tile, tail, place):
    turned = tile if place == 0 else pltpu.roll(tile, 128 - tail * place, 1)
    return turned[:, :tail]


def put_rows(ref, first, values):
    rows = values[0].shape[0]
    for place, value in enumerate(values):
        ref[first + rows * place : first + rows * (place + 1), :] = value[:, :128]
    for part in range(0, len(values), 3):
        start = first + rows * (len(values) + part // 3)
        ref[start : start + rows, :] = tails_of(values[part : part + 3])


def get_rows(ref, first, rows, tail, count, place):
    main = ref[first + rows * place : first + rows * (place + 1), :]
    start = first + rows * (count + place // 3)
    return jnp.concatenate([main, tail_at(ref[start : start + rows, :], tail, place % 3)], axis=1)


def send_along_blk(local, outward, prev_ref, next_ref, first):
    for ref, way, cells in ((prev_ref, 2, (0, 2)), (next_ref, 3, (1, 3))):
        put_rows(
            ref, first,
            [
                outward[2 * way], outward[2 * way + 1], local[cells[0]], local[cells[1]],
                outward[2 + cells[0] % 2],
            ],
        )


def send_to_dom_prev(local, outward, prev_ref, first):
    put_rows(
        prev_ref, first,
        [outward[0], outward[1], local[0], local[1], outward[4], outward[6]],
    )


def setup_kernel(
    nbr_ref, flag_ref, src_ref, diag_hbm_ref, face_hbm_ref,
    high_ref, low_ref, inv_high_ref, inv_low_ref, base_ref, local_ref, outward_ref,
    blk_prev_ref, blk_next_ref, dom_prev_ref, dom_next_ref, slot_ref,
    center_ref, x_ref, y_ref, product_ref, face_ref, cell_ref, face_of_ref, diag_sem, face_sem,
    *, dom_count, blk_count,
):
    width = diag_hbm_ref.shape[0]
    diag_copies = [
        pltpu.make_async_copy(
            diag_hbm_ref.at[:, slot, :], center_ref.at[slot], diag_sem.at[slot]
        )
        for slot in range(CELLS)
    ]
    face_copies = [
        [
            pltpu.make_async_copy(
                face_hbm_ref.at[face, :, slot, :], face_ref.at[slot, face], face_sem.at[slot, face]
            )
            for face in range(6)
        ]
        for slot in range(CELLS)
    ]
    for slot in range(CELLS):
        diag_copies[slot].start()
    for slot in range(CELLS):
        for face in range(6):
            pl.when(flag_ref[slot, face] == 1)(face_copies[slot][face].start)
    dom_here = lax.axis_index("dom")
    blk_here = lax.axis_index("blk")
    here = dom_here * blk_count + blk_here
    for slot in range(CELLS):
        up_x = jnp.int32(0)
        down_x = jnp.int32(0)
        up_y = jnp.int32(0)
        down_y = jnp.int32(0)
        for face in range(6):
            other = nbr_ref[slot, face]
            gap = jnp.where(other >= 0, other // CELLS - here, 0)
            up_x = jnp.where(gap == blk_count, 1, up_x)
            down_x = jnp.where(gap == -blk_count, 1, down_x)
            up_y = jnp.where(gap == 1, 1, up_y)
            down_y = jnp.where(gap == -1, 1, down_y)
        cell_x = jnp.where(dom_here < dom_count - 1, up_x, 1 - down_x)
        cell_y = jnp.where(blk_here < blk_count - 1, up_y, 1 - down_y)
        cell = 2 * cell_x + cell_y
        cell_ref[slot] = cell
        slot_ref[cell] = slot
    for entry in range(CELLS * 4):
        face_of_ref[entry] = -1
    for slot in range(CELLS):
        cell = cell_ref[slot]
        for face in range(6):
            other = nbr_ref[slot, face]
            inside = other >= 0
            safe = jnp.where(inside, other, 0)
            gap = safe // CELLS - here
            mate = cell_ref[safe % CELLS]
            change = jnp.bitwise_xor(mate, cell)
            way_x = jnp.where(cell >= 2, 0, 1)
            way_y = jnp.where(cell % 2 == 1, 2, 3)
            way_in = jnp.where(change == 2, way_x, way_y)
            way = jnp.where(
                gap == 0, way_in,
                jnp.where(
                    gap == -blk_count, 0,
                    jnp.where(gap == blk_count, 1, jnp.where(gap == -1, 2, 3)),
                ),
            )

            @pl.when(inside)
            def _():
                face_of_ref[slot * 4 + way] = face

    rows = lax.broadcasted_iota(jnp.int32, (width, width), 0)
    cols = lax.broadcasted_iota(jnp.int32, (width, width), 1)
    on_diag = rows == cols
    for slot in range(CELLS):
        base_ref[cell_ref[slot]] = src_ref[:, slot, :]
        diag_copies[slot].wait()
    for slot in range(CELLS):
        for face in range(6):
            pl.when(nbr_ref[slot, face] >= 0)(face_copies[slot][face].start)
    for slot in range(CELLS):
        for face in range(6):

            @pl.when(flag_ref[slot, face] == 1)
            def _():
                face_copies[slot][face].wait()
                center_ref[slot] = center_ref[slot] + face_ref[slot, face]

    for slot in range(CELLS):
        center = center_ref[slot]
        marked = jnp.where(on_diag, center, 0.0)
        inv_row = 1.0 / jnp.sum(marked, axis=0, keepdims=True)
        inv_col = 1.0 / jnp.sum(marked, axis=1, keepdims=True)
        first = jnp.where(on_diag, inv_col, 0.0)
        x_ref[slot] = 2.0 * first - inv_col * (center * inv_row)
    for sweep in range(SWEEPS - 1):
        for slot in range(CELLS):
            y_ref[slot] = dot_full(center_ref[slot], x_ref[slot])
        for slot in range(CELLS):
            x_ref[slot] = 2.0 * x_ref[slot] - dot_full(x_ref[slot], y_ref[slot])
    for slot in range(CELLS):
        for face in range(6):
            pl.when(nbr_ref[slot, face] >= 0)(face_copies[slot][face].wait)
    for slot in range(CELLS):
        cell = cell_ref[slot]
        x_high, x_low = split_halves(x_ref[slot])
        inv_high_ref[cell] = x_high
        inv_low_ref[cell] = x_low
        own = dot_full(x_ref[slot], center_ref[slot]) - jnp.where(on_diag, 1.0, 0.0)
        high_ref[cell], low_ref[cell] = split_halves(own)
        for way in range(4):
            face = face_of_ref[slot * 4 + way]
            block = jnp.where(face >= 0, face_ref[slot, jnp.maximum(face, 0)], 0.0)
            f_high, f_low = split_halves(block)
            product = dot32(x_high, f_high) + dot32(x_low, f_high) + dot32(x_high, f_low)
            if way < 2:
                leaves = cell // 2 == way
                inner = FROM_X + cell
                place = cell % 2
            else:
                leaves = cell % 2 == way - 2
                inner = FROM_Y + cell
                place = cell // 2
            entry = jnp.where(leaves, OUTWARD + 2 * way + place, inner)
            high_ref[entry], low_ref[entry] = split_halves(product)
            product_ref[entry] = product
    tall = padded(width)
    for way, ref in enumerate((dom_prev_ref, dom_next_ref, blk_prev_ref, blk_next_ref)):
        pair = [product_ref[OUTWARD + 2 * way + place] for place in range(2)]
        for place in range(2):
            ref[tall * place : tall * place + width, :] = pair[place][:, :128]
        ref[2 * tall : 2 * tall + width, :] = tails_of(pair)
    halves = [stack_halves(base_ref[cell]) for cell in range(CELLS)]
    local = local_products(halves, high_ref, low_ref)
    outward = outward_products(halves, high_ref, low_ref)
    for cell in range(CELLS):
        local_ref[cell] = local[cell]
    for entry in range(8):
        outward_ref[entry] = outward[entry]
    send_along_blk(local, outward, blk_prev_ref, blk_next_ref, 3 * tall)
    send_to_dom_prev(local, outward, dom_prev_ref, 3 * tall)


FROM_BLK = 5
FROM_DOM = 6
RELAYED = 2


def middle_kernel(first, local_ref, outward_ref, prev_ref, next_ref, sum_ref, dom_next_ref):
    rows = local_ref.shape[1]
    tail = local_ref.shape[2] - 128

    def got(ref, place):
        return get_rows(ref, first, rows, tail, FROM_BLK, place)

    sums = []
    for cell in range(CELLS):
        given = prev_ref if cell % 2 == 0 else next_ref
        sums.append(local_ref[cell] + got(given, cell // 2))
        sum_ref[cell] = sums[cell]
    put_rows(
        dom_next_ref, 0,
        [outward_ref[2], outward_ref[3], sums[2], sums[3], got(prev_ref, 4), got(next_ref, 4)],
    )


def relay_kernel(first, tail, sum_ref, dom_ref, prev_ref, next_ref):
    rows = sum_ref.shape[1]

    def got(place):
        return get_rows(dom_ref, first, rows, tail, FROM_DOM, place)

    put_rows(prev_ref, 0, [got(4), got(0)])
    put_rows(next_ref, 0, [got(5), got(1)])


def odd_kernel(first_pair, *refs):
    sum_ref, outward_ref, blk_prev_ref, blk_next_ref, dom_prev_ref, dom_next_ref = refs[:6]
    high_ref, low_ref = refs[6:8]
    rows = sum_ref.shape[1]
    width = sum_ref.shape[2]
    tail = width - 128
    first = 0
    if first_pair:
        tall = padded(width)
        first = 3 * tall
        dom_blocks_ref = refs[8]
        odd_ref, even_ref, in_high_ref, in_low_ref = refs[9:]
        for way, ref in enumerate((dom_blocks_ref, dom_next_ref, blk_prev_ref, blk_next_ref)):
            for place in range(2):
                main = ref[tall * place : tall * place + width, :]
                rest = tail_at(ref[2 * tall : 2 * tall + width, :], tail, place)
                high, low = split_halves(jnp.concatenate([main, rest], axis=1))
                in_high_ref[2 * way + place] = high
                in_low_ref[2 * way + place] = low
    else:
        in_high_ref, in_low_ref, odd_ref, even_ref = refs[8:]

    def from_blk(ref, place):
        return get_rows(ref, first, rows, tail, FROM_BLK, place)

    def from_dom_prev(place):
        return get_rows(dom_prev_ref, 0, rows, tail, FROM_DOM, place)

    def from_dom_next(place):
        return get_rows(dom_next_ref, first, rows, tail, FROM_DOM, place)

    odd = [
        sum_ref[cell] + (from_dom_prev if cell < 2 else from_dom_next)(cell % 2)
        for cell in range(CELLS)
    ]
    ring = [
        from_dom_prev(2) + outward_ref[0],
        from_dom_prev(3) + outward_ref[1],
        from_dom_next(2) + outward_ref[2],
        from_dom_next(3) + outward_ref[3],
        from_blk(blk_prev_ref, 2) + outward_ref[4] + from_dom_prev(4),
        from_blk(blk_prev_ref, 3) + outward_ref[5],
        from_blk(blk_next_ref, 2) + outward_ref[6] + from_dom_prev(5),
        from_blk(blk_next_ref, 3) + outward_ref[7],
    ]
    even = local_products([stack_halves(value) for value in odd], high_ref, low_ref)
    for place, value in enumerate(ring):
        cell = RING_TARGETS[place]
        even[cell] = even[cell] + row_times(
            *stack_halves(value), in_high_ref[place], in_low_ref[place]
        )
    for cell in range(CELLS):
        odd_ref[cell] = odd[cell]
        even_ref[cell] = even[cell]


TURNED = ((2, 0, 0), (3, 1, 0), (5, 0, 1), (7, 1, 1))


def even_kernel(last_pair, older_count, *refs):
    part_ref, turn_prev_ref, turn_next_ref, in_high_ref, in_low_ref = refs[:5]
    refs = refs[5:]
    rows = part_ref.shape[1]
    tail = part_ref.shape[2] - 128
    even = [part_ref[cell] for cell in range(CELLS)]
    for place, side, item in TURNED:
        value = get_rows((turn_prev_ref, turn_next_ref)[side], 0, rows, tail, RELAYED, item)
        cell = RING_TARGETS[place]
        even[cell] = even[cell] + row_times(
            *stack_halves(value), in_high_ref[place], in_low_ref[place]
        )
    if last_pair:
        older = refs[:older_count]
        gram_in_ref, gram_ref, even_ref = refs[older_count:]
    else:
        high_ref, low_ref = refs[:2]
        even_ref, local_out_ref, outward_out_ref, prev_ref, next_ref, dom_out_ref = refs[2:]
    for cell in range(CELLS):
        even_ref[cell] = even[cell]
    if last_pair:
        gram = gram_rows(ITERS, list(older) + [even_ref], gram_in_ref[...])
        half = gram.shape[0] // 2
        gram = gram[:half] + pltpu.roll(gram[half:], 64, 1)
        for place in range(gram_ref.shape[0]):
            gram_ref[place] = gram
    else:
        halves = [stack_halves(value) for value in even]
        local = local_products(halves, high_ref, low_ref)
        outward = outward_products(halves, high_ref, low_ref)
        for cell in range(CELLS):
            local_out_ref[cell] = local[cell]
        for entry in range(8):
            outward_out_ref[entry] = outward[entry]
        send_along_blk(local, outward, prev_ref, next_ref, 0)
        send_to_dom_prev(local, outward, dom_out_ref, 0)


def gram_kernel(newest, *refs):
    base_refs = refs[: newest + 1]
    gram = None if newest == 1 else refs[newest + 1][...]
    gram = gram_rows(newest - 1, base_refs, gram)
    refs[-1][...] = gram_rows(newest, base_refs, gram)


def gram_rows(step, base_refs, gram):
    newest = base_refs[step]
    nrhs = newest.shape[1]
    lanes = lax.broadcasted_iota(jnp.int32, (nrhs, 128), 1)
    if gram is None:
        gram = jnp.zeros((nrhs, 128), F32)
    for col in range(step + 1):
        total = newest[0] * base_refs[col][0]
        for cell in range(1, CELLS):
            total = total + newest[cell] * base_refs[col][cell]
        value = jnp.sum(total, axis=1, keepdims=True)
        gram = jnp.where(lanes == pair_lane(step, col), value, gram)
    return gram


def finish_kernel(*refs):
    gram_ref = refs[0]
    base_refs = refs[1 : 1 + ITERS]
    inv_high_ref, inv_low_ref, slot_ref, adjoint_ref, rel_ref, fine_ref = refs[1 + ITERS :]
    count = ITERS + 1
    packed = sum_parts(gram_ref)
    gram = jnp.concatenate([packed, pltpu.roll(packed, 64, 1)], axis=0)

    def lane(row, col):
        place = pair_lane(row, col)
        return jnp.broadcast_to(gram[:, place : place + 1], gram.shape)

    diag = [lane(j, j) for j in range(count)]
    scale = [lax.rsqrt(value) for value in diag]
    start = diag[0] * scale[0]
    lower = [[None] * count for j in range(count)]
    solved = []
    ratio = [scale[j] * start for j in range(count)]
    smallest = jnp.ones_like(gram)
    inv_pivot = []
    for col in range(count):
        pivot = jnp.ones_like(gram)
        for k in range(col):
            pivot = pivot - lower[col][k] * lower[col][k]
        smallest = jnp.minimum(smallest, pivot)
        inv_root = lax.rsqrt(pivot)
        inv_pivot.append(inv_root)
        for row in range(col + 1, count):
            value = lane(row, col) * scale[row] * scale[col]
            for k in range(col):
                value = value - lower[row][k] * lower[col][k]
            lower[row][col] = value * inv_root
        right = ratio[col] if col % 2 == 0 else -ratio[col]
        for k in range(col):
            right = right - lower[col][k] * solved[k]
        solved.append(right * inv_root)
    squares = solved[0] * solved[0]
    for j in range(1, count):
        squares = squares + solved[j] * solved[j]
    rel = lax.rsqrt(squares)
    back = [None] * count
    for j in reversed(range(count)):
        value = solved[j]
        for k in range(j + 1, count):
            value = value - lower[k][j] * back[k]
        back[j] = value * inv_pivot[j]
    inv_squares = 1.0 / squares
    residual = [ratio[j] * back[j] * inv_squares for j in range(count)]
    coeffs = [None] * ITERS
    coeffs[ITERS - 1] = -residual[ITERS]
    for j in reversed(range(1, ITERS)):
        coeffs[j - 1] = -residual[j] - coeffs[j]
    lanes = lax.broadcasted_iota(jnp.int32, gram.shape, 1)
    good = (smallest > PIVOT_FLOOR) & (rel > RESIDUAL_FLOOR) & (rel < 2.0)
    for j in range(count):
        good = good & (diag[j] > 1e-30) & (diag[j] < 1e36)
    worst = jnp.min(jnp.where(good, 1.0, 0.0))
    fine_ref[0] = jnp.where(worst > 0.5, 1, 0).astype(jnp.int32)
    rel_ref[...] = jnp.transpose(rel)[0:1, :]
    width = base_refs[0].shape[-1]
    wide = [
        jnp.concatenate([value, value], axis=1)[:, :width] for value in coeffs
    ]
    results = []
    for cell in range(CELLS):
        total = wide[0] * base_refs[0][cell]
        for j in range(1, ITERS):
            total = total + wide[j] * base_refs[j][cell]
        stacked, high = stack_halves(total)
        results.append(row_times(stacked, high, inv_high_ref[cell], inv_low_ref[cell]))
    for slot in range(CELLS):
        value = results[0]
        for cell in range(1, CELLS):
            value = jnp.where(slot_ref[cell] == slot, results[cell], value)
        adjoint_ref[:, slot, :] = value


def vmem(count):
    return [pl.BlockSpec(memory_space=pltpu.VMEM)] * count


def smem(count):
    return [pl.BlockSpec(memory_space=pltpu.SMEM)] * count


PARAMS = pltpu.CompilerParams(vmem_limit_bytes=VMEM_LIMIT)


def struct(*shape, kind=F32):
    return jax.ShapeDtypeStruct(shape, kind)


def spread_kernel(parts_ref, copies_ref):
    total = sum_parts(parts_ref)
    for place in range(copies_ref.shape[0]):
        copies_ref[place] = total


def sum_parts(parts_ref):
    total = parts_ref[0]
    for place in range(1, parts_ref.shape[0]):
        total = total + parts_ref[place]
    return total


def near_size():
    dom_count = lax.axis_size("dom")
    return 4 if dom_count % 4 == 0 else dom_count


def sum_devices(copies):
    dom_count, blk_count = (lax.axis_size("dom"), lax.axis_size("blk"))
    inner = near_size()
    size = inner * blk_count
    near = [
        [first + k for k in range(size)] for first in range(0, dom_count * blk_count, size)
    ]
    far = [[first + k for k in range(0, dom_count, inner)] for first in range(inner)]
    parts = lax.all_to_all(copies, ("dom", "blk"), 0, 0, axis_index_groups=near)
    copies = pl.pallas_call(
        spread_kernel,
        out_shape=struct(dom_count // inner, *copies.shape[1:]),
        in_specs=vmem(1),
        out_specs=vmem(1)[0],
        compiler_params=PARAMS,
        name="sum_near",
    )(parts)
    return lax.all_to_all(copies, "dom", 0, 0, axis_index_groups=far)


def rotated(value, axis, steps):
    count = lax.axis_size(axis)
    return lax.ppermute(
        value, axis, [(source, (source + steps) % count) for source in range(count)]
    )


def both_ways(to_prev, to_next, axis):
    return rotated(to_next, axis, 1), rotated(to_prev, axis, -1)


def shards(adjoint_source, diag_blocks, face_blocks, neighbors, partner, flags):
    nrhs, elements, width = adjoint_source.shape
    block = (width, width)
    tall = padded(width)
    field = struct(CELLS, nrhs, width)
    ring = struct(8, nrhs, width)
    blk_edge = struct(7 * nrhs, 128)
    dom_edge = struct(8 * nrhs, 128)
    turn_edge = struct(3 * nrhs, 128)
    with_blocks = lambda edge: struct(3 * tall + edge.shape[0], 128)
    cost = lambda flops, data: pl.CostEstimate(
        flops=flops, bytes_accessed=data, transcendentals=0
    )
    products = 2 * nrhs * width * width * 3
    outs = pl.pallas_call(
        functools.partial(
            setup_kernel, dom_count=lax.axis_size("dom"), blk_count=lax.axis_size("blk")
        ),
        out_shape=(
            struct(BLOCKS, *block, kind=BF16), struct(BLOCKS, *block, kind=BF16),
            struct(CELLS, *block, kind=BF16), struct(CELLS, *block, kind=BF16),
            field, field, ring, with_blocks(blk_edge), with_blocks(blk_edge),
            with_blocks(dom_edge), struct(3 * tall, 128),
            struct(CELLS, kind=jnp.int32),
        ),
        in_specs=smem(2) + vmem(1) + [pl.BlockSpec(memory_space=pl.ANY)] * 2,
        out_specs=tuple(vmem(11) + smem(1)),
        scratch_shapes=[
            pltpu.VMEM((CELLS,) + block, F32),
            pltpu.VMEM((CELLS,) + block, F32),
            pltpu.VMEM((CELLS,) + block, F32),
            pltpu.VMEM((BLOCKS,) + block, F32),
            pltpu.VMEM((CELLS, 6) + block, F32),
            pltpu.SMEM((CELLS,), jnp.int32),
            pltpu.SMEM((CELLS * 4,), jnp.int32),
            pltpu.SemaphoreType.DMA((CELLS,)),
            pltpu.SemaphoreType.DMA((CELLS, 6)),
        ],
        compiler_params=PARAMS,
        name="setup_blocks",
    )(
        neighbors, flags, adjoint_source,
        jnp.transpose(diag_blocks, (1, 0, 2)), jnp.transpose(face_blocks, (1, 2, 0, 3)),
    )
    high, low, inv_high, inv_low, base, local, outward = outs[:7]
    blk_sends = outs[7:9]
    dom_send, dom_blocks = outs[9:11]
    slots = outs[11]
    bases = [base]
    gram = None
    inward = ()
    for pair in range(ITERS // 2):
        first_pair = pair == 0
        last_pair = pair == ITERS // 2 - 1
        first = 3 * tall if first_pair else 0
        from_blk = both_ways(*blk_sends, "blk")
        from_dom_next = rotated(dom_send, "dom", -1)
        if first_pair:
            inward = (rotated(dom_blocks, "dom", 1),)
        sums, dom_send = pl.pallas_call(
            functools.partial(middle_kernel, first),
            out_shape=(field, dom_edge),
            in_specs=vmem(4),
            out_specs=tuple(vmem(2)),
            compiler_params=PARAMS,
            name=f"middle_part_{pair}",
        )(local, outward, *from_blk)
        from_dom_prev = rotated(dom_send, "dom", 1)
        turns = pl.pallas_call(
            functools.partial(relay_kernel, first, width - 128),
            out_shape=(turn_edge, turn_edge),
            in_specs=vmem(2),
            out_specs=tuple(vmem(2)),
            compiler_params=PARAMS,
            name=f"relay_part_{pair}",
        )(sums, from_dom_next)
        turns = both_ways(*turns, "blk")
        given = [sums, outward, *from_blk, from_dom_prev, from_dom_next, high, low, *inward]
        shapes = (field, field)
        if first_pair:
            shapes += (struct(8, *block, kind=BF16), struct(8, *block, kind=BF16))
        odd, part, *made = pl.pallas_call(
            functools.partial(odd_kernel, first_pair),
            out_shape=shapes,
            in_specs=vmem(len(given)),
            out_specs=tuple(vmem(len(shapes))),
            compiler_params=PARAMS,
            cost_estimate=cost(20 * products, 6000000),
            name=f"odd_part_{pair}",
        )(*given)
        if first_pair:
            inward = made
        bases.append(odd)
        newest = len(bases) - 1
        given = bases + ([gram] if newest > 1 else [])
        gram = pl.pallas_call(
            functools.partial(gram_kernel, newest),
            out_shape=struct(nrhs, 128),
            in_specs=vmem(len(given)),
            out_specs=vmem(1)[0],
            compiler_params=PARAMS,
            cost_estimate=cost(100000 * (newest + 1), 2000000),
            name=f"gram_part_{pair}",
        )(*given)
        given = [part, *turns, *inward]
        if last_pair:
            given += [*bases, gram]
            shapes = (struct(near_size() * lax.axis_size("blk"), nrhs // 2, 128), field)
        else:
            given += [high, low]
            shapes = (field, field, ring, blk_edge, blk_edge, dom_edge)
        outs = pl.pallas_call(
            functools.partial(even_kernel, last_pair, len(bases)),
            out_shape=shapes,
            in_specs=vmem(len(given)),
            out_specs=tuple(vmem(len(shapes))),
            compiler_params=PARAMS,
            cost_estimate=cost(24 * products, 6000000),
            name=f"even_part_{pair}",
        )(*given)
        if last_pair:
            gram = outs[0]
        else:
            bases.append(outs[0])
            local, outward = outs[1:3]
            blk_sends = outs[3:5]
            dom_send = outs[5]
    gram = sum_devices(gram)
    given = [gram] + bases + [inv_high, inv_low, slots]
    adjoint, rel, fine = pl.pallas_call(
        finish_kernel,
        out_shape=(
            struct(nrhs, elements, width), struct(1, nrhs), struct(1, kind=jnp.int32)
        ),
        in_specs=vmem(len(given) - 1) + smem(1),
        out_specs=tuple(vmem(2) + smem(1)),
        compiler_params=PARAMS,
        name="finish_part",
    )(*given)
    return lax.cond(
        fine[0] == 1,
        lambda given: (adjoint, rel.reshape(nrhs)),
        lambda given: direct_path(*given),
        (adjoint_source, diag_blocks, face_blocks, neighbors, partner, flags),
    )


def solution(mesh):
    in_specs = (
        P(None, ("dom", "blk"), None),
        P(("dom", "blk"), None, None),
        P(("dom", "blk"), None, None, None),
        P(("dom", "blk"), None),
        P(("dom", "blk"), None),
        P(("dom", "blk"), None),
    )
    out_specs = (P(None, ("dom", "blk"), None), P())
    return jax.shard_map(shards, mesh=mesh, in_specs=in_specs, out_specs=out_specs, check_vma=False)
```

```python
import functools

import jax
import jax.numpy as jnp
from jax import lax
from jax.experimental import pallas as pl
from jax.experimental.pallas import tpu as pltpu
from jax.sharding import PartitionSpec as P

EX = 2
EY = 2
ITERS = 8
SWEEPS = 3


HIGH = lax.Precision.HIGHEST


def shifted(value, axis, steps):
    count = lax.axis_size(axis)
    leading, last = (max(0, -steps), min(count, count - steps))
    return lax.ppermute(value, axis, [(source, source + steps) for source in range(leading, last)])


def invert_blocks(center):
    width = center.shape[-1]
    identity = jnp.eye(width, dtype=center.dtype)
    pivots = jnp.diagonal(center, axis1=1, axis2=2)
    estimate = identity[None, :, :] / pivots[:, :, None]
    for sweep_index in range(SWEEPS):
        product = jnp.einsum("eab,ebc->eac", center, estimate, precision=HIGH)
        estimate = 2.0 * estimate - jnp.einsum("eab,ebc->eac", estimate, product, precision=HIGH)
    return estimate


def least_squares(hessen, start_norm):
    count = len(hessen)
    cosines = []
    sines = []
    rotated_rhs = [start_norm] + [jnp.zeros_like(start_norm) for row_index in range(count)]
    upper = []
    for col_index in range(count):
        column = [hessen[col_index][row_index] for row_index in range(col_index + 2)]
        for row_index in range(col_index):
            rotated = (
                cosines[row_index] * column[row_index] + sines[row_index] * column[row_index + 1]
            )
            column[row_index + 1] = (
                -sines[row_index] * column[row_index] + cosines[row_index] * column[row_index + 1]
            )
            column[row_index] = rotated
        radius = jnp.sqrt(
            column[col_index] * column[col_index] + column[col_index + 1] * column[col_index + 1]
        )
        cosine = column[col_index] / radius
        sine_value = column[col_index + 1] / radius
        column[col_index] = radius
        cosines.append(cosine)
        sines.append(sine_value)
        rotated_rhs[col_index + 1] = -sine_value * rotated_rhs[col_index]
        rotated_rhs[col_index] = cosine * rotated_rhs[col_index]
        upper.append(column[: col_index + 1])
    coeffs = [None] * count
    for row_index in reversed(range(count)):
        total = rotated_rhs[row_index]
        for col_index in range(row_index + 1, count):
            total = total - upper[col_index][row_index] * coeffs[col_index]
        coeffs[row_index] = total / upper[row_index][row_index]
    return (coeffs, jnp.abs(rotated_rhs[count]) / start_norm)


def move_vectors_dom(vectors, offset):
    return shifted(vectors, "dom", offset)


def move_vectors_blk(vectors, offset):
    return shifted(vectors, "blk", offset)


def move_facing_dom(blocks, offset):
    return shifted(blocks, "dom", offset)


def move_facing_blk(blocks, offset):
    return shifted(blocks, "blk", offset)


def direct_path(adjoint_source, diag_blocks, face_blocks, neighbors, partner, flags):
    nrhs, elements, width = adjoint_source.shape
    blk_count = lax.axis_size("blk")
    dom_here = lax.axis_index("dom")
    blk_here = lax.axis_index("blk")
    wall_mask = (flags == 1).astype(jnp.float32)
    center = diag_blocks + jnp.einsum("ef,efab->eab", wall_mask, face_blocks, precision=HIGH)
    inverse = invert_blocks(center)
    inside = neighbors >= 0
    source_elem = jnp.where(inside, neighbors, 0)
    source_face = jnp.where(inside, partner, 0)
    owner_dev = source_elem // elements
    owner_dom = owner_dev // blk_count
    owner_blk = owner_dev % blk_count
    direction = jnp.where(
        owner_dom == dom_here - 1,
        1,
        jnp.where(
            owner_dom == dom_here + 1,
            2,
            jnp.where(owner_blk == blk_here - 1, 3, jnp.where(owner_blk == blk_here + 1, 4, 0)),
        ),
    )
    direction = jnp.where(inside, direction, 0).astype(jnp.int32)
    local_slot = source_elem % elements
    flat_direction = direction.reshape(-1)
    flat_inside = inside.reshape(-1)
    flat_local = (local_slot * 6 + source_face).reshape(-1)
    face_keys = (source_elem * 6 + source_face).reshape(-1)
    same_way = (flat_direction[None, :] == flat_direction[:, None]) & flat_inside[None, :]
    placing = jnp.sum(
        (same_way & (face_keys[None, :] < face_keys[:, None])).astype(jnp.int32), axis=1
    )
    offsets = jnp.array(
        [0, 6 * elements, 6 * elements + EY, 6 * elements + 2 * EY, 6 * elements + 2 * EY + EX],
        jnp.int32,
    )
    candidate = jnp.where(flat_direction == 0, flat_local, offsets[flat_direction] + placing)
    slot_range = jnp.arange(elements * 6, dtype=jnp.int32)

    def pick_rows(target, count):
        marked = ((flat_direction == target) & flat_inside).astype(jnp.int32)
        ranking = jnp.cumsum(marked) - marked
        chooser = (ranking[None, :] == jnp.arange(count)[:, None]) & (marked[None, :] > 0)
        return jnp.sum(jnp.where(chooser, slot_range[None, :], 0), axis=1)

    toward_next_dom = pick_rows(2, EY)
    toward_prev_dom = pick_rows(1, EY)
    toward_next_blk = pick_rows(4, EX)
    toward_prev_blk = pick_rows(3, EX)
    flat_blocks = face_blocks.reshape(elements * 6, width, width)
    block_pool = jnp.concatenate(
        [
            flat_blocks,
            move_facing_dom(jnp.take(flat_blocks, toward_next_dom, axis=0), 1),
            move_facing_dom(jnp.take(flat_blocks, toward_prev_dom, axis=0), -1),
            move_facing_blk(jnp.take(flat_blocks, toward_next_blk, axis=0), 1),
            move_facing_blk(jnp.take(flat_blocks, toward_prev_blk, axis=0), -1),
        ],
        axis=0,
    )
    column_blocks = (
        jnp.take(block_pool, candidate, axis=0) * flat_inside.astype(jnp.float32)[:, None, None]
    )
    column_blocks = column_blocks.reshape(elements, 6, width, width)
    vector_index = (direction * elements + local_slot).reshape(-1)

    def precondition(vectors):
        return jnp.einsum("eab,rea->reb", inverse, vectors, precision=HIGH)

    start_norm = jnp.sqrt(
        lax.psum(jnp.sum(adjoint_source * adjoint_source, axis=(1, 2)), ("dom", "blk"))
    )
    krylov_basis = [adjoint_source / start_norm[:, None, None]]
    hessen = []
    for iteration in range(ITERS):
        operator_vectors = precondition(krylov_basis[-1])
        gathered = jnp.concatenate(
            [
                operator_vectors,
                move_vectors_dom(operator_vectors, 1),
                move_vectors_dom(operator_vectors, -1),
                move_vectors_blk(operator_vectors, 1),
                move_vectors_blk(operator_vectors, -1),
            ],
            axis=1,
        )
        nearby = jnp.take(gathered, vector_index, axis=1).reshape(nrhs, elements, 6, width)
        own_part = jnp.einsum("eab,rea->reb", center, operator_vectors, precision=HIGH)
        mapped = own_part + jnp.einsum("egab,rega->reb", column_blocks, nearby, precision=HIGH)
        local_dots = [jnp.sum(mapped * member, axis=(1, 2)) for member in krylov_basis]
        projections = lax.psum(jnp.stack(local_dots), ("dom", "blk"))
        for row_index in range(len(krylov_basis)):
            mapped = mapped - projections[row_index][:, None, None] * krylov_basis[row_index]
        new_norm = jnp.sqrt(lax.psum(jnp.sum(mapped * mapped, axis=(1, 2)), ("dom", "blk")))
        hessen.append(jnp.concatenate([projections, new_norm[None, :]], axis=0))
        krylov_basis.append(mapped / new_norm[:, None, None])
    coeffs, rel_residual = least_squares(hessen, start_norm)
    combined = coeffs[0][:, None, None] * krylov_basis[0]
    for col_index in range(1, ITERS):
        combined = combined + coeffs[col_index][:, None, None] * krylov_basis[col_index]
    return (precondition(combined), rel_residual)


CELLS = EX * EY
F32 = jnp.float32
BF16 = jnp.bfloat16
VMEM_LIMIT = 40 * 1024 * 1024
OUT_CELLS = ((0, 1), (2, 3), (0, 2), (1, 3))
PIVOT_FLOOR = 0.02
RESIDUAL_FLOOR = 0.02


def pair_lane(row, col):
    return row * (row + 1) // 2 + col


def split_halves(value):
    high = value.astype(BF16)
    low = (value - high.astype(F32)).astype(BF16)
    return high, low


def dot32(left, right):
    return jnp.dot(left, right, preferred_element_type=F32)


def dot_halves(left_high, left_low, right_high, right_low):
    small = dot32(left_low, right_high) + dot32(left_high, right_low)
    return dot32(left_high, right_high) + small


def stack_halves(vector):
    high, low = split_halves(vector)
    return jnp.concatenate([high, low], axis=0), high


def row_times(stacked, high, block_high, block_low):
    rows = high.shape[0]
    both = dot32(stacked, block_high)
    return both[:rows] + both[rows:] + dot32(high, block_low)


FROM_X = CELLS
FROM_Y = 2 * CELLS
OUTWARD = 3 * CELLS
BLOCKS = OUTWARD + 8
RING_TARGETS = (0, 1, 2, 3, 0, 2, 1, 3)


def local_products(halves, high_ref, low_ref):
    results = []
    for cell in range(CELLS):
        total = None
        for source, entry in (
            (cell, cell), (cell ^ 2, FROM_X + (cell ^ 2)), (cell ^ 1, FROM_Y + (cell ^ 1))
        ):
            part = row_times(*halves[source], high_ref[entry], low_ref[entry])
            total = part if total is None else total + part
        results.append(total)
    return results


def outward_products(halves, high_ref, low_ref):
    results = []
    for way in range(4):
        for place in range(2):
            entry = OUTWARD + 2 * way + place
            results.append(
                row_times(*halves[OUT_CELLS[way][place]], high_ref[entry], low_ref[entry])
            )
    return results


def padded(width):
    return (width + 7) // 8 * 8


def tails_of(values):
    rows, width = values[0].shape
    tail = width - 128
    total = None
    for place, value in enumerate(values):
        tile = jnp.concatenate([value[:, 128:], jnp.zeros((rows, 128 - tail), F32)], axis=1)
        tile = tile if place == 0 else pltpu.roll(tile, tail * place, 1)
        total = tile if total is None else total + tile
    return total


def tail_at(tile, tail, place):
    turned = tile if place == 0 else pltpu.roll(tile, 128 - tail * place, 1)
    return turned[:, :tail]


def put_rows(ref, first, values):
    rows = values[0].shape[0]
    for place, value in enumerate(values):
        ref[first + rows * place : first + rows * (place + 1), :] = value[:, :128]
    for part in range(0, len(values), 3):
        start = first + rows * (len(values) + part // 3)
        ref[start : start + rows, :] = tails_of(values[part : part + 3])


def get_rows(ref, first, rows, tail, count, place):
    main = ref[first + rows * place : first + rows * (place + 1), :]
    start = first + rows * (count + place // 3)
    return jnp.concatenate([main, tail_at(ref[start : start + rows, :], tail, place % 3)], axis=1)


def send_along_blk(local, outward, prev_ref, next_ref, first):
    for ref, way, cells in ((prev_ref, 2, (0, 2)), (next_ref, 3, (1, 3))):
        put_rows(
            ref, first,
            [
                outward[2 * way], outward[2 * way + 1], local[cells[0]], local[cells[1]],
                outward[2 + cells[0] % 2],
            ],
        )


def send_to_dom_prev(local, outward, prev_ref, first):
    put_rows(
        prev_ref, first,
        [outward[0], outward[1], local[0], local[1], outward[4], outward[6]],
    )


def setup_kernel(
    nbr_ref, flag_ref, src_ref, diag_hbm_ref, face_hbm_ref,
    high_ref, low_ref, inv_high_ref, inv_low_ref, base_ref, local_ref, outward_ref,
    blk_prev_ref, blk_next_ref, dom_prev_ref, dom_next_ref, slot_ref,
    center_ref, x_ref, d_high_ref, d_low_ref, product_ref, face_ref, cell_ref, face_of_ref, diag_sem, face_sem,
    *, dom_count, blk_count,
):
    width = diag_hbm_ref.shape[0]
    diag_copies = [
        pltpu.make_async_copy(
            diag_hbm_ref.at[:, slot, :], center_ref.at[slot], diag_sem.at[slot]
        )
        for slot in range(CELLS)
    ]
    face_copies = [
        [
            pltpu.make_async_copy(
                face_hbm_ref.at[face, :, slot, :], face_ref.at[slot, face], face_sem.at[slot, face]
            )
            for face in range(6)
        ]
        for slot in range(CELLS)
    ]
    for slot in range(CELLS):
        diag_copies[slot].start()
    for slot in range(CELLS):
        for face in range(6):
            pl.when(flag_ref[slot, face] == 1)(face_copies[slot][face].start)
    for slot in range(CELLS):
        for face in range(6):
            pl.when(nbr_ref[slot, face] >= 0)(face_copies[slot][face].start)
    dom_here = lax.axis_index("dom")
    blk_here = lax.axis_index("blk")
    here = dom_here * blk_count + blk_here
    for slot in range(CELLS):
        up_x = jnp.int32(0)
        down_x = jnp.int32(0)
        up_y = jnp.int32(0)
        down_y = jnp.int32(0)
        for face in range(6):
            other = nbr_ref[slot, face]
            gap = jnp.where(other >= 0, other // CELLS - here, 0)
            up_x = jnp.where(gap == blk_count, 1, up_x)
            down_x = jnp.where(gap == -blk_count, 1, down_x)
            up_y = jnp.where(gap == 1, 1, up_y)
            down_y = jnp.where(gap == -1, 1, down_y)
        cell_x = jnp.where(dom_here < dom_count - 1, up_x, 1 - down_x)
        cell_y = jnp.where(blk_here < blk_count - 1, up_y, 1 - down_y)
        cell = 2 * cell_x + cell_y
        cell_ref[slot] = cell
        slot_ref[cell] = slot
    for entry in range(CELLS * 4):
        face_of_ref[entry] = -1
    for slot in range(CELLS):
        cell = cell_ref[slot]
        for face in range(6):
            other = nbr_ref[slot, face]
            inside = other >= 0
            safe = jnp.where(inside, other, 0)
            gap = safe // CELLS - here
            mate = cell_ref[safe % CELLS]
            change = jnp.bitwise_xor(mate, cell)
            way_x = jnp.where(cell >= 2, 0, 1)
            way_y = jnp.where(cell % 2 == 1, 2, 3)
            way_in = jnp.where(change == 2, way_x, way_y)
            way = jnp.where(
                gap == 0, way_in,
                jnp.where(
                    gap == -blk_count, 0,
                    jnp.where(gap == blk_count, 1, jnp.where(gap == -1, 2, 3)),
                ),
            )

            @pl.when(inside)
            def _():
                face_of_ref[slot * 4 + way] = face

    rows = lax.broadcasted_iota(jnp.int32, (width, width), 0)
    cols = lax.broadcasted_iota(jnp.int32, (width, width), 1)
    on_diag = rows == cols
    for slot in range(CELLS):
        base_ref[cell_ref[slot]] = src_ref[:, slot, :]
        diag_copies[slot].wait()
    for slot in range(CELLS):
        for face in range(6):

            @pl.when(flag_ref[slot, face] == 1)
            def _():
                face_copies[slot][face].wait()
                center_ref[slot] = center_ref[slot] + face_ref[slot, face]

    for slot in range(CELLS):
        center = center_ref[slot]
        marked = jnp.where(on_diag, center, 0.0)
        inv_row = 1.0 / jnp.sum(marked, axis=0, keepdims=True)
        inv_col = 1.0 / jnp.sum(marked, axis=1, keepdims=True)
        defect = jnp.where(on_diag, 0.0, -inv_col * center)
        x_ref[slot] = jnp.where(on_diag, inv_col, defect * inv_row)
        d_high_ref[slot], d_low_ref[slot] = split_halves(defect)
    for sweep in range(1, SWEEPS):
        squares = [
            dot_halves(d_high_ref[slot], d_low_ref[slot], d_high_ref[slot], d_low_ref[slot])
            for slot in range(CELLS)
        ]
        for slot in range(CELLS):
            d_high_ref[slot], d_low_ref[slot] = split_halves(squares[slot])
        for slot in range(CELLS):
            x_high, x_low = split_halves(x_ref[slot])
            x_ref[slot] = x_ref[slot] + dot_halves(
                d_high_ref[slot], d_low_ref[slot], x_high, x_low
            )
    for slot in range(CELLS):
        for face in range(6):
            pl.when(nbr_ref[slot, face] >= 0)(face_copies[slot][face].wait)
    for slot in range(CELLS):
        cell = cell_ref[slot]
        x_high, x_low = split_halves(x_ref[slot])
        inv_high_ref[cell] = x_high
        inv_low_ref[cell] = x_low
        own = -dot_halves(d_high_ref[slot], d_low_ref[slot], d_high_ref[slot], d_low_ref[slot])
        high_ref[cell], low_ref[cell] = split_halves(own)
        for way in range(4):
            face = face_of_ref[slot * 4 + way]
            block = jnp.where(face >= 0, face_ref[slot, jnp.maximum(face, 0)], 0.0)
            f_high, f_low = split_halves(block)
            product = dot_halves(x_high, x_low, f_high, f_low)
            if way < 2:
                leaves = cell // 2 == way
                inner = FROM_X + cell
                place = cell % 2
            else:
                leaves = cell % 2 == way - 2
                inner = FROM_Y + cell
                place = cell // 2
            entry = jnp.where(leaves, OUTWARD + 2 * way + place, inner)
            high_ref[entry], low_ref[entry] = split_halves(product)
            product_ref[entry] = product
    tall = padded(width)
    for way, ref in enumerate((dom_prev_ref, dom_next_ref, blk_prev_ref, blk_next_ref)):
        pair = [product_ref[OUTWARD + 2 * way + place] for place in range(2)]
        for place in range(2):
            ref[tall * place : tall * place + width, :] = pair[place][:, :128]
        ref[2 * tall : 2 * tall + width, :] = tails_of(pair)
    halves = [stack_halves(base_ref[cell]) for cell in range(CELLS)]
    local = local_products(halves, high_ref, low_ref)
    outward = outward_products(halves, high_ref, low_ref)
    for cell in range(CELLS):
        local_ref[cell] = local[cell]
    for entry in range(8):
        outward_ref[entry] = outward[entry]
    send_along_blk(local, outward, blk_prev_ref, blk_next_ref, 3 * tall)
    send_to_dom_prev(local, outward, dom_prev_ref, 3 * tall)


FROM_BLK = 5
FROM_DOM = 6
RELAYED = 2


def middle_kernel(first, local_ref, outward_ref, prev_ref, next_ref, sum_ref, dom_next_ref):
    rows = local_ref.shape[1]
    tail = local_ref.shape[2] - 128

    def got(ref, place):
        return get_rows(ref, first, rows, tail, FROM_BLK, place)

    sums = []
    for cell in range(CELLS):
        given = prev_ref if cell % 2 == 0 else next_ref
        sums.append(local_ref[cell] + got(given, cell // 2))
        sum_ref[cell] = sums[cell]
    put_rows(
        dom_next_ref, 0,
        [outward_ref[2], outward_ref[3], sums[2], sums[3], got(prev_ref, 4), got(next_ref, 4)],
    )


def relay_kernel(first, tail, sum_ref, dom_ref, prev_ref, next_ref):
    rows = sum_ref.shape[1]

    def got(place):
        return get_rows(dom_ref, first, rows, tail, FROM_DOM, place)

    put_rows(prev_ref, 0, [got(4), got(0)])
    put_rows(next_ref, 0, [got(5), got(1)])


def odd_kernel(first_pair, *refs):
    sum_ref, outward_ref, blk_prev_ref, blk_next_ref, dom_prev_ref, dom_next_ref = refs[:6]
    high_ref, low_ref = refs[6:8]
    rows = sum_ref.shape[1]
    width = sum_ref.shape[2]
    tail = width - 128
    first = 0
    if first_pair:
        tall = padded(width)
        first = 3 * tall
        dom_blocks_ref = refs[8]
        odd_ref, even_ref, in_high_ref, in_low_ref = refs[9:]
        for way, ref in enumerate((dom_blocks_ref, dom_next_ref, blk_prev_ref, blk_next_ref)):
            for place in range(2):
                main = ref[tall * place : tall * place + width, :]
                rest = tail_at(ref[2 * tall : 2 * tall + width, :], tail, place)
                high, low = split_halves(jnp.concatenate([main, rest], axis=1))
                in_high_ref[2 * way + place] = high
                in_low_ref[2 * way + place] = low
    else:
        in_high_ref, in_low_ref, odd_ref, even_ref = refs[8:]

    def from_blk(ref, place):
        return get_rows(ref, first, rows, tail, FROM_BLK, place)

    def from_dom_prev(place):
        return get_rows(dom_prev_ref, 0, rows, tail, FROM_DOM, place)

    def from_dom_next(place):
        return get_rows(dom_next_ref, first, rows, tail, FROM_DOM, place)

    odd = [
        sum_ref[cell] + (from_dom_prev if cell < 2 else from_dom_next)(cell % 2)
        for cell in range(CELLS)
    ]
    ring = [
        from_dom_prev(2) + outward_ref[0],
        from_dom_prev(3) + outward_ref[1],
        from_dom_next(2) + outward_ref[2],
        from_dom_next(3) + outward_ref[3],
        from_blk(blk_prev_ref, 2) + outward_ref[4] + from_dom_prev(4),
        from_blk(blk_prev_ref, 3) + outward_ref[5],
        from_blk(blk_next_ref, 2) + outward_ref[6] + from_dom_prev(5),
        from_blk(blk_next_ref, 3) + outward_ref[7],
    ]
    even = local_products([stack_halves(value) for value in odd], high_ref, low_ref)
    for place, value in enumerate(ring):
        cell = RING_TARGETS[place]
        even[cell] = even[cell] + row_times(
            *stack_halves(value), in_high_ref[place], in_low_ref[place]
        )
    for cell in range(CELLS):
        odd_ref[cell] = odd[cell]
        even_ref[cell] = even[cell]


TURNED = ((2, 0, 0), (3, 1, 0), (5, 0, 1), (7, 1, 1))


def even_kernel(last_pair, older_count, *refs):
    part_ref, turn_prev_ref, turn_next_ref, in_high_ref, in_low_ref = refs[:5]
    refs = refs[5:]
    rows = part_ref.shape[1]
    tail = part_ref.shape[2] - 128
    even = [part_ref[cell] for cell in range(CELLS)]
    for place, side, item in TURNED:
        value = get_rows((turn_prev_ref, turn_next_ref)[side], 0, rows, tail, RELAYED, item)
        cell = RING_TARGETS[place]
        even[cell] = even[cell] + row_times(
            *stack_halves(value), in_high_ref[place], in_low_ref[place]
        )
    if last_pair:
        older = refs[:older_count]
        gram_in_ref, gram_ref, even_ref = refs[older_count:]
    else:
        high_ref, low_ref = refs[:2]
        even_ref, local_out_ref, outward_out_ref, prev_ref, next_ref, dom_out_ref = refs[2:]
    for cell in range(CELLS):
        even_ref[cell] = even[cell]
    if last_pair:
        gram = gram_rows(ITERS, list(older) + [even_ref], gram_in_ref[...])
        half = gram.shape[0] // 2
        gram = gram[:half] + pltpu.roll(gram[half:], 64, 1)
        for place in range(gram_ref.shape[0]):
            gram_ref[place] = gram
    else:
        halves = [stack_halves(value) for value in even]
        local = local_products(halves, high_ref, low_ref)
        outward = outward_products(halves, high_ref, low_ref)
        for cell in range(CELLS):
            local_out_ref[cell] = local[cell]
        for entry in range(8):
            outward_out_ref[entry] = outward[entry]
        send_along_blk(local, outward, prev_ref, next_ref, 0)
        send_to_dom_prev(local, outward, dom_out_ref, 0)


def gram_kernel(newest, *refs):
    base_refs = refs[: newest + 1]
    gram = None if newest == 1 else refs[newest + 1][...]
    gram = gram_rows(newest - 1, base_refs, gram)
    refs[-1][...] = gram_rows(newest, base_refs, gram)


def gram_rows(step, base_refs, gram):
    newest = base_refs[step]
    nrhs = newest.shape[1]
    lanes = lax.broadcasted_iota(jnp.int32, (nrhs, 128), 1)
    if gram is None:
        gram = jnp.zeros((nrhs, 128), F32)
    for col in range(step + 1):
        total = newest[0] * base_refs[col][0]
        for cell in range(1, CELLS):
            total = total + newest[cell] * base_refs[col][cell]
        value = jnp.sum(total, axis=1, keepdims=True)
        gram = jnp.where(lanes == pair_lane(step, col), value, gram)
    return gram


def finish_kernel(*refs):
    gram_ref = refs[0]
    base_refs = refs[1 : 1 + ITERS]
    inv_high_ref, inv_low_ref, slot_ref, adjoint_ref, rel_ref, fine_ref = refs[1 + ITERS :]
    count = ITERS + 1
    packed = sum_parts(gram_ref)
    gram = jnp.concatenate([packed, pltpu.roll(packed, 64, 1)], axis=0)

    def lane(row, col):
        place = pair_lane(row, col)
        return jnp.broadcast_to(gram[:, place : place + 1], gram.shape)

    diag = [lane(j, j) for j in range(count)]
    scale = [lax.rsqrt(value) for value in diag]
    start = diag[0] * scale[0]
    lower = [[None] * count for j in range(count)]
    solved = []
    ratio = [scale[j] * start for j in range(count)]
    smallest = jnp.ones_like(gram)
    inv_pivot = []
    for col in range(count):
        pivot = jnp.ones_like(gram)
        for k in range(col):
            pivot = pivot - lower[col][k] * lower[col][k]
        smallest = jnp.minimum(smallest, pivot)
        inv_root = lax.rsqrt(pivot)
        inv_pivot.append(inv_root)
        for row in range(col + 1, count):
            value = lane(row, col) * scale[row] * scale[col]
            for k in range(col):
                value = value - lower[row][k] * lower[col][k]
            lower[row][col] = value * inv_root
        right = ratio[col] if col % 2 == 0 else -ratio[col]
        for k in range(col):
            right = right - lower[col][k] * solved[k]
        solved.append(right * inv_root)
    squares = solved[0] * solved[0]
    for j in range(1, count):
        squares = squares + solved[j] * solved[j]
    rel = lax.rsqrt(squares)
    back = [None] * count
    for j in reversed(range(count)):
        value = solved[j]
        for k in range(j + 1, count):
            value = value - lower[k][j] * back[k]
        back[j] = value * inv_pivot[j]
    inv_squares = 1.0 / squares
    residual = [ratio[j] * back[j] * inv_squares for j in range(count)]
    coeffs = [None] * ITERS
    coeffs[ITERS - 1] = -residual[ITERS]
    for j in reversed(range(1, ITERS)):
        coeffs[j - 1] = -residual[j] - coeffs[j]
    lanes = lax.broadcasted_iota(jnp.int32, gram.shape, 1)
    good = (smallest > PIVOT_FLOOR) & (rel > RESIDUAL_FLOOR) & (rel < 2.0)
    for j in range(count):
        good = good & (diag[j] > 1e-30) & (diag[j] < 1e36)
    worst = jnp.min(jnp.where(good, 1.0, 0.0))
    fine_ref[0] = jnp.where(worst > 0.5, 1, 0).astype(jnp.int32)
    rel_ref[...] = jnp.transpose(rel)[0:1, :]
    width = base_refs[0].shape[-1]
    wide = [
        jnp.concatenate([value, value], axis=1)[:, :width] for value in coeffs
    ]
    results = []
    for cell in range(CELLS):
        total = wide[0] * base_refs[0][cell]
        for j in range(1, ITERS):
            total = total + wide[j] * base_refs[j][cell]
        stacked, high = stack_halves(total)
        results.append(row_times(stacked, high, inv_high_ref[cell], inv_low_ref[cell]))
    for slot in range(CELLS):
        value = results[0]
        for cell in range(1, CELLS):
            value = jnp.where(slot_ref[cell] == slot, results[cell], value)
        adjoint_ref[:, slot, :] = value


def vmem(count):
    return [pl.BlockSpec(memory_space=pltpu.VMEM)] * count


def smem(count):
    return [pl.BlockSpec(memory_space=pltpu.SMEM)] * count


PARAMS = pltpu.CompilerParams(vmem_limit_bytes=VMEM_LIMIT)


def struct(*shape, kind=F32):
    return jax.ShapeDtypeStruct(shape, kind)


def spread_kernel(parts_ref, copies_ref):
    total = sum_parts(parts_ref)
    for place in range(copies_ref.shape[0]):
        copies_ref[place] = total


def sum_parts(parts_ref):
    total = parts_ref[0]
    for place in range(1, parts_ref.shape[0]):
        total = total + parts_ref[place]
    return total


def near_size():
    dom_count = lax.axis_size("dom")
    return 4 if dom_count % 4 == 0 else dom_count


def sum_devices(copies):
    dom_count, blk_count = (lax.axis_size("dom"), lax.axis_size("blk"))
    inner = near_size()
    size = inner * blk_count
    near = [
        [first + k for k in range(size)] for first in range(0, dom_count * blk_count, size)
    ]
    far = [[first + k for k in range(0, dom_count, inner)] for first in range(inner)]
    parts = lax.all_to_all(copies, ("dom", "blk"), 0, 0, axis_index_groups=near)
    copies = pl.pallas_call(
        spread_kernel,
        out_shape=struct(dom_count // inner, *copies.shape[1:]),
        in_specs=vmem(1),
        out_specs=vmem(1)[0],
        compiler_params=PARAMS,
        name="sum_near",
    )(parts)
    return lax.all_to_all(copies, "dom", 0, 0, axis_index_groups=far)


def rotated(value, axis, steps):
    count = lax.axis_size(axis)
    return lax.ppermute(
        value, axis, [(source, (source + steps) % count) for source in range(count)]
    )


def both_ways(to_prev, to_next, axis):
    return rotated(to_next, axis, 1), rotated(to_prev, axis, -1)


def shards(adjoint_source, diag_blocks, face_blocks, neighbors, partner, flags):
    nrhs, elements, width = adjoint_source.shape
    block = (width, width)
    tall = padded(width)
    field = struct(CELLS, nrhs, width)
    ring = struct(8, nrhs, width)
    blk_edge = struct(7 * nrhs, 128)
    dom_edge = struct(8 * nrhs, 128)
    turn_edge = struct(3 * nrhs, 128)
    with_blocks = lambda edge: struct(3 * tall + edge.shape[0], 128)
    cost = lambda flops, data: pl.CostEstimate(
        flops=flops, bytes_accessed=data, transcendentals=0
    )
    products = 2 * nrhs * width * width * 3
    outs = pl.pallas_call(
        functools.partial(
            setup_kernel, dom_count=lax.axis_size("dom"), blk_count=lax.axis_size("blk")
        ),
        out_shape=(
            struct(BLOCKS, *block, kind=BF16), struct(BLOCKS, *block, kind=BF16),
            struct(CELLS, *block, kind=BF16), struct(CELLS, *block, kind=BF16),
            field, field, ring, with_blocks(blk_edge), with_blocks(blk_edge),
            with_blocks(dom_edge), struct(3 * tall, 128),
            struct(CELLS, kind=jnp.int32),
        ),
        in_specs=smem(2) + vmem(1) + [pl.BlockSpec(memory_space=pl.ANY)] * 2,
        out_specs=tuple(vmem(11) + smem(1)),
        scratch_shapes=[
            pltpu.VMEM((CELLS,) + block, F32),
            pltpu.VMEM((CELLS,) + block, F32),
            pltpu.VMEM((CELLS,) + block, BF16),
            pltpu.VMEM((CELLS,) + block, BF16),
            pltpu.VMEM((BLOCKS,) + block, F32),
            pltpu.VMEM((CELLS, 6) + block, F32),
            pltpu.SMEM((CELLS,), jnp.int32),
            pltpu.SMEM((CELLS * 4,), jnp.int32),
            pltpu.SemaphoreType.DMA((CELLS,)),
            pltpu.SemaphoreType.DMA((CELLS, 6)),
        ],
        compiler_params=PARAMS,
        name="setup_blocks",
    )(
        neighbors, flags, adjoint_source,
        jnp.transpose(diag_blocks, (1, 0, 2)), jnp.transpose(face_blocks, (1, 2, 0, 3)),
    )
    high, low, inv_high, inv_low, base, local, outward = outs[:7]
    blk_sends = outs[7:9]
    dom_send, dom_blocks = outs[9:11]
    slots = outs[11]
    bases = [base]
    gram = None
    inward = ()
    for pair in range(ITERS // 2):
        first_pair = pair == 0
        last_pair = pair == ITERS // 2 - 1
        first = 3 * tall if first_pair else 0
        from_blk = both_ways(*blk_sends, "blk")
        from_dom_next = rotated(dom_send, "dom", -1)
        if first_pair:
            inward = (rotated(dom_blocks, "dom", 1),)
        sums, dom_send = pl.pallas_call(
            functools.partial(middle_kernel, first),
            out_shape=(field, dom_edge),
            in_specs=vmem(4),
            out_specs=tuple(vmem(2)),
            compiler_params=PARAMS,
            name=f"middle_part_{pair}",
        )(local, outward, *from_blk)
        from_dom_prev = rotated(dom_send, "dom", 1)
        turns = pl.pallas_call(
            functools.partial(relay_kernel, first, width - 128),
            out_shape=(turn_edge, turn_edge),
            in_specs=vmem(2),
            out_specs=tuple(vmem(2)),
            compiler_params=PARAMS,
            name=f"relay_part_{pair}",
        )(sums, from_dom_next)
        turns = both_ways(*turns, "blk")
        given = [sums, outward, *from_blk, from_dom_prev, from_dom_next, high, low, *inward]
        shapes = (field, field)
        if first_pair:
            shapes += (struct(8, *block, kind=BF16), struct(8, *block, kind=BF16))
        odd, part, *made = pl.pallas_call(
            functools.partial(odd_kernel, first_pair),
            out_shape=shapes,
            in_specs=vmem(len(given)),
            out_specs=tuple(vmem(len(shapes))),
            compiler_params=PARAMS,
            cost_estimate=cost(20 * products, 6000000),
            name=f"odd_part_{pair}",
        )(*given)
        if first_pair:
            inward = made
        bases.append(odd)
        newest = len(bases) - 1
        given = bases + ([gram] if newest > 1 else [])
        gram = pl.pallas_call(
            functools.partial(gram_kernel, newest),
            out_shape=struct(nrhs, 128),
            in_specs=vmem(len(given)),
            out_specs=vmem(1)[0],
            compiler_params=PARAMS,
            cost_estimate=cost(100000 * (newest + 1), 2000000),
            name=f"gram_part_{pair}",
        )(*given)
        given = [part, *turns, *inward]
        if last_pair:
            given += [*bases, gram]
            shapes = (struct(near_size() * lax.axis_size("blk"), nrhs // 2, 128), field)
        else:
            given += [high, low]
            shapes = (field, field, ring, blk_edge, blk_edge, dom_edge)
        outs = pl.pallas_call(
            functools.partial(even_kernel, last_pair, len(bases)),
            out_shape=shapes,
            in_specs=vmem(len(given)),
            out_specs=tuple(vmem(len(shapes))),
            compiler_params=PARAMS,
            cost_estimate=cost(24 * products, 6000000),
            name=f"even_part_{pair}",
        )(*given)
        if last_pair:
            gram = outs[0]
        else:
            bases.append(outs[0])
            local, outward = outs[1:3]
            blk_sends = outs[3:5]
            dom_send = outs[5]
    gram = sum_devices(gram)
    given = [gram] + bases + [inv_high, inv_low, slots]
    adjoint, rel, fine = pl.pallas_call(
        finish_kernel,
        out_shape=(
            struct(nrhs, elements, width), struct(1, nrhs), struct(1, kind=jnp.int32)
        ),
        in_specs=vmem(len(given) - 1) + smem(1),
        out_specs=tuple(vmem(2) + smem(1)),
        compiler_params=PARAMS,
        name="finish_part",
    )(*given)
    return lax.cond(
        fine[0] == 1,
        lambda given: (adjoint, rel.reshape(nrhs)),
        lambda given: direct_path(*given),
        (adjoint_source, diag_blocks, face_blocks, neighbors, partner, flags),
    )


def solution(mesh):
    in_specs = (
        P(None, ("dom", "blk"), None),
        P(("dom", "blk"), None, None),
        P(("dom", "blk"), None, None, None),
        P(("dom", "blk"), None),
        P(("dom", "blk"), None),
        P(("dom", "blk"), None),
    )
    out_specs = (P(None, ("dom", "blk"), None), P())
    return jax.shard_map(shards, mesh=mesh, in_specs=in_specs, out_specs=out_specs, check_vma=False)
```

```python
import functools

import jax
import jax.numpy as jnp
from jax import lax
from jax.experimental import pallas as pl
from jax.experimental.pallas import tpu as pltpu
from jax.sharding import PartitionSpec as P

EX = 2
EY = 2
ITERS = 8
SWEEPS = 3


HIGH = lax.Precision.HIGHEST


def shifted(value, axis, steps):
    count = lax.axis_size(axis)
    leading, last = (max(0, -steps), min(count, count - steps))
    return lax.ppermute(value, axis, [(source, source + steps) for source in range(leading, last)])


def invert_blocks(center):
    width = center.shape[-1]
    identity = jnp.eye(width, dtype=center.dtype)
    pivots = jnp.diagonal(center, axis1=1, axis2=2)
    estimate = identity[None, :, :] / pivots[:, :, None]
    for sweep_index in range(SWEEPS):
        product = jnp.einsum("eab,ebc->eac", center, estimate, precision=HIGH)
        estimate = 2.0 * estimate - jnp.einsum("eab,ebc->eac", estimate, product, precision=HIGH)
    return estimate


def least_squares(hessen, start_norm):
    count = len(hessen)
    cosines = []
    sines = []
    rotated_rhs = [start_norm] + [jnp.zeros_like(start_norm) for row_index in range(count)]
    upper = []
    for col_index in range(count):
        column = [hessen[col_index][row_index] for row_index in range(col_index + 2)]
        for row_index in range(col_index):
            rotated = (
                cosines[row_index] * column[row_index] + sines[row_index] * column[row_index + 1]
            )
            column[row_index + 1] = (
                -sines[row_index] * column[row_index] + cosines[row_index] * column[row_index + 1]
            )
            column[row_index] = rotated
        radius = jnp.sqrt(
            column[col_index] * column[col_index] + column[col_index + 1] * column[col_index + 1]
        )
        cosine = column[col_index] / radius
        sine_value = column[col_index + 1] / radius
        column[col_index] = radius
        cosines.append(cosine)
        sines.append(sine_value)
        rotated_rhs[col_index + 1] = -sine_value * rotated_rhs[col_index]
        rotated_rhs[col_index] = cosine * rotated_rhs[col_index]
        upper.append(column[: col_index + 1])
    coeffs = [None] * count
    for row_index in reversed(range(count)):
        total = rotated_rhs[row_index]
        for col_index in range(row_index + 1, count):
            total = total - upper[col_index][row_index] * coeffs[col_index]
        coeffs[row_index] = total / upper[row_index][row_index]
    return (coeffs, jnp.abs(rotated_rhs[count]) / start_norm)


def move_vectors_dom(vectors, offset):
    return shifted(vectors, "dom", offset)


def move_vectors_blk(vectors, offset):
    return shifted(vectors, "blk", offset)


def move_facing_dom(blocks, offset):
    return shifted(blocks, "dom", offset)


def move_facing_blk(blocks, offset):
    return shifted(blocks, "blk", offset)


def direct_path(adjoint_source, diag_blocks, face_blocks, neighbors, partner, flags):
    nrhs, elements, width = adjoint_source.shape
    blk_count = lax.axis_size("blk")
    dom_here = lax.axis_index("dom")
    blk_here = lax.axis_index("blk")
    wall_mask = (flags == 1).astype(jnp.float32)
    center = diag_blocks + jnp.einsum("ef,efab->eab", wall_mask, face_blocks, precision=HIGH)
    inverse = invert_blocks(center)
    inside = neighbors >= 0
    source_elem = jnp.where(inside, neighbors, 0)
    source_face = jnp.where(inside, partner, 0)
    owner_dev = source_elem // elements
    owner_dom = owner_dev // blk_count
    owner_blk = owner_dev % blk_count
    direction = jnp.where(
        owner_dom == dom_here - 1,
        1,
        jnp.where(
            owner_dom == dom_here + 1,
            2,
            jnp.where(owner_blk == blk_here - 1, 3, jnp.where(owner_blk == blk_here + 1, 4, 0)),
        ),
    )
    direction = jnp.where(inside, direction, 0).astype(jnp.int32)
    local_slot = source_elem % elements
    flat_direction = direction.reshape(-1)
    flat_inside = inside.reshape(-1)
    flat_local = (local_slot * 6 + source_face).reshape(-1)
    face_keys = (source_elem * 6 + source_face).reshape(-1)
    same_way = (flat_direction[None, :] == flat_direction[:, None]) & flat_inside[None, :]
    placing = jnp.sum(
        (same_way & (face_keys[None, :] < face_keys[:, None])).astype(jnp.int32), axis=1
    )
    offsets = jnp.array(
        [0, 6 * elements, 6 * elements + EY, 6 * elements + 2 * EY, 6 * elements + 2 * EY + EX],
        jnp.int32,
    )
    candidate = jnp.where(flat_direction == 0, flat_local, offsets[flat_direction] + placing)
    slot_range = jnp.arange(elements * 6, dtype=jnp.int32)

    def pick_rows(target, count):
        marked = ((flat_direction == target) & flat_inside).astype(jnp.int32)
        ranking = jnp.cumsum(marked) - marked
        chooser = (ranking[None, :] == jnp.arange(count)[:, None]) & (marked[None, :] > 0)
        return jnp.sum(jnp.where(chooser, slot_range[None, :], 0), axis=1)

    toward_next_dom = pick_rows(2, EY)
    toward_prev_dom = pick_rows(1, EY)
    toward_next_blk = pick_rows(4, EX)
    toward_prev_blk = pick_rows(3, EX)
    flat_blocks = face_blocks.reshape(elements * 6, width, width)
    block_pool = jnp.concatenate(
        [
            flat_blocks,
            move_facing_dom(jnp.take(flat_blocks, toward_next_dom, axis=0), 1),
            move_facing_dom(jnp.take(flat_blocks, toward_prev_dom, axis=0), -1),
            move_facing_blk(jnp.take(flat_blocks, toward_next_blk, axis=0), 1),
            move_facing_blk(jnp.take(flat_blocks, toward_prev_blk, axis=0), -1),
        ],
        axis=0,
    )
    column_blocks = (
        jnp.take(block_pool, candidate, axis=0) * flat_inside.astype(jnp.float32)[:, None, None]
    )
    column_blocks = column_blocks.reshape(elements, 6, width, width)
    vector_index = (direction * elements + local_slot).reshape(-1)

    def precondition(vectors):
        return jnp.einsum("eab,rea->reb", inverse, vectors, precision=HIGH)

    start_norm = jnp.sqrt(
        lax.psum(jnp.sum(adjoint_source * adjoint_source, axis=(1, 2)), ("dom", "blk"))
    )
    krylov_basis = [adjoint_source / start_norm[:, None, None]]
    hessen = []
    for iteration in range(ITERS):
        operator_vectors = precondition(krylov_basis[-1])
        gathered = jnp.concatenate(
            [
                operator_vectors,
                move_vectors_dom(operator_vectors, 1),
                move_vectors_dom(operator_vectors, -1),
                move_vectors_blk(operator_vectors, 1),
                move_vectors_blk(operator_vectors, -1),
            ],
            axis=1,
        )
        nearby = jnp.take(gathered, vector_index, axis=1).reshape(nrhs, elements, 6, width)
        own_part = jnp.einsum("eab,rea->reb", center, operator_vectors, precision=HIGH)
        mapped = own_part + jnp.einsum("egab,rega->reb", column_blocks, nearby, precision=HIGH)
        local_dots = [jnp.sum(mapped * member, axis=(1, 2)) for member in krylov_basis]
        projections = lax.psum(jnp.stack(local_dots), ("dom", "blk"))
        for row_index in range(len(krylov_basis)):
            mapped = mapped - projections[row_index][:, None, None] * krylov_basis[row_index]
        new_norm = jnp.sqrt(lax.psum(jnp.sum(mapped * mapped, axis=(1, 2)), ("dom", "blk")))
        hessen.append(jnp.concatenate([projections, new_norm[None, :]], axis=0))
        krylov_basis.append(mapped / new_norm[:, None, None])
    coeffs, rel_residual = least_squares(hessen, start_norm)
    combined = coeffs[0][:, None, None] * krylov_basis[0]
    for col_index in range(1, ITERS):
        combined = combined + coeffs[col_index][:, None, None] * krylov_basis[col_index]
    return (precondition(combined), rel_residual)


CELLS = EX * EY
F32 = jnp.float32
BF16 = jnp.bfloat16
VMEM_LIMIT = 40 * 1024 * 1024
OUT_CELLS = ((0, 1), (2, 3), (0, 2), (1, 3))
PIVOT_FLOOR = 0.02
RESIDUAL_FLOOR = 0.02


def pair_lane(row, col):
    return row * (row + 1) // 2 + col


def split_halves(value):
    high = value.astype(BF16)
    low = (value - high.astype(F32)).astype(BF16)
    return high, low


def dot32(left, right):
    return jnp.dot(left, right, preferred_element_type=F32)


def dot_halves(left_high, left_low, right_high, right_low):
    small = dot32(left_low, right_high) + dot32(left_high, right_low)
    return dot32(left_high, right_high) + small


def stack_halves(vector):
    high, low = split_halves(vector)
    return jnp.concatenate([high, low], axis=0), high


def row_times(stacked, high, block_high, block_low):
    rows = high.shape[0]
    both = dot32(stacked, block_high)
    return both[:rows] + both[rows:] + dot32(high, block_low)


FROM_X = CELLS
FROM_Y = 2 * CELLS
OUTWARD = 3 * CELLS
BLOCKS = OUTWARD + 8
RING_TARGETS = (0, 1, 2, 3, 0, 2, 1, 3)


def local_products(halves, high_ref, low_ref):
    results = []
    for cell in range(CELLS):
        total = None
        for source, entry in (
            (cell, cell), (cell ^ 2, FROM_X + (cell ^ 2)), (cell ^ 1, FROM_Y + (cell ^ 1))
        ):
            part = row_times(*halves[source], high_ref[entry], low_ref[entry])
            total = part if total is None else total + part
        results.append(total)
    return results


def outward_products(halves, high_ref, low_ref):
    results = []
    for way in range(4):
        for place in range(2):
            entry = OUTWARD + 2 * way + place
            results.append(
                row_times(*halves[OUT_CELLS[way][place]], high_ref[entry], low_ref[entry])
            )
    return results


def padded(width):
    return (width + 7) // 8 * 8


def tails_of(values):
    rows, width = values[0].shape
    tail = width - 128
    total = None
    for place, value in enumerate(values):
        tile = jnp.concatenate([value[:, 128:], jnp.zeros((rows, 128 - tail), F32)], axis=1)
        tile = tile if place == 0 else pltpu.roll(tile, tail * place, 1)
        total = tile if total is None else total + tile
    return total


def tail_at(tile, tail, place):
    turned = tile if place == 0 else pltpu.roll(tile, 128 - tail * place, 1)
    return turned[:, :tail]


def put_rows(ref, first, values):
    rows = values[0].shape[0]
    for place, value in enumerate(values):
        ref[first + rows * place : first + rows * (place + 1), :] = value[:, :128]
    for part in range(0, len(values), 3):
        start = first + rows * (len(values) + part // 3)
        ref[start : start + rows, :] = tails_of(values[part : part + 3])


def get_rows(ref, first, rows, tail, count, place):
    main = ref[first + rows * place : first + rows * (place + 1), :]
    start = first + rows * (count + place // 3)
    return jnp.concatenate([main, tail_at(ref[start : start + rows, :], tail, place % 3)], axis=1)


def send_along_blk(local, outward, prev_ref, next_ref, first):
    for ref, way, cells in ((prev_ref, 2, (0, 2)), (next_ref, 3, (1, 3))):
        put_rows(
            ref, first,
            [
                outward[2 * way], outward[2 * way + 1], local[cells[0]], local[cells[1]],
                outward[2 + cells[0] % 2],
            ],
        )


def send_to_dom_prev(local, outward, prev_ref, first):
    put_rows(
        prev_ref, first,
        [outward[0], outward[1], local[0], local[1], outward[4], outward[6]],
    )


def setup_kernel(
    nbr_ref, flag_ref, src_ref, diag_hbm_ref, face_hbm_ref,
    high_ref, low_ref, inv_high_ref, inv_low_ref, base_ref, local_ref, outward_ref,
    blk_prev_ref, blk_next_ref, dom_prev_ref, dom_next_ref, slot_ref,
    center_ref, x_ref, d_high_ref, d_low_ref, product_ref, face_ref, cell_ref, face_of_ref, diag_sem, face_sem,
    *, dom_count, blk_count,
):
    width = diag_hbm_ref.shape[0]
    diag_copies = [
        pltpu.make_async_copy(
            diag_hbm_ref.at[:, slot, :], center_ref.at[slot], diag_sem.at[slot]
        )
        for slot in range(CELLS)
    ]
    face_copies = [
        [
            pltpu.make_async_copy(
                face_hbm_ref.at[face, :, slot, :], face_ref.at[slot, face], face_sem.at[slot, face]
            )
            for face in range(6)
        ]
        for slot in range(CELLS)
    ]
    for slot in range(CELLS):
        diag_copies[slot].start()
    for slot in range(CELLS):
        for face in range(6):
            pl.when(flag_ref[slot, face] == 1)(face_copies[slot][face].start)
    for slot in range(CELLS):
        for face in range(6):
            pl.when(nbr_ref[slot, face] >= 0)(face_copies[slot][face].start)
    dom_here = lax.axis_index("dom")
    blk_here = lax.axis_index("blk")
    here = dom_here * blk_count + blk_here
    for slot in range(CELLS):
        up_x = jnp.int32(0)
        down_x = jnp.int32(0)
        up_y = jnp.int32(0)
        down_y = jnp.int32(0)
        for face in range(6):
            other = nbr_ref[slot, face]
            gap = jnp.where(other >= 0, other // CELLS - here, 0)
            up_x = jnp.where(gap == blk_count, 1, up_x)
            down_x = jnp.where(gap == -blk_count, 1, down_x)
            up_y = jnp.where(gap == 1, 1, up_y)
            down_y = jnp.where(gap == -1, 1, down_y)
        cell_x = jnp.where(dom_here < dom_count - 1, up_x, 1 - down_x)
        cell_y = jnp.where(blk_here < blk_count - 1, up_y, 1 - down_y)
        cell = 2 * cell_x + cell_y
        cell_ref[slot] = cell
        slot_ref[cell] = slot
    for entry in range(CELLS * 4):
        face_of_ref[entry] = -1
    for slot in range(CELLS):
        cell = cell_ref[slot]
        for face in range(6):
            other = nbr_ref[slot, face]
            inside = other >= 0
            safe = jnp.where(inside, other, 0)
            gap = safe // CELLS - here
            mate = cell_ref[safe % CELLS]
            change = jnp.bitwise_xor(mate, cell)
            way_x = jnp.where(cell >= 2, 0, 1)
            way_y = jnp.where(cell % 2 == 1, 2, 3)
            way_in = jnp.where(change == 2, way_x, way_y)
            way = jnp.where(
                gap == 0, way_in,
                jnp.where(
                    gap == -blk_count, 0,
                    jnp.where(gap == blk_count, 1, jnp.where(gap == -1, 2, 3)),
                ),
            )

            @pl.when(inside)
            def _():
                face_of_ref[slot * 4 + way] = face

    rows = lax.broadcasted_iota(jnp.int32, (width, width), 0)
    cols = lax.broadcasted_iota(jnp.int32, (width, width), 1)
    on_diag = rows == cols
    for slot in range(CELLS):
        base_ref[cell_ref[slot]] = src_ref[:, slot, :]
        diag_copies[slot].wait()
    for slot in range(CELLS):
        for face in range(6):

            @pl.when(flag_ref[slot, face] == 1)
            def _():
                face_copies[slot][face].wait()
                center_ref[slot] = center_ref[slot] + face_ref[slot, face]

    for slot in range(CELLS):
        center = center_ref[slot]
        marked = jnp.where(on_diag, center, 0.0)
        inv_row = 1.0 / jnp.sum(marked, axis=0, keepdims=True)
        inv_col = 1.0 / jnp.sum(marked, axis=1, keepdims=True)
        defect = jnp.where(on_diag, 0.0, -inv_col * center)
        x_ref[slot] = jnp.where(on_diag, inv_col, defect * inv_row)
        d_high_ref[slot], d_low_ref[slot] = split_halves(defect)
    for sweep in range(1, SWEEPS):
        squares = [
            dot_halves(d_high_ref[slot], d_low_ref[slot], d_high_ref[slot], d_low_ref[slot])
            for slot in range(CELLS)
        ]
        for slot in range(CELLS):
            d_high_ref[slot], d_low_ref[slot] = split_halves(squares[slot])
        for slot in range(CELLS):
            x_high, x_low = split_halves(x_ref[slot])
            x_ref[slot] = x_ref[slot] + dot_halves(
                d_high_ref[slot], d_low_ref[slot], x_high, x_low
            )
    for slot in range(CELLS):
        for face in range(6):
            pl.when(nbr_ref[slot, face] >= 0)(face_copies[slot][face].wait)
    for slot in range(CELLS):
        cell = cell_ref[slot]
        x_high, x_low = split_halves(x_ref[slot])
        inv_high_ref[cell] = x_high
        inv_low_ref[cell] = x_low
        own = -dot_halves(d_high_ref[slot], d_low_ref[slot], d_high_ref[slot], d_low_ref[slot])
        high_ref[cell], low_ref[cell] = split_halves(own)
        for way in range(4):
            face = face_of_ref[slot * 4 + way]
            block = jnp.where(face >= 0, face_ref[slot, jnp.maximum(face, 0)], 0.0)
            f_high, f_low = split_halves(block)
            product = dot_halves(x_high, x_low, f_high, f_low)
            if way < 2:
                leaves = cell // 2 == way
                inner = FROM_X + cell
                place = cell % 2
            else:
                leaves = cell % 2 == way - 2
                inner = FROM_Y + cell
                place = cell // 2
            entry = jnp.where(leaves, OUTWARD + 2 * way + place, inner)
            high_ref[entry], low_ref[entry] = split_halves(product)
            product_ref[entry] = product
    tall = padded(width)
    for way, ref in enumerate((dom_prev_ref, dom_next_ref, blk_prev_ref, blk_next_ref)):
        pair = [product_ref[OUTWARD + 2 * way + place] for place in range(2)]
        for place in range(2):
            ref[tall * place : tall * place + width, :] = pair[place][:, :128]
        ref[2 * tall : 2 * tall + width, :] = tails_of(pair)
    halves = [stack_halves(base_ref[cell]) for cell in range(CELLS)]
    local = local_products(halves, high_ref, low_ref)
    outward = outward_products(halves, high_ref, low_ref)
    for cell in range(CELLS):
        local_ref[cell] = local[cell]
    for entry in range(8):
        outward_ref[entry] = outward[entry]
    send_along_blk(local, outward, blk_prev_ref, blk_next_ref, 3 * tall)
    send_to_dom_prev(local, outward, dom_prev_ref, 3 * tall)


FROM_BLK = 5
FROM_DOM = 6
RELAYED = 2


def middle_kernel(first, local_ref, outward_ref, next_ref, prev_ref, sum_ref, dom_next_ref):
    rows = local_ref.shape[1]
    tail = local_ref.shape[2] - 128

    def got(ref, place):
        return get_rows(ref, first, rows, tail, FROM_BLK, place)

    sums = []
    for cell in range(CELLS):
        given = prev_ref if cell % 2 == 0 else next_ref
        sums.append(local_ref[cell] + got(given, cell // 2))
        sum_ref[cell] = sums[cell]
    put_rows(
        dom_next_ref, 0,
        [outward_ref[2], outward_ref[3], sums[2], sums[3], got(prev_ref, 4), got(next_ref, 4)],
    )


def relay_kernel(first, tail, sum_ref, dom_ref, prev_ref, next_ref):
    rows = sum_ref.shape[1]

    def got(place):
        return get_rows(dom_ref, first, rows, tail, FROM_DOM, place)

    put_rows(prev_ref, 0, [got(4), got(0)])
    put_rows(next_ref, 0, [got(5), got(1)])


def odd_kernel(first_pair, *refs):
    sum_ref, outward_ref, blk_next_ref, blk_prev_ref, dom_prev_ref, dom_next_ref = refs[:6]
    high_ref, low_ref = refs[6:8]
    rows = sum_ref.shape[1]
    width = sum_ref.shape[2]
    tail = width - 128
    first = 0
    if first_pair:
        tall = padded(width)
        first = 3 * tall
        dom_blocks_ref = refs[8]
        odd_ref, even_ref, in_high_ref, in_low_ref = refs[9:]
        for way, ref in enumerate((dom_blocks_ref, dom_next_ref, blk_prev_ref, blk_next_ref)):
            for place in range(2):
                main = ref[tall * place : tall * place + width, :]
                rest = tail_at(ref[2 * tall : 2 * tall + width, :], tail, place)
                high, low = split_halves(jnp.concatenate([main, rest], axis=1))
                in_high_ref[2 * way + place] = high
                in_low_ref[2 * way + place] = low
    else:
        in_high_ref, in_low_ref, odd_ref, even_ref = refs[8:]

    def from_blk(ref, place):
        return get_rows(ref, first, rows, tail, FROM_BLK, place)

    def from_dom_prev(place):
        return get_rows(dom_prev_ref, 0, rows, tail, FROM_DOM, place)

    def from_dom_next(place):
        return get_rows(dom_next_ref, first, rows, tail, FROM_DOM, place)

    odd = [
        sum_ref[cell] + (from_dom_prev if cell < 2 else from_dom_next)(cell % 2)
        for cell in range(CELLS)
    ]
    ring = [
        from_dom_prev(2) + outward_ref[0],
        from_dom_prev(3) + outward_ref[1],
        from_dom_next(2) + outward_ref[2],
        from_dom_next(3) + outward_ref[3],
        from_blk(blk_prev_ref, 2) + outward_ref[4] + from_dom_prev(4),
        from_blk(blk_prev_ref, 3) + outward_ref[5],
        from_blk(blk_next_ref, 2) + outward_ref[6] + from_dom_prev(5),
        from_blk(blk_next_ref, 3) + outward_ref[7],
    ]
    even = local_products([stack_halves(value) for value in odd], high_ref, low_ref)
    for place, value in enumerate(ring):
        cell = RING_TARGETS[place]
        even[cell] = even[cell] + row_times(
            *stack_halves(value), in_high_ref[place], in_low_ref[place]
        )
    for cell in range(CELLS):
        odd_ref[cell] = odd[cell]
        even_ref[cell] = even[cell]


TURNED = ((2, 0, 0), (3, 1, 0), (5, 0, 1), (7, 1, 1))


def even_kernel(last_pair, older_count, *refs):
    part_ref, turn_next_ref, turn_prev_ref, in_high_ref, in_low_ref = refs[:5]
    refs = refs[5:]
    rows = part_ref.shape[1]
    tail = part_ref.shape[2] - 128
    even = [part_ref[cell] for cell in range(CELLS)]
    for place, side, item in TURNED:
        value = get_rows((turn_prev_ref, turn_next_ref)[side], 0, rows, tail, RELAYED, item)
        cell = RING_TARGETS[place]
        even[cell] = even[cell] + row_times(
            *stack_halves(value), in_high_ref[place], in_low_ref[place]
        )
    if last_pair:
        older = refs[:older_count]
        gram_in_ref, gram_ref, even_ref = refs[older_count:]
    else:
        high_ref, low_ref = refs[:2]
        even_ref, local_out_ref, outward_out_ref, prev_ref, next_ref, dom_out_ref = refs[2:]
    for cell in range(CELLS):
        even_ref[cell] = even[cell]
    if last_pair:
        gram = gram_rows(ITERS, list(older) + [even_ref], gram_in_ref[...])
        half = gram.shape[0] // 2
        gram = gram[:half] + pltpu.roll(gram[half:], 64, 1)
        for place in range(gram_ref.shape[0]):
            gram_ref[place] = gram
    else:
        halves = [stack_halves(value) for value in even]
        local = local_products(halves, high_ref, low_ref)
        outward = outward_products(halves, high_ref, low_ref)
        for cell in range(CELLS):
            local_out_ref[cell] = local[cell]
        for entry in range(8):
            outward_out_ref[entry] = outward[entry]
        send_along_blk(local, outward, prev_ref, next_ref, 0)
        send_to_dom_prev(local, outward, dom_out_ref, 0)


def gram_kernel(newest, *refs):
    base_refs = refs[: newest + 1]
    gram = None if newest == 1 else refs[newest + 1][...]
    gram = gram_rows(newest - 1, base_refs, gram)
    refs[-1][...] = gram_rows(newest, base_refs, gram)


def gram_rows(step, base_refs, gram):
    newest = base_refs[step]
    nrhs = newest.shape[1]
    lanes = lax.broadcasted_iota(jnp.int32, (nrhs, 128), 1)
    if gram is None:
        gram = jnp.zeros((nrhs, 128), F32)
    for col in range(step + 1):
        total = newest[0] * base_refs[col][0]
        for cell in range(1, CELLS):
            total = total + newest[cell] * base_refs[col][cell]
        value = jnp.sum(total, axis=1, keepdims=True)
        gram = jnp.where(lanes == pair_lane(step, col), value, gram)
    return gram


def finish_kernel(*refs):
    gram_ref = refs[0]
    base_refs = refs[1 : 1 + ITERS]
    inv_high_ref, inv_low_ref, slot_ref, adjoint_ref, rel_ref, fine_ref = refs[1 + ITERS :]
    count = ITERS + 1
    packed = sum_parts(gram_ref)
    gram = jnp.concatenate([packed, pltpu.roll(packed, 64, 1)], axis=0)

    def lane(row, col):
        place = pair_lane(row, col)
        return jnp.broadcast_to(gram[:, place : place + 1], gram.shape)

    diag = [lane(j, j) for j in range(count)]
    scale = [lax.rsqrt(value) for value in diag]
    start = diag[0] * scale[0]
    lower = [[None] * count for j in range(count)]
    solved = []
    ratio = [scale[j] * start for j in range(count)]
    smallest = jnp.ones_like(gram)
    inv_pivot = []
    for col in range(count):
        pivot = jnp.ones_like(gram)
        for k in range(col):
            pivot = pivot - lower[col][k] * lower[col][k]
        smallest = jnp.minimum(smallest, pivot)
        inv_root = lax.rsqrt(pivot)
        inv_pivot.append(inv_root)
        for row in range(col + 1, count):
            value = lane(row, col) * scale[row] * scale[col]
            for k in range(col):
                value = value - lower[row][k] * lower[col][k]
            lower[row][col] = value * inv_root
        right = ratio[col] if col % 2 == 0 else -ratio[col]
        for k in range(col):
            right = right - lower[col][k] * solved[k]
        solved.append(right * inv_root)
    squares = solved[0] * solved[0]
    for j in range(1, count):
        squares = squares + solved[j] * solved[j]
    rel = lax.rsqrt(squares)
    back = [None] * count
    for j in reversed(range(count)):
        value = solved[j]
        for k in range(j + 1, count):
            value = value - lower[k][j] * back[k]
        back[j] = value * inv_pivot[j]
    inv_squares = 1.0 / squares
    residual = [ratio[j] * back[j] * inv_squares for j in range(count)]
    coeffs = [None] * ITERS
    coeffs[ITERS - 1] = -residual[ITERS]
    for j in reversed(range(1, ITERS)):
        coeffs[j - 1] = -residual[j] - coeffs[j]
    lanes = lax.broadcasted_iota(jnp.int32, gram.shape, 1)
    good = (smallest > PIVOT_FLOOR) & (rel > RESIDUAL_FLOOR) & (rel < 2.0)
    for j in range(count):
        good = good & (diag[j] > 1e-30) & (diag[j] < 1e36)
    worst = jnp.min(jnp.where(good, 1.0, 0.0))
    fine_ref[0] = jnp.where(worst > 0.5, 1, 0).astype(jnp.int32)
    rel_ref[...] = jnp.transpose(rel)[0:1, :]
    width = base_refs[0].shape[-1]
    wide = [
        jnp.concatenate([value, value], axis=1)[:, :width] for value in coeffs
    ]
    results = []
    for cell in range(CELLS):
        total = wide[0] * base_refs[0][cell]
        for j in range(1, ITERS):
            total = total + wide[j] * base_refs[j][cell]
        stacked, high = stack_halves(total)
        results.append(row_times(stacked, high, inv_high_ref[cell], inv_low_ref[cell]))
    for slot in range(CELLS):
        value = results[0]
        for cell in range(1, CELLS):
            value = jnp.where(slot_ref[cell] == slot, results[cell], value)
        adjoint_ref[:, slot, :] = value


def vmem(count):
    return [pl.BlockSpec(memory_space=pltpu.VMEM)] * count


def smem(count):
    return [pl.BlockSpec(memory_space=pltpu.SMEM)] * count


PARAMS = pltpu.CompilerParams(vmem_limit_bytes=VMEM_LIMIT)


def struct(*shape, kind=F32):
    return jax.ShapeDtypeStruct(shape, kind)


def spread_kernel(parts_ref, copies_ref):
    total = sum_parts(parts_ref)
    for place in range(copies_ref.shape[0]):
        copies_ref[place] = total


def sum_parts(parts_ref):
    total = parts_ref[0]
    for place in range(1, parts_ref.shape[0]):
        total = total + parts_ref[place]
    return total


def near_size():
    dom_count = lax.axis_size("dom")
    return 4 if dom_count % 4 == 0 else dom_count


def sum_devices(copies):
    dom_count, blk_count = (lax.axis_size("dom"), lax.axis_size("blk"))
    inner = near_size()
    size = inner * blk_count
    near = [
        [first + k for k in range(size)] for first in range(0, dom_count * blk_count, size)
    ]
    far = [[first + k for k in range(0, dom_count, inner)] for first in range(inner)]
    parts = lax.all_to_all(copies, ("dom", "blk"), 0, 0, axis_index_groups=near)
    copies = pl.pallas_call(
        spread_kernel,
        out_shape=struct(dom_count // inner, *copies.shape[1:]),
        in_specs=vmem(1),
        out_specs=vmem(1)[0],
        compiler_params=PARAMS,
        name="sum_near",
    )(parts)
    return lax.all_to_all(copies, "dom", 0, 0, axis_index_groups=far)


def rotated(value, axis, steps):
    count = lax.axis_size(axis)
    return lax.ppermute(
        value, axis, [(source, (source + steps) % count) for source in range(count)]
    )


def both_ways(to_prev, to_next, axis):
    from_next = rotated(to_prev, axis, -1)
    from_prev = rotated(to_next, axis, 1)
    return from_next, from_prev


def shards(adjoint_source, diag_blocks, face_blocks, neighbors, partner, flags):
    nrhs, elements, width = adjoint_source.shape
    block = (width, width)
    tall = padded(width)
    field = struct(CELLS, nrhs, width)
    ring = struct(8, nrhs, width)
    blk_edge = struct(7 * nrhs, 128)
    dom_edge = struct(8 * nrhs, 128)
    turn_edge = struct(3 * nrhs, 128)
    with_blocks = lambda edge: struct(3 * tall + edge.shape[0], 128)
    cost = lambda flops, data: pl.CostEstimate(
        flops=flops, bytes_accessed=data, transcendentals=0
    )
    products = 2 * nrhs * width * width * 3
    outs = pl.pallas_call(
        functools.partial(
            setup_kernel, dom_count=lax.axis_size("dom"), blk_count=lax.axis_size("blk")
        ),
        out_shape=(
            struct(BLOCKS, *block, kind=BF16), struct(BLOCKS, *block, kind=BF16),
            struct(CELLS, *block, kind=BF16), struct(CELLS, *block, kind=BF16),
            field, field, ring, with_blocks(blk_edge), with_blocks(blk_edge),
            with_blocks(dom_edge), struct(3 * tall, 128),
            struct(CELLS, kind=jnp.int32),
        ),
        in_specs=smem(2) + vmem(1) + [pl.BlockSpec(memory_space=pl.ANY)] * 2,
        out_specs=tuple(vmem(11) + smem(1)),
        scratch_shapes=[
            pltpu.VMEM((CELLS,) + block, F32),
            pltpu.VMEM((CELLS,) + block, F32),
            pltpu.VMEM((CELLS,) + block, BF16),
            pltpu.VMEM((CELLS,) + block, BF16),
            pltpu.VMEM((BLOCKS,) + block, F32),
            pltpu.VMEM((CELLS, 6) + block, F32),
            pltpu.SMEM((CELLS,), jnp.int32),
            pltpu.SMEM((CELLS * 4,), jnp.int32),
            pltpu.SemaphoreType.DMA((CELLS,)),
            pltpu.SemaphoreType.DMA((CELLS, 6)),
        ],
        compiler_params=PARAMS,
        name="setup_blocks",
    )(
        neighbors, flags, adjoint_source,
        jnp.transpose(diag_blocks, (1, 0, 2)), jnp.transpose(face_blocks, (1, 2, 0, 3)),
    )
    high, low, inv_high, inv_low, base, local, outward = outs[:7]
    blk_sends = outs[7:9]
    dom_send, dom_blocks = outs[9:11]
    slots = outs[11]
    bases = [base]
    gram = None
    inward = ()
    for pair in range(ITERS // 2):
        first_pair = pair == 0
        last_pair = pair == ITERS // 2 - 1
        first = 3 * tall if first_pair else 0
        from_blk = both_ways(*blk_sends, "blk")
        from_dom_next = rotated(dom_send, "dom", -1)
        if first_pair:
            inward = (rotated(dom_blocks, "dom", 1),)
        sums, dom_send = pl.pallas_call(
            functools.partial(middle_kernel, first),
            out_shape=(field, dom_edge),
            in_specs=vmem(4),
            out_specs=tuple(vmem(2)),
            compiler_params=PARAMS,
            name=f"middle_part_{pair}",
        )(local, outward, *from_blk)
        from_dom_prev = rotated(dom_send, "dom", 1)
        turns = pl.pallas_call(
            functools.partial(relay_kernel, first, width - 128),
            out_shape=(turn_edge, turn_edge),
            in_specs=vmem(2),
            out_specs=tuple(vmem(2)),
            compiler_params=PARAMS,
            name=f"relay_part_{pair}",
        )(sums, from_dom_next)
        turns = both_ways(*turns, "blk")
        given = [sums, outward, *from_blk, from_dom_prev, from_dom_next, high, low, *inward]
        shapes = (field, field)
        if first_pair:
            shapes += (struct(8, *block, kind=BF16), struct(8, *block, kind=BF16))
        odd, part, *made = pl.pallas_call(
            functools.partial(odd_kernel, first_pair),
            out_shape=shapes,
            in_specs=vmem(len(given)),
            out_specs=tuple(vmem(len(shapes))),
            compiler_params=PARAMS,
            cost_estimate=cost(20 * products, 6000000),
            name=f"odd_part_{pair}",
        )(*given)
        if first_pair:
            inward = made
        bases.append(odd)
        newest = len(bases) - 1
        given = bases + ([gram] if newest > 1 else [])
        gram = pl.pallas_call(
            functools.partial(gram_kernel, newest),
            out_shape=struct(nrhs, 128),
            in_specs=vmem(len(given)),
            out_specs=vmem(1)[0],
            compiler_params=PARAMS,
            cost_estimate=cost(100000 * (newest + 1), 2000000),
            name=f"gram_part_{pair}",
        )(*given)
        given = [part, *turns, *inward]
        if last_pair:
            given += [*bases, gram]
            shapes = (struct(near_size() * lax.axis_size("blk"), nrhs // 2, 128), field)
        else:
            given += [high, low]
            shapes = (field, field, ring, blk_edge, blk_edge, dom_edge)
        outs = pl.pallas_call(
            functools.partial(even_kernel, last_pair, len(bases)),
            out_shape=shapes,
            in_specs=vmem(len(given)),
            out_specs=tuple(vmem(len(shapes))),
            compiler_params=PARAMS,
            cost_estimate=cost(24 * products, 6000000),
            name=f"even_part_{pair}",
        )(*given)
        if last_pair:
            gram = outs[0]
        else:
            bases.append(outs[0])
            local, outward = outs[1:3]
            blk_sends = outs[3:5]
            dom_send = outs[5]
    gram = sum_devices(gram)
    given = [gram] + bases + [inv_high, inv_low, slots]
    adjoint, rel, fine = pl.pallas_call(
        finish_kernel,
        out_shape=(
            struct(nrhs, elements, width), struct(1, nrhs), struct(1, kind=jnp.int32)
        ),
        in_specs=vmem(len(given) - 1) + smem(1),
        out_specs=tuple(vmem(2) + smem(1)),
        compiler_params=PARAMS,
        name="finish_part",
    )(*given)
    return lax.cond(
        fine[0] == 1,
        lambda given: (adjoint, rel.reshape(nrhs)),
        lambda given: direct_path(*given),
        (adjoint_source, diag_blocks, face_blocks, neighbors, partner, flags),
    )


def solution(mesh):
    in_specs = (
        P(None, ("dom", "blk"), None),
        P(("dom", "blk"), None, None),
        P(("dom", "blk"), None, None, None),
        P(("dom", "blk"), None),
        P(("dom", "blk"), None),
        P(("dom", "blk"), None),
    )
    out_specs = (P(None, ("dom", "blk"), None), P())
    return jax.shard_map(shards, mesh=mesh, in_specs=in_specs, out_specs=out_specs, check_vma=False)
```

```python
import functools

import jax
import jax.numpy as jnp
from jax import lax
from jax.experimental import pallas as pl
from jax.experimental.pallas import tpu as pltpu
from jax.sharding import PartitionSpec as P

EX = 2
EY = 2
ITERS = 8
SWEEPS = 3


HIGH = lax.Precision.HIGHEST


def shifted(value, axis, steps):
    count = lax.axis_size(axis)
    leading, last = (max(0, -steps), min(count, count - steps))
    return lax.ppermute(value, axis, [(source, source + steps) for source in range(leading, last)])


def invert_blocks(center):
    width = center.shape[-1]
    identity = jnp.eye(width, dtype=center.dtype)
    pivots = jnp.diagonal(center, axis1=1, axis2=2)
    estimate = identity[None, :, :] / pivots[:, :, None]
    for sweep_index in range(SWEEPS):
        product = jnp.einsum("eab,ebc->eac", center, estimate, precision=HIGH)
        estimate = 2.0 * estimate - jnp.einsum("eab,ebc->eac", estimate, product, precision=HIGH)
    return estimate


def least_squares(hessen, start_norm):
    count = len(hessen)
    cosines = []
    sines = []
    rotated_rhs = [start_norm] + [jnp.zeros_like(start_norm) for row_index in range(count)]
    upper = []
    for col_index in range(count):
        column = [hessen[col_index][row_index] for row_index in range(col_index + 2)]
        for row_index in range(col_index):
            rotated = (
                cosines[row_index] * column[row_index] + sines[row_index] * column[row_index + 1]
            )
            column[row_index + 1] = (
                -sines[row_index] * column[row_index] + cosines[row_index] * column[row_index + 1]
            )
            column[row_index] = rotated
        radius = jnp.sqrt(
            column[col_index] * column[col_index] + column[col_index + 1] * column[col_index + 1]
        )
        cosine = column[col_index] / radius
        sine_value = column[col_index + 1] / radius
        column[col_index] = radius
        cosines.append(cosine)
        sines.append(sine_value)
        rotated_rhs[col_index + 1] = -sine_value * rotated_rhs[col_index]
        rotated_rhs[col_index] = cosine * rotated_rhs[col_index]
        upper.append(column[: col_index + 1])
    coeffs = [None] * count
    for row_index in reversed(range(count)):
        total = rotated_rhs[row_index]
        for col_index in range(row_index + 1, count):
            total = total - upper[col_index][row_index] * coeffs[col_index]
        coeffs[row_index] = total / upper[row_index][row_index]
    return (coeffs, jnp.abs(rotated_rhs[count]) / start_norm)


def move_vectors_dom(vectors, offset):
    return shifted(vectors, "dom", offset)


def move_vectors_blk(vectors, offset):
    return shifted(vectors, "blk", offset)


def move_facing_dom(blocks, offset):
    return shifted(blocks, "dom", offset)


def move_facing_blk(blocks, offset):
    return shifted(blocks, "blk", offset)


def direct_path(adjoint_source, diag_blocks, face_blocks, neighbors, partner, flags):
    nrhs, elements, width = adjoint_source.shape
    blk_count = lax.axis_size("blk")
    dom_here = lax.axis_index("dom")
    blk_here = lax.axis_index("blk")
    wall_mask = (flags == 1).astype(jnp.float32)
    center = diag_blocks + jnp.einsum("ef,efab->eab", wall_mask, face_blocks, precision=HIGH)
    inverse = invert_blocks(center)
    inside = neighbors >= 0
    source_elem = jnp.where(inside, neighbors, 0)
    source_face = jnp.where(inside, partner, 0)
    owner_dev = source_elem // elements
    owner_dom = owner_dev // blk_count
    owner_blk = owner_dev % blk_count
    direction = jnp.where(
        owner_dom == dom_here - 1,
        1,
        jnp.where(
            owner_dom == dom_here + 1,
            2,
            jnp.where(owner_blk == blk_here - 1, 3, jnp.where(owner_blk == blk_here + 1, 4, 0)),
        ),
    )
    direction = jnp.where(inside, direction, 0).astype(jnp.int32)
    local_slot = source_elem % elements
    flat_direction = direction.reshape(-1)
    flat_inside = inside.reshape(-1)
    flat_local = (local_slot * 6 + source_face).reshape(-1)
    face_keys = (source_elem * 6 + source_face).reshape(-1)
    same_way = (flat_direction[None, :] == flat_direction[:, None]) & flat_inside[None, :]
    placing = jnp.sum(
        (same_way & (face_keys[None, :] < face_keys[:, None])).astype(jnp.int32), axis=1
    )
    offsets = jnp.array(
        [0, 6 * elements, 6 * elements + EY, 6 * elements + 2 * EY, 6 * elements + 2 * EY + EX],
        jnp.int32,
    )
    candidate = jnp.where(flat_direction == 0, flat_local, offsets[flat_direction] + placing)
    slot_range = jnp.arange(elements * 6, dtype=jnp.int32)

    def pick_rows(target, count):
        marked = ((flat_direction == target) & flat_inside).astype(jnp.int32)
        ranking = jnp.cumsum(marked) - marked
        chooser = (ranking[None, :] == jnp.arange(count)[:, None]) & (marked[None, :] > 0)
        return jnp.sum(jnp.where(chooser, slot_range[None, :], 0), axis=1)

    toward_next_dom = pick_rows(2, EY)
    toward_prev_dom = pick_rows(1, EY)
    toward_next_blk = pick_rows(4, EX)
    toward_prev_blk = pick_rows(3, EX)
    flat_blocks = face_blocks.reshape(elements * 6, width, width)
    block_pool = jnp.concatenate(
        [
            flat_blocks,
            move_facing_dom(jnp.take(flat_blocks, toward_next_dom, axis=0), 1),
            move_facing_dom(jnp.take(flat_blocks, toward_prev_dom, axis=0), -1),
            move_facing_blk(jnp.take(flat_blocks, toward_next_blk, axis=0), 1),
            move_facing_blk(jnp.take(flat_blocks, toward_prev_blk, axis=0), -1),
        ],
        axis=0,
    )
    column_blocks = (
        jnp.take(block_pool, candidate, axis=0) * flat_inside.astype(jnp.float32)[:, None, None]
    )
    column_blocks = column_blocks.reshape(elements, 6, width, width)
    vector_index = (direction * elements + local_slot).reshape(-1)

    def precondition(vectors):
        return jnp.einsum("eab,rea->reb", inverse, vectors, precision=HIGH)

    start_norm = jnp.sqrt(
        lax.psum(jnp.sum(adjoint_source * adjoint_source, axis=(1, 2)), ("dom", "blk"))
    )
    krylov_basis = [adjoint_source / start_norm[:, None, None]]
    hessen = []
    for iteration in range(ITERS):
        operator_vectors = precondition(krylov_basis[-1])
        gathered = jnp.concatenate(
            [
                operator_vectors,
                move_vectors_dom(operator_vectors, 1),
                move_vectors_dom(operator_vectors, -1),
                move_vectors_blk(operator_vectors, 1),
                move_vectors_blk(operator_vectors, -1),
            ],
            axis=1,
        )
        nearby = jnp.take(gathered, vector_index, axis=1).reshape(nrhs, elements, 6, width)
        own_part = jnp.einsum("eab,rea->reb", center, operator_vectors, precision=HIGH)
        mapped = own_part + jnp.einsum("egab,rega->reb", column_blocks, nearby, precision=HIGH)
        local_dots = [jnp.sum(mapped * member, axis=(1, 2)) for member in krylov_basis]
        projections = lax.psum(jnp.stack(local_dots), ("dom", "blk"))
        for row_index in range(len(krylov_basis)):
            mapped = mapped - projections[row_index][:, None, None] * krylov_basis[row_index]
        new_norm = jnp.sqrt(lax.psum(jnp.sum(mapped * mapped, axis=(1, 2)), ("dom", "blk")))
        hessen.append(jnp.concatenate([projections, new_norm[None, :]], axis=0))
        krylov_basis.append(mapped / new_norm[:, None, None])
    coeffs, rel_residual = least_squares(hessen, start_norm)
    combined = coeffs[0][:, None, None] * krylov_basis[0]
    for col_index in range(1, ITERS):
        combined = combined + coeffs[col_index][:, None, None] * krylov_basis[col_index]
    return (precondition(combined), rel_residual)


CELLS = EX * EY
F32 = jnp.float32
BF16 = jnp.bfloat16
VMEM_LIMIT = 40 * 1024 * 1024
OUT_CELLS = ((0, 1), (2, 3), (0, 2), (1, 3))
PIVOT_FLOOR = 0.02
RESIDUAL_FLOOR = 0.02


def pair_lane(row, col):
    return row * (row + 1) // 2 + col


def split_halves(value):
    high = value.astype(BF16)
    low = (value - high.astype(F32)).astype(BF16)
    return high, low


def dot32(left, right):
    return jnp.dot(left, right, preferred_element_type=F32)


def dot_halves(left_high, left_low, right_high, right_low):
    small = dot32(left_low, right_high) + dot32(left_high, right_low)
    return dot32(left_high, right_high) + small


def stack_halves(vector):
    high, low = split_halves(vector)
    return jnp.concatenate([high, low], axis=0), high


def row_times(stacked, high, block_high, block_low):
    rows = high.shape[0]
    both = dot32(stacked, block_high)
    return both[:rows] + both[rows:] + dot32(high, block_low)


FROM_X = CELLS
FROM_Y = 2 * CELLS
OUTWARD = 3 * CELLS
BLOCKS = OUTWARD + 8
RING_TARGETS = (0, 1, 2, 3, 0, 2, 1, 3)


def local_products(halves, high_ref, low_ref):
    results = []
    for cell in range(CELLS):
        total = None
        for source, entry in (
            (cell, cell), (cell ^ 2, FROM_X + (cell ^ 2)), (cell ^ 1, FROM_Y + (cell ^ 1))
        ):
            part = row_times(*halves[source], high_ref[entry], low_ref[entry])
            total = part if total is None else total + part
        results.append(total)
    return results


def outward_products(halves, high_ref, low_ref):
    results = []
    for way in range(4):
        for place in range(2):
            entry = OUTWARD + 2 * way + place
            results.append(
                row_times(*halves[OUT_CELLS[way][place]], high_ref[entry], low_ref[entry])
            )
    return results


def padded(width):
    return (width + 7) // 8 * 8


def tails_of(values):
    rows, width = values[0].shape
    tail = width - 128
    total = None
    for place, value in enumerate(values):
        tile = jnp.concatenate([value[:, 128:], jnp.zeros((rows, 128 - tail), F32)], axis=1)
        tile = tile if place == 0 else pltpu.roll(tile, tail * place, 1)
        total = tile if total is None else total + tile
    return total


def tail_at(tile, tail, place):
    turned = tile if place == 0 else pltpu.roll(tile, 128 - tail * place, 1)
    return turned[:, :tail]


def put_rows(ref, first, values):
    rows = values[0].shape[0]
    for place, value in enumerate(values):
        ref[first + rows * place : first + rows * (place + 1), :] = value[:, :128]
    for part in range(0, len(values), 3):
        start = first + rows * (len(values) + part // 3)
        ref[start : start + rows, :] = tails_of(values[part : part + 3])


def get_rows(ref, first, rows, tail, count, place):
    main = ref[first + rows * place : first + rows * (place + 1), :]
    start = first + rows * (count + place // 3)
    return jnp.concatenate([main, tail_at(ref[start : start + rows, :], tail, place % 3)], axis=1)


def send_along_blk(local, outward, prev_ref, next_ref, first):
    for ref, way, cells in ((prev_ref, 2, (0, 2)), (next_ref, 3, (1, 3))):
        put_rows(
            ref, first,
            [
                outward[2 * way], outward[2 * way + 1], local[cells[0]], local[cells[1]],
                outward[2 + cells[0] % 2],
            ],
        )


def send_to_dom_prev(local, outward, prev_ref, first):
    put_rows(
        prev_ref, first,
        [outward[0], outward[1], local[0], local[1], outward[4], outward[6]],
    )


def setup_kernel(
    nbr_ref, flag_ref, src_ref, diag_hbm_ref, face_hbm_ref,
    high_ref, low_ref, inv_high_ref, inv_low_ref, base_ref, local_ref, outward_ref,
    blk_prev_ref, blk_next_ref, dom_prev_ref, dom_next_ref, slot_ref,
    center_ref, x_ref, d_high_ref, d_low_ref, product_ref, face_ref, cell_ref, face_of_ref, diag_sem, face_sem,
    *, dom_count, blk_count,
):
    width = diag_hbm_ref.shape[0]
    diag_copies = [
        pltpu.make_async_copy(
            diag_hbm_ref.at[:, slot, :], center_ref.at[slot], diag_sem.at[slot]
        )
        for slot in range(CELLS)
    ]
    face_copies = [
        [
            pltpu.make_async_copy(
                face_hbm_ref.at[face, :, slot, :], face_ref.at[slot, face], face_sem.at[slot, face]
            )
            for face in range(6)
        ]
        for slot in range(CELLS)
    ]
    for slot in range(CELLS):
        diag_copies[slot].start()
    for slot in range(CELLS):
        for face in range(6):
            pl.when(flag_ref[slot, face] == 1)(face_copies[slot][face].start)
    for slot in range(CELLS):
        for face in range(6):
            pl.when(nbr_ref[slot, face] >= 0)(face_copies[slot][face].start)
    dom_here = lax.axis_index("dom")
    blk_here = lax.axis_index("blk")
    here = dom_here * blk_count + blk_here
    for slot in range(CELLS):
        up_x = jnp.int32(0)
        down_x = jnp.int32(0)
        up_y = jnp.int32(0)
        down_y = jnp.int32(0)
        for face in range(6):
            other = nbr_ref[slot, face]
            gap = jnp.where(other >= 0, other // CELLS - here, 0)
            up_x = jnp.where(gap == blk_count, 1, up_x)
            down_x = jnp.where(gap == -blk_count, 1, down_x)
            up_y = jnp.where(gap == 1, 1, up_y)
            down_y = jnp.where(gap == -1, 1, down_y)
        cell_x = jnp.where(dom_here < dom_count - 1, up_x, 1 - down_x)
        cell_y = jnp.where(blk_here < blk_count - 1, up_y, 1 - down_y)
        cell = 2 * cell_x + cell_y
        cell_ref[slot] = cell
        slot_ref[cell] = slot
    for entry in range(CELLS * 4):
        face_of_ref[entry] = -1
    for slot in range(CELLS):
        cell = cell_ref[slot]
        for face in range(6):
            other = nbr_ref[slot, face]
            inside = other >= 0
            safe = jnp.where(inside, other, 0)
            gap = safe // CELLS - here
            mate = cell_ref[safe % CELLS]
            change = jnp.bitwise_xor(mate, cell)
            way_x = jnp.where(cell >= 2, 0, 1)
            way_y = jnp.where(cell % 2 == 1, 2, 3)
            way_in = jnp.where(change == 2, way_x, way_y)
            way = jnp.where(
                gap == 0, way_in,
                jnp.where(
                    gap == -blk_count, 0,
                    jnp.where(gap == blk_count, 1, jnp.where(gap == -1, 2, 3)),
                ),
            )

            @pl.when(inside)
            def _():
                face_of_ref[slot * 4 + way] = face

    rows = lax.broadcasted_iota(jnp.int32, (width, width), 0)
    cols = lax.broadcasted_iota(jnp.int32, (width, width), 1)
    on_diag = rows == cols
    for slot in range(CELLS):
        base_ref[cell_ref[slot]] = src_ref[:, slot, :]
        diag_copies[slot].wait()
    for slot in range(CELLS):
        for face in range(6):

            @pl.when(flag_ref[slot, face] == 1)
            def _():
                face_copies[slot][face].wait()
                center_ref[slot] = center_ref[slot] + face_ref[slot, face]

    for slot in range(CELLS):
        center = center_ref[slot]
        marked = jnp.where(on_diag, center, 0.0)
        inv_row = 1.0 / jnp.sum(marked, axis=0, keepdims=True)
        inv_col = 1.0 / jnp.sum(marked, axis=1, keepdims=True)
        defect = jnp.where(on_diag, 0.0, -inv_col * center)
        x_ref[slot] = jnp.where(on_diag, inv_col, defect * inv_row)
        d_high_ref[slot], d_low_ref[slot] = split_halves(defect)
    for sweep in range(1, SWEEPS):
        squares = [
            dot_halves(d_high_ref[slot], d_low_ref[slot], d_high_ref[slot], d_low_ref[slot])
            for slot in range(CELLS)
        ]
        for slot in range(CELLS):
            d_high_ref[slot], d_low_ref[slot] = split_halves(squares[slot])
        for slot in range(CELLS):
            x_high, x_low = split_halves(x_ref[slot])
            x_ref[slot] = x_ref[slot] + dot_halves(
                d_high_ref[slot], d_low_ref[slot], x_high, x_low
            )
    for slot in range(CELLS):
        for face in range(6):
            pl.when(nbr_ref[slot, face] >= 0)(face_copies[slot][face].wait)
    for slot in range(CELLS):
        cell = cell_ref[slot]
        x_high, x_low = split_halves(x_ref[slot])
        inv_high_ref[cell] = x_high
        inv_low_ref[cell] = x_low
        own = -dot_halves(d_high_ref[slot], d_low_ref[slot], d_high_ref[slot], d_low_ref[slot])
        high_ref[cell], low_ref[cell] = split_halves(own)
        for way in range(4):
            face = face_of_ref[slot * 4 + way]
            block = jnp.where(face >= 0, face_ref[slot, jnp.maximum(face, 0)], 0.0)
            f_high, f_low = split_halves(block)
            product = dot_halves(x_high, x_low, f_high, f_low)
            if way < 2:
                leaves = cell // 2 == way
                inner = FROM_X + cell
                place = cell % 2
            else:
                leaves = cell % 2 == way - 2
                inner = FROM_Y + cell
                place = cell // 2
            entry = jnp.where(leaves, OUTWARD + 2 * way + place, inner)
            high_ref[entry], low_ref[entry] = split_halves(product)
            product_ref[entry] = product
    tall = padded(width)
    for way, ref in enumerate((dom_prev_ref, dom_next_ref, blk_prev_ref, blk_next_ref)):
        pair = [product_ref[OUTWARD + 2 * way + place] for place in range(2)]
        for place in range(2):
            ref[tall * place : tall * place + width, :] = pair[place][:, :128]
        ref[2 * tall : 2 * tall + width, :] = tails_of(pair)
    halves = [stack_halves(base_ref[cell]) for cell in range(CELLS)]
    local = local_products(halves, high_ref, low_ref)
    outward = outward_products(halves, high_ref, low_ref)
    for cell in range(CELLS):
        local_ref[cell] = local[cell]
    for entry in range(8):
        outward_ref[entry] = outward[entry]
    send_along_blk(local, outward, blk_prev_ref, blk_next_ref, 3 * tall)
    send_to_dom_prev(local, outward, dom_prev_ref, 3 * tall)


FROM_BLK = 5
FROM_DOM = 6
RELAYED = 2


def middle_kernel(first, local_ref, outward_ref, next_ref, prev_ref, sum_ref, dom_next_ref):
    rows = local_ref.shape[1]
    tail = local_ref.shape[2] - 128

    def got(ref, place):
        return get_rows(ref, first, rows, tail, FROM_BLK, place)

    sums = []
    for cell in range(CELLS):
        given = prev_ref if cell % 2 == 0 else next_ref
        sums.append(local_ref[cell] + got(given, cell // 2))
        sum_ref[cell] = sums[cell]
    put_rows(
        dom_next_ref, 0,
        [outward_ref[2], outward_ref[3], sums[2], sums[3], got(prev_ref, 4), got(next_ref, 4)],
    )


def relay_kernel(first, tail, sum_ref, dom_ref, prev_ref, next_ref):
    rows = sum_ref.shape[1]

    def got(place):
        return get_rows(dom_ref, first, rows, tail, FROM_DOM, place)

    put_rows(prev_ref, 0, [got(4), got(0)])
    put_rows(next_ref, 0, [got(5), got(1)])


def odd_kernel(first_pair, *refs):
    sum_ref, outward_ref, blk_next_ref, blk_prev_ref, dom_prev_ref, dom_next_ref = refs[:6]
    high_ref, low_ref = refs[6:8]
    rows = sum_ref.shape[1]
    width = sum_ref.shape[2]
    tail = width - 128
    first = 0
    if first_pair:
        tall = padded(width)
        first = 3 * tall
        dom_blocks_ref = refs[8]
        odd_ref, even_ref, in_high_ref, in_low_ref = refs[9:]
        for way, ref in enumerate((dom_blocks_ref, dom_next_ref, blk_prev_ref, blk_next_ref)):
            for place in range(2):
                main = ref[tall * place : tall * place + width, :]
                rest = tail_at(ref[2 * tall : 2 * tall + width, :], tail, place)
                high, low = split_halves(jnp.concatenate([main, rest], axis=1))
                in_high_ref[2 * way + place] = high
                in_low_ref[2 * way + place] = low
    else:
        in_high_ref, in_low_ref, odd_ref, even_ref = refs[8:]

    def from_blk(ref, place):
        return get_rows(ref, first, rows, tail, FROM_BLK, place)

    def from_dom_prev(place):
        return get_rows(dom_prev_ref, 0, rows, tail, FROM_DOM, place)

    def from_dom_next(place):
        return get_rows(dom_next_ref, first, rows, tail, FROM_DOM, place)

    odd = [
        sum_ref[cell] + (from_dom_prev if cell < 2 else from_dom_next)(cell % 2)
        for cell in range(CELLS)
    ]
    ring = [
        from_dom_prev(2) + outward_ref[0],
        from_dom_prev(3) + outward_ref[1],
        from_dom_next(2) + outward_ref[2],
        from_dom_next(3) + outward_ref[3],
        from_blk(blk_prev_ref, 2) + outward_ref[4] + from_dom_prev(4),
        from_blk(blk_prev_ref, 3) + outward_ref[5],
        from_blk(blk_next_ref, 2) + outward_ref[6] + from_dom_prev(5),
        from_blk(blk_next_ref, 3) + outward_ref[7],
    ]
    even = local_products([stack_halves(value) for value in odd], high_ref, low_ref)
    for place, value in enumerate(ring):
        cell = RING_TARGETS[place]
        even[cell] = even[cell] + row_times(
            *stack_halves(value), in_high_ref[place], in_low_ref[place]
        )
    for cell in range(CELLS):
        odd_ref[cell] = odd[cell]
        even_ref[cell] = even[cell]


TURNED = ((2, 0, 0), (3, 1, 0), (5, 0, 1), (7, 1, 1))


def even_kernel(last_pair, older_count, *refs):
    part_ref, turn_next_ref, turn_prev_ref, in_high_ref, in_low_ref = refs[:5]
    refs = refs[5:]
    rows = part_ref.shape[1]
    tail = part_ref.shape[2] - 128
    even = [part_ref[cell] for cell in range(CELLS)]
    for place, side, item in TURNED:
        value = get_rows((turn_prev_ref, turn_next_ref)[side], 0, rows, tail, RELAYED, item)
        cell = RING_TARGETS[place]
        even[cell] = even[cell] + row_times(
            *stack_halves(value), in_high_ref[place], in_low_ref[place]
        )
    if last_pair:
        older = refs[:older_count]
        gram_in_ref, gram_ref, even_ref = refs[older_count:]
    else:
        high_ref, low_ref = refs[:2]
        even_ref, local_out_ref, outward_out_ref, prev_ref, next_ref, dom_out_ref = refs[2:]
    for cell in range(CELLS):
        even_ref[cell] = even[cell]
    if last_pair:
        gram = gram_rows(ITERS, list(older) + [even_ref], gram_in_ref[...])
        half = gram.shape[0] // 2
        gram = gram[:half] + pltpu.roll(gram[half:], 64, 1)
        for place in range(gram_ref.shape[0]):
            gram_ref[place] = gram
    else:
        halves = [stack_halves(value) for value in even]
        local = local_products(halves, high_ref, low_ref)
        outward = outward_products(halves, high_ref, low_ref)
        for cell in range(CELLS):
            local_out_ref[cell] = local[cell]
        for entry in range(8):
            outward_out_ref[entry] = outward[entry]
        send_along_blk(local, outward, prev_ref, next_ref, 0)
        send_to_dom_prev(local, outward, dom_out_ref, 0)


def gram_kernel(newest, *refs):
    base_refs = refs[: newest + 1]
    gram = None if newest == 1 else refs[newest + 1][...]
    gram = gram_rows(newest - 1, base_refs, gram)
    refs[-1][...] = gram_rows(newest, base_refs, gram)


def gram_rows(step, base_refs, gram):
    newest = base_refs[step]
    nrhs = newest.shape[1]
    lanes = lax.broadcasted_iota(jnp.int32, (nrhs, 128), 1)
    if gram is None:
        gram = jnp.zeros((nrhs, 128), F32)
    for col in range(step + 1):
        total = newest[0] * base_refs[col][0]
        for cell in range(1, CELLS):
            total = total + newest[cell] * base_refs[col][cell]
        value = jnp.sum(total, axis=1, keepdims=True)
        gram = jnp.where(lanes == pair_lane(step, col), value, gram)
    return gram


def finish_kernel(*refs):
    gram_ref = refs[0]
    base_refs = refs[1 : 1 + ITERS]
    inv_high_ref, inv_low_ref, slot_ref, adjoint_ref, rel_ref, fine_ref = refs[1 + ITERS :]
    count = ITERS + 1
    packed = sum_parts(gram_ref)
    gram = jnp.concatenate([packed, pltpu.roll(packed, 64, 1)], axis=0)

    def lane(row, col):
        place = pair_lane(row, col)
        return jnp.broadcast_to(gram[:, place : place + 1], gram.shape)

    diag = [lane(j, j) for j in range(count)]
    scale = [lax.rsqrt(value) for value in diag]
    start = diag[0] * scale[0]
    lower = [[None] * count for j in range(count)]
    solved = []
    ratio = [scale[j] * start for j in range(count)]
    smallest = jnp.ones_like(gram)
    inv_pivot = []
    for col in range(count):
        pivot = jnp.ones_like(gram)
        for k in range(col):
            pivot = pivot - lower[col][k] * lower[col][k]
        smallest = jnp.minimum(smallest, pivot)
        inv_root = lax.rsqrt(pivot)
        inv_pivot.append(inv_root)
        for row in range(col + 1, count):
            value = lane(row, col) * scale[row] * scale[col]
            for k in range(col):
                value = value - lower[row][k] * lower[col][k]
            lower[row][col] = value * inv_root
        right = ratio[col] if col % 2 == 0 else -ratio[col]
        for k in range(col):
            right = right - lower[col][k] * solved[k]
        solved.append(right * inv_root)
    squares = solved[0] * solved[0]
    for j in range(1, count):
        squares = squares + solved[j] * solved[j]
    rel = lax.rsqrt(squares)
    back = [None] * count
    for j in reversed(range(count)):
        value = solved[j]
        for k in reversed(range(j + 1, count)):
            value = value - lower[k][j] * back[k]
        back[j] = value * inv_pivot[j]
    inv_squares = 1.0 / squares
    residual = [ratio[j] * back[j] * inv_squares for j in range(count)]
    coeffs = [None] * ITERS
    coeffs[ITERS - 1] = -residual[ITERS]
    for j in reversed(range(1, ITERS)):
        coeffs[j - 1] = -residual[j] - coeffs[j]
    lanes = lax.broadcasted_iota(jnp.int32, gram.shape, 1)
    good = (smallest > PIVOT_FLOOR) & (rel > RESIDUAL_FLOOR) & (rel < 2.0)
    for j in range(count):
        good = good & (diag[j] > 1e-30) & (diag[j] < 1e36)
    worst = jnp.min(jnp.where(good, 1.0, 0.0))
    fine_ref[0] = jnp.where(worst > 0.5, 1, 0).astype(jnp.int32)
    rel_ref[...] = jnp.transpose(rel)[0:1, :]
    width = base_refs[0].shape[-1]
    wide = [
        jnp.concatenate([value, value], axis=1)[:, :width] for value in coeffs
    ]
    results = []
    for cell in range(CELLS):
        total = wide[0] * base_refs[0][cell]
        for j in range(1, ITERS):
            total = total + wide[j] * base_refs[j][cell]
        stacked, high = stack_halves(total)
        results.append(row_times(stacked, high, inv_high_ref[cell], inv_low_ref[cell]))
    for slot in range(CELLS):
        value = results[0]
        for cell in range(1, CELLS):
            value = jnp.where(slot_ref[cell] == slot, results[cell], value)
        adjoint_ref[:, slot, :] = value


def vmem(count):
    return [pl.BlockSpec(memory_space=pltpu.VMEM)] * count


def smem(count):
    return [pl.BlockSpec(memory_space=pltpu.SMEM)] * count


PARAMS = pltpu.CompilerParams(vmem_limit_bytes=VMEM_LIMIT)


def struct(*shape, kind=F32):
    return jax.ShapeDtypeStruct(shape, kind)


def spread_kernel(parts_ref, copies_ref):
    total = sum_parts(parts_ref)
    for place in range(copies_ref.shape[0]):
        copies_ref[place] = total


def sum_parts(parts_ref):
    total = parts_ref[0]
    for place in range(1, parts_ref.shape[0]):
        total = total + parts_ref[place]
    return total


def near_size():
    dom_count = lax.axis_size("dom")
    return 4 if dom_count % 4 == 0 else dom_count


def sum_devices(copies):
    dom_count, blk_count = (lax.axis_size("dom"), lax.axis_size("blk"))
    inner = near_size()
    size = inner * blk_count
    near = [
        [first + k for k in range(size)] for first in range(0, dom_count * blk_count, size)
    ]
    far = [[first + k for k in range(0, dom_count, inner)] for first in range(inner)]
    parts = lax.all_to_all(copies, ("dom", "blk"), 0, 0, axis_index_groups=near)
    copies = pl.pallas_call(
        spread_kernel,
        out_shape=struct(dom_count // inner, *copies.shape[1:]),
        in_specs=vmem(1),
        out_specs=vmem(1)[0],
        compiler_params=PARAMS,
        name="sum_near",
    )(parts)
    return lax.all_to_all(copies, "dom", 0, 0, axis_index_groups=far)


def rotated(value, axis, steps):
    count = lax.axis_size(axis)
    return lax.ppermute(
        value, axis, [(source, (source + steps) % count) for source in range(count)]
    )


def both_ways(to_prev, to_next, axis):
    from_next = rotated(to_prev, axis, -1)
    from_prev = rotated(to_next, axis, 1)
    return from_next, from_prev


def shards(adjoint_source, diag_blocks, face_blocks, neighbors, partner, flags):
    nrhs, elements, width = adjoint_source.shape
    block = (width, width)
    tall = padded(width)
    field = struct(CELLS, nrhs, width)
    ring = struct(8, nrhs, width)
    blk_edge = struct(7 * nrhs, 128)
    dom_edge = struct(8 * nrhs, 128)
    turn_edge = struct(3 * nrhs, 128)
    with_blocks = lambda edge: struct(3 * tall + edge.shape[0], 128)
    cost = lambda flops, data: pl.CostEstimate(
        flops=flops, bytes_accessed=data, transcendentals=0
    )
    products = 2 * nrhs * width * width * 3
    outs = pl.pallas_call(
        functools.partial(
            setup_kernel, dom_count=lax.axis_size("dom"), blk_count=lax.axis_size("blk")
        ),
        out_shape=(
            struct(BLOCKS, *block, kind=BF16), struct(BLOCKS, *block, kind=BF16),
            struct(CELLS, *block, kind=BF16), struct(CELLS, *block, kind=BF16),
            field, field, ring, with_blocks(blk_edge), with_blocks(blk_edge),
            with_blocks(dom_edge), struct(3 * tall, 128),
            struct(CELLS, kind=jnp.int32),
        ),
        in_specs=smem(2) + vmem(1) + [pl.BlockSpec(memory_space=pl.ANY)] * 2,
        out_specs=tuple(vmem(11) + smem(1)),
        scratch_shapes=[
            pltpu.VMEM((CELLS,) + block, F32),
            pltpu.VMEM((CELLS,) + block, F32),
            pltpu.VMEM((CELLS,) + block, BF16),
            pltpu.VMEM((CELLS,) + block, BF16),
            pltpu.VMEM((BLOCKS,) + block, F32),
            pltpu.VMEM((CELLS, 6) + block, F32),
            pltpu.SMEM((CELLS,), jnp.int32),
            pltpu.SMEM((CELLS * 4,), jnp.int32),
            pltpu.SemaphoreType.DMA((CELLS,)),
            pltpu.SemaphoreType.DMA((CELLS, 6)),
        ],
        compiler_params=PARAMS,
        name="setup_blocks",
    )(
        neighbors, flags, adjoint_source,
        jnp.transpose(diag_blocks, (1, 0, 2)), jnp.transpose(face_blocks, (1, 2, 0, 3)),
    )
    high, low, inv_high, inv_low, base, local, outward = outs[:7]
    blk_sends = outs[7:9]
    dom_send, dom_blocks = outs[9:11]
    slots = outs[11]
    bases = [base]
    gram = None
    inward = ()
    for pair in range(ITERS // 2):
        first_pair = pair == 0
        last_pair = pair == ITERS // 2 - 1
        first = 3 * tall if first_pair else 0
        from_blk = both_ways(*blk_sends, "blk")
        from_dom_next = rotated(dom_send, "dom", -1)
        if first_pair:
            inward = (rotated(dom_blocks, "dom", 1),)
        sums, dom_send = pl.pallas_call(
            functools.partial(middle_kernel, first),
            out_shape=(field, dom_edge),
            in_specs=vmem(4),
            out_specs=tuple(vmem(2)),
            compiler_params=PARAMS,
            name=f"middle_part_{pair}",
        )(local, outward, *from_blk)
        from_dom_prev = rotated(dom_send, "dom", 1)
        turns = pl.pallas_call(
            functools.partial(relay_kernel, first, width - 128),
            out_shape=(turn_edge, turn_edge),
            in_specs=vmem(2),
            out_specs=tuple(vmem(2)),
            compiler_params=PARAMS,
            name=f"relay_part_{pair}",
        )(sums, from_dom_next)
        turns = both_ways(*turns, "blk")
        given = [sums, outward, *from_blk, from_dom_prev, from_dom_next, high, low, *inward]
        shapes = (field, field)
        if first_pair:
            shapes += (struct(8, *block, kind=BF16), struct(8, *block, kind=BF16))
        odd, part, *made = pl.pallas_call(
            functools.partial(odd_kernel, first_pair),
            out_shape=shapes,
            in_specs=vmem(len(given)),
            out_specs=tuple(vmem(len(shapes))),
            compiler_params=PARAMS,
            cost_estimate=cost(20 * products, 6000000),
            name=f"odd_part_{pair}",
        )(*given)
        if first_pair:
            inward = made
        bases.append(odd)
        newest = len(bases) - 1
        given = bases + ([gram] if newest > 1 else [])
        gram = pl.pallas_call(
            functools.partial(gram_kernel, newest),
            out_shape=struct(nrhs, 128),
            in_specs=vmem(len(given)),
            out_specs=vmem(1)[0],
            compiler_params=PARAMS,
            cost_estimate=cost(100000 * (newest + 1), 2000000),
            name=f"gram_part_{pair}",
        )(*given)
        given = [part, *turns, *inward]
        if last_pair:
            given += [*bases, gram]
            shapes = (struct(near_size() * lax.axis_size("blk"), nrhs // 2, 128), field)
        else:
            given += [high, low]
            shapes = (field, field, ring, blk_edge, blk_edge, dom_edge)
        outs = pl.pallas_call(
            functools.partial(even_kernel, last_pair, len(bases)),
            out_shape=shapes,
            in_specs=vmem(len(given)),
            out_specs=tuple(vmem(len(shapes))),
            compiler_params=PARAMS,
            cost_estimate=cost(24 * products, 6000000),
            name=f"even_part_{pair}",
        )(*given)
        if last_pair:
            gram = outs[0]
        else:
            bases.append(outs[0])
            local, outward = outs[1:3]
            blk_sends = outs[3:5]
            dom_send = outs[5]
    gram = sum_devices(gram)
    given = [gram] + bases + [inv_high, inv_low, slots]
    adjoint, rel, fine = pl.pallas_call(
        finish_kernel,
        out_shape=(
            struct(nrhs, elements, width), struct(1, nrhs), struct(1, kind=jnp.int32)
        ),
        in_specs=vmem(len(given) - 1) + smem(1),
        out_specs=tuple(vmem(2) + smem(1)),
        compiler_params=PARAMS,
        name="finish_part",
    )(*given)
    return lax.switch(
        fine[0],
        [lambda given: direct_path(*given), lambda given: (adjoint, rel.reshape(nrhs))],
        (adjoint_source, diag_blocks, face_blocks, neighbors, partner, flags),
    )


def solution(mesh):
    in_specs = (
        P(None, ("dom", "blk"), None),
        P(("dom", "blk"), None, None),
        P(("dom", "blk"), None, None, None),
        P(("dom", "blk"), None),
        P(("dom", "blk"), None),
        P(("dom", "blk"), None),
    )
    out_specs = (P(None, ("dom", "blk"), None), P())
    return jax.shard_map(shards, mesh=mesh, in_specs=in_specs, out_specs=out_specs, check_vma=False)
```
